256 devices in a mesh: gx: 8 (over z), gy: 32 (over x, y, core).
Axes of the slice: x: 4, y: 4, z: 8, core: 2. Of those that a mesh axis runs over, the one named last changes fastest.
Arguments:
- right_side: float32 [128, 256, 128], P('gx', 'gy'), may hold values from -6 to 6
- alpha: float32 [128, 256, 128], P('gx', 'gy'), may hold values from 0.1 to 40
- beta_x: float32 [128, 256, 128], P('gx', 'gy'), may hold values from 0.125 to 8
- beta_y: float32 [128, 256, 128], P('gx', 'gy'), may hold values from 0.125 to 8
- beta_z: float32 [128, 256, 128], P('gx', 'gy'), may hold values from 0.125 to 8
Outputs:
- correction: float32 [128, 256, 128], P('gx', 'gy')
The draws below stay inside these ranges and needn't reach their ends.
All inputs are finite; a program needn't handle non-finite values.
Results may differ from the reference program's by a relative error of at most 0.0001.
Values sent between devices are 32-bit elements; how exact they have to be, the bound alone decides.
A program may use at most 320 MiB of HBM per device.

```python
import math
import jax
import jax.numpy as jnp

CXD = 16
CYD = 8
NZ = 128
LEVELS = 5
SWEEPS = 4
COARSE_SWEEPS = 12
NX = 128
NY = 256


def spread_blocks(level):
    wide = jnp.repeat(level, CXD, axis=0)
    wide = jnp.repeat(wide, CYD, axis=1)
    return jnp.repeat(wide, NZ // 2, axis=2)


def rough_factor(key):
    return jnp.exp(jax.random.uniform(key, (NX, NY, NZ), jnp.float32, math.log(0.5), math.log(2.0)))


def block_level(key, lower, upper):
    shape = (NX // CXD, NY // CYD, 2)
    level = jnp.exp(jax.random.uniform(key, shape, jnp.float32, math.log(lower), math.log(upper)))
    return level


def draw_alpha(key, part):
    key = jax.random.fold_in(key, 11)
    first, second = jax.random.split(key)
    return spread_blocks(block_level(first, 0.2, 20.0)) * rough_factor(second)


def draw_beta_x(key, part):
    key = jax.random.fold_in(key, 23)
    first, second = jax.random.split(key)
    return spread_blocks(block_level(first, 0.25, 4.0)) * rough_factor(second)


def draw_beta_y(key, part):
    key = jax.random.fold_in(key, 37)
    first, second = jax.random.split(key)
    return spread_blocks(block_level(first, 0.25, 4.0)) * rough_factor(second)


def draw_beta_z(key, part):
    key = jax.random.fold_in(key, 41)
    first, second = jax.random.split(key)
    return spread_blocks(block_level(first, 0.25, 4.0)) * rough_factor(second)


def block_scale(rng, shape, pieces, least, top_value):
    level = 1.0
    for position, shards_of in pieces:
        draws = jax.random.uniform(jax.random.fold_in(jax.random.fold_in(rng, 6), position), (shards_of,), jnp.float32, least / len(pieces), top_value / len(pieces))
        level = level * jnp.repeat(jnp.exp(draws), shape[position] // shards_of).reshape((-1,) + (1,) * (len(shape) - 1 - position))
    return level


def gaussian(key, dims, scale, limit, shards=(), kind=jnp.bfloat16):
    array = scale * jax.random.normal(key, dims, jnp.float32)
    if shards:
        array = array * block_scale(key, dims, shards, -0.22, 0.18)
    return jnp.clip(array, -limit, limit).astype(kind)


def setup_inputs(seed: int = 0) -> dict:
    keys = jax.random.split(jax.random.key(seed), 6)
    return {
        "right_side": gaussian(keys[0], (NX, NY, NZ), 1.0, 6.0, ((0, 8), (1, 32)), jnp.float32),
        "alpha": draw_alpha(jax.random.fold_in(keys[5], 71), 0),
        "beta_x": draw_beta_x(jax.random.fold_in(keys[5], 71), 0),
        "beta_y": draw_beta_y(jax.random.fold_in(keys[5], 71), 0),
        "beta_z": draw_beta_z(jax.random.fold_in(keys[5], 71), 0),
    }


SHIFT = 0.002
LOW = 0.25
HIGH = 2.0
COARSE_LOW = 0.1


def chebyshev_table(count, lower, upper):
    theta = (upper + lower) / 2.0
    delta = (upper - lower) / 2.0
    sigma = theta / delta
    rho_prev = 1.0 / sigma
    table = []
    for sweep in range(count):
        if sweep == 0:
            table.append((0.0, 1.0 / theta))
        else:
            rho_next = 1.0 / (2.0 * sigma - rho_prev)
            table.append((rho_next * rho_prev, 2.0 * rho_next / delta))
            rho_prev = rho_next
    return table


def restrict_cells(values):
    size_x, size_y, size_z = values.shape
    return values.reshape(size_x // 2, 2, size_y // 2, 2, size_z // 2, 2).mean(axis=(1, 3, 5))


def prolong(values):
    size_x, size_y, size_z = values.shape
    spread = jnp.broadcast_to(values[:, None, :, None, :, None], (size_x, 2, size_y, 2, size_z, 2))
    return spread.reshape(2 * size_x, 2 * size_y, 2 * size_z)


def restrict_coefs(coeffs):
    alpha, face_x, face_y, face_z = coeffs
    size_x, size_y, size_z = alpha.shape
    new_alpha = restrict_cells(alpha)
    new_x = face_x[0::2].reshape(size_x // 2 + 1, size_y // 2, 2, size_z // 2, 2).mean(axis=(2, 4))
    new_y = face_y[:, 0::2].reshape(size_x // 2, 2, size_y // 2 + 1, size_z // 2, 2).mean(axis=(1, 4))
    new_z = face_z[:, :, 0::2].reshape(size_x // 2, 2, size_y // 2, 2, size_z // 2).mean(axis=(1, 3))
    return (new_alpha, new_x, new_y, new_z)


def prepare(coeffs, level):
    alpha, face_x, face_y, face_z = coeffs
    upper_z = jnp.concatenate([face_z[:, :, 1:], jnp.zeros_like(face_z[:, :, :1])], axis=2)
    scale = 0.25 ** level
    diagonal = SHIFT * alpha + scale * (face_x[:-1] + face_x[1:] + face_y[:, :-1] + face_y[:, 1:] + face_z + upper_z)
    return (alpha, face_x, face_y, face_z, upper_z, 1.0 / diagonal, scale)


def operate(padded, coeffs):
    alpha, face_x, face_y, face_z, upper_z, inverse, scale = coeffs
    centre = padded[1:-1, 1:-1]
    flux_x = face_x[:-1] * (centre - padded[:-2, 1:-1]) + face_x[1:] * (centre - padded[2:, 1:-1])
    flux_y = face_y[:, :-1] * (centre - padded[1:-1, :-2]) + face_y[:, 1:] * (centre - padded[1:-1, 2:])
    along_z = jnp.pad(centre, ((0, 0), (0, 0), (1, 1)))
    flux_z = face_z * (centre - along_z[:, :, :-2]) + upper_z * (centre - along_z[:, :, 2:])
    return SHIFT * alpha * centre + scale * (flux_x + flux_y + flux_z)


def local_pad(field):
    return jnp.pad(field, ((1, 1), (1, 1), (0, 0)))


def smooth(field, source, coeffs, count, lower, upper, padder):
    inverse = coeffs[5]
    update = None
    for sweep, (keep, gain) in enumerate(chebyshev_table(count, lower, upper)):
        if field is None:
            resid = inverse * source
        else:
            resid = inverse * (source - operate(padder(field), coeffs))
        update = gain * resid if sweep == 0 else keep * update + gain * resid
        field = update if field is None else field + update
    return field


def cycle(source, levels):
    if len(levels) == 1:
        return smooth(None, source, levels[0], COARSE_SWEEPS, COARSE_LOW, HIGH, local_pad)
    field = smooth(None, source, levels[0], SWEEPS, LOW, HIGH, local_pad)
    resid = source - operate(local_pad(field), levels[0])
    field = field + prolong(cycle(restrict_cells(resid), levels[1:]))
    return smooth(field, source, levels[0], SWEEPS, LOW, HIGH, local_pad)


def reference(right_side, alpha, beta_x, beta_y, beta_z):
    face_x = jnp.concatenate([beta_x, jnp.zeros_like(beta_x[:1])], axis=0)
    face_y = jnp.concatenate([beta_y, jnp.zeros_like(beta_y[:, :1])], axis=1)
    raw = [(alpha, face_x, face_y, beta_z)]
    for level in range(LEVELS - 1):
        raw.append(restrict_coefs(raw[-1]))
    levels = [prepare(raw[level], level) for level in range(LEVELS)]
    return cycle(right_side, levels)
```

```python
import functools

import jax
import jax.numpy as jnp
from jax import lax
from jax.experimental import pallas as pl
from jax.experimental.pallas import tpu as pltpu
from jax.sharding import PartitionSpec as P

MESH = pl.DeviceIdType.MESH
F32 = jnp.float32

SHIFT = 0.002
LOW = 0.25
HIGH = 2.0
COARSE_LOW = 0.1
SWEEPS = 4
COARSE_SWEEPS = 12
GX = 8
GY = 32


def chebyshev_table(count, lower, upper):
    theta = (upper + lower) / 2.0
    delta = (upper - lower) / 2.0
    sigma = theta / delta
    rho_prev = 1.0 / sigma
    table = []
    for sweep in range(count):
        if sweep == 0:
            table.append((0.0, 1.0 / theta))
        else:
            rho_next = 1.0 / (2.0 * sigma - rho_prev)
            table.append((rho_next * rho_prev, 2.0 * rho_next / delta))
            rho_prev = rho_next
    return table


TABLE = chebyshev_table(SWEEPS, LOW, HIGH)
COARSE = chebyshev_table(COARSE_SWEEPS, COARSE_LOW, HIGH)

NEAR = [(-1, 0), (1, 0), (0, -1), (0, 1), (-1, -1), (-1, 1), (1, -1), (1, 1)]
FAR_Y = [(0, -2), (0, 2)]
FAR_XY = [(-1, -2), (-1, 2), (1, -2), (1, 2)]


def lanes(shape):
    return lax.broadcasted_iota(jnp.int32, shape, len(shape) - 1)


def roll(value, shift):
    shape = value.shape
    if len(shape) == 3:
        value = value.reshape(shape[0] * shape[1], shape[2])
    out = pltpu.roll(value, shift % 128, 1)
    return out.reshape(shape)


def partner(value, step):
    lane = lanes(value.shape)
    return jnp.where((lane // step) % 2 == 0, roll(value, -step), roll(value, step))


def pair_sum(value, step):
    return value + partner(value, step)


def pair_first(value, step):
    lane = lanes(value.shape)
    return jnp.where((lane // step) % 2 == 0, value, roll(value, step))


def choose(index, values):
    out = jnp.float32(values[-1])
    for i in range(len(values) - 2, -1, -1):
        out = jnp.where(index == i, jnp.float32(values[i]), out)
    return out


def kernel(
    f_in, al_in, bx_in, by_in, bz_in, out,
    b0, c0, v0, x0, t0, b1, c1, v1, x1, t1, pr,
    gc, g2, lin, a2, k2, v2, a3, k3, v3, a4, k4, v4,
    in_sem, ss, rs,
):
    gx = lax.axis_index("gx")
    gy = lax.axis_index("gy")
    counter = [0]

    def near(dx, dy):
        return (lax.rem(gx + dx + GX, GX), lax.rem(gy + dy + GY, GY))

    def gx_peer(i):
        return (lax.rem(gx + i, GX), gy)

    def gy_peer(i):
        return (gx, lax.rem(gy + i, GY))

    def remote(src, dst, index, device):
        return pltpu.make_async_remote_copy(
            src_ref=src, dst_ref=dst, send_sem=ss.at[index], recv_sem=rs.at[index],
            device_id=device, device_id_type=MESH,
        )

    def halo(view, sides, off_x, n_x, off_y, n_y, widths):
        copies = []
        for dx, dy in sides:
            first_x, last_x, first_y, last_y = widths(dx, dy)
            lo_x, w_x = (off_x, n_x) if dx == 0 else (off_x, first_x) if dx < 0 else (off_x + n_x - last_x, last_x)
            lo_y, w_y = (off_y, n_y) if dy == 0 else (off_y, first_y) if dy < 0 else (off_y + n_y - last_y, last_y)
            src = view(pl.ds(lo_x, w_x), pl.ds(lo_y, w_y))
            dst = view(pl.ds(lo_x - dx * n_x, w_x), pl.ds(lo_y - dy * n_y, w_y))
            copies.append(remote(src, dst, counter[0], near(dx, dy)))
            counter[0] += 1
        return copies

    def start(copies):
        for copy in copies:
            copy.start()

    def arrive(copies):
        for copy in copies:
            copy.wait_recv()

    def many(count, make):
        base = counter[0]
        counter[0] += count

        def each(what):
            def body(i, carry):
                what(make(i, base + i - 1))
                return carry

            lax.fori_loop(1, count + 1, body, 0)

        return each

    def own_rows(rows):
        return pl.ds(pl.multiple_of(8 * gy, 8), rows)

    def c2_gx(i, s):
        return remote(gc.at[gx, own_rows(8)], gc.at[gx, own_rows(8)], s, gx_peer(i))

    def c2_gy(i, s):
        return remote(gc.at[:, own_rows(8)], gc.at[:, own_rows(8)], s, gy_peer(i))

    def r2_gx(i, s):
        return remote(g2.at[gx, own_rows(2)], g2.at[gx, own_rows(2)], s, gx_peer(i))

    def r2_gy(i, s):
        return remote(g2.at[:, own_rows(2)], g2.at[:, own_rows(2)], s, gy_peer(i))

    send_b0 = halo(
        lambda x, y: b0.at[:, x, y], NEAR, 4, 16, 4, 8,
        lambda dx, dy: (5, 4, 5, 4) if dx == 0 or dy == 0 else (4, 4, 4, 4),
    )
    send_c1 = halo(
        lambda x, y: b1.at[pl.ds(1, 4), x, y], NEAR + FAR_Y + FAR_XY, 8, 8, 8, 4,
        lambda dx, dy: (2, 2, 2, 1) if abs(dy) == 2 else (6, 5, 4, 4),
    )
    send_f1 = halo(
        lambda x, y: b1.at[0, x, y], NEAR + FAR_Y + FAR_XY, 8, 8, 8, 4,
        lambda dx, dy: (1, 1, 1, 1) if abs(dy) == 2 else (5, 5, 4, 4),
    )
    send_x0 = halo(
        lambda x, y: x0.at[x, y], NEAR, 4, 16, 4, 8,
        lambda dx, dy: (4, 4, 4, 4) if dx == 0 or dy == 0 else (3, 3, 3, 3),
    )
    send_x1 = halo(
        lambda x, y: x1.at[x, y], NEAR + FAR_Y + FAR_XY, 8, 8, 8, 4,
        lambda dx, dy: (2, 2, 2, 2) if abs(dy) == 2 else (6, 6, 4, 4),
    )
    send_c2a = many(GX - 1, c2_gx)
    send_c2b = many(GY - 1, c2_gy)
    send_r2a = many(GX - 1, r2_gx)
    send_r2b = many(GY - 1, r2_gy)

    inputs = [
        pltpu.make_async_copy(ref, b0.at[i, pl.ds(4, 16), pl.ds(4, 8)], in_sem.at[i])
        for i, ref in enumerate((f_in, al_in, bx_in, by_in, bz_in))
    ]
    start(inputs)
    barrier = pltpu.get_barrier_semaphore()

    def greet(device):
        pl.semaphore_signal(barrier, inc=1, device_id=device, device_id_type=MESH)

    def greet_gx(i, carry):
        greet(gx_peer(i))
        return carry

    def greet_gy(i, carry):
        greet(gy_peer(i))
        return carry

    diagonal = [side for side in NEAR + FAR_XY if side[0] and side[1]]
    lax.fori_loop(1, GX, greet_gx, 0)
    lax.fori_loop(1, GY, greet_gy, 0)
    for dx, dy in diagonal:
        greet(near(dx, dy))

    for ref in (a2, a3, a4, v2, v3, v4, lin):
        flat = ref
        edge = jnp.zeros((32, 128), F32)
        if len(ref.shape) == 3:
            flat[0] = jnp.zeros(ref.shape[1:], F32)
            flat[GX + 1] = jnp.zeros(ref.shape[1:], F32)

            def rows_of(i, carry, flat=flat):
                flat[i, 0:8] = jnp.zeros((8, 128), F32)
                flat[i, 72:80] = jnp.zeros((8, 128), F32)
                return carry

            lax.fori_loop(1, GX + 1, rows_of, 0)
        else:

            def clear(i, carry, flat=flat, edge=edge):
                p, q = i // flat.shape[1], i % flat.shape[1]
                flat[p, q, 0] = edge
                flat[p, q, GX + 1] = edge
                flat[p, q, 1 : GX + 1, 0:8] = jnp.zeros((GX, 8, 128), F32)
                flat[p, q, 1 : GX + 1, 24:32] = jnp.zeros((GX, 8, 128), F32)
                return carry

            lax.fori_loop(0, flat.shape[0] * flat.shape[1], clear, 0)
    for copy in inputs:
        copy.wait()

    def split_slots(value):
        pairs = value.reshape(value.shape[0] // 2, 2, *value.shape[1:])
        return pairs[:, 0], pairs[:, 1]

    def coarsen(ref, lo, n, off, rows, step, first):
        def take(i, odd):
            return split_slots(ref[i, pl.ds(lo, n), pl.ds(off + odd, rows // 2, stride=2)])

        result = []
        for name in range(4):
            i = first + name
            even_a, even_b = take(i, 0)
            if name == 2:
                value = pair_sum(even_a + even_b, step) * 0.25
            else:
                odd_a, odd_b = take(i, 1)
                if name == 0:
                    value = pair_sum((even_a + even_b) + (odd_a + odd_b), step) * 0.125
                elif name == 1:
                    value = pair_sum(even_a + odd_a, step) * 0.25
                else:
                    value = pair_first((even_a + even_b) + (odd_a + odd_b), step) * 0.25
            result.append(value)
        return result

    for i, value in enumerate(coarsen(b0, 4, 16, 4, 8, 1, 1)):
        b1[1 + i, 8:16, 8:12] = value

    def pack(value):
        lane = lanes(value.shape[1:]) % 4
        packed = value[3]
        for i in range(2, -1, -1):
            packed = jnp.where(lane == i, value[i], packed)
        return packed

    packed = [pack(value) for value in coarsen(b1, 8, 8, 8, 4, 2, 1)]
    for i in range(4):
        gc[gx, pl.ds(8 * gy + 2 * i, 2)] = packed[i]

    pl.semaphore_wait(barrier, GX - 1 + GY - 1 + len(diagonal))

    start(send_b0)
    send_c2a(lambda copy: copy.start())
    start(send_c1)
    send_c2a(lambda copy: copy.wait_recv())
    send_c2b(lambda copy: copy.start())

    def valid(s, rows, off_x, n_x, off_y, n_y):
        x = gx * n_x + s - off_x
        y = gy * n_y + lax.broadcasted_iota(jnp.int32, (16, 128), 0) + rows - off_y
        inside = jnp.logical_and(y >= 0, y < GY * n_y)
        return jnp.logical_and(inside, jnp.logical_and(x >= 0, x < GX * n_x)), x, y

    def slots(lo, hi, body, unroll=2):
        def run(s, carry):
            body(s)
            return carry

        lax.fori_loop(lo, hi, run, 0, unroll=unroll)

    def prepare(b, c, row, scale, step, n_x, n_y, off, lo, hi):
        lane = lanes((16, 128))

        def body(s):
            ok, x, y = valid(s, row, off, n_x, off, n_y)
            low_x, low_y, low_z = b[2, s, pl.ds(row, 16)], b[3, s, pl.ds(row, 16)], b[4, s, pl.ds(row, 16)]
            up_x = jnp.where(x + 1 < GX * n_x, b[2, s + 1, pl.ds(row, 16)], 0.0)
            up_y = jnp.where(y + 1 < GY * n_y, b[3, s, pl.ds(row + 1, 16)], 0.0)
            up_z = jnp.where(lane >= 128 - step, 0.0, roll(low_z, -step))
            diagonal = SHIFT * b[1, s, pl.ds(row, 16)] + scale * (low_x + up_x + low_y + up_y + low_z + up_z)
            inverse = jnp.where(ok, 1.0 / diagonal, 0.0)
            scaled = scale * inverse
            c[1, s] = low_x * scaled
            c[2, s] = up_x * scaled
            c[3, s] = low_y * scaled
            c[4, s] = up_y * scaled
            c[5, s] = jnp.where(lane < step, 0.0, low_z * scaled)
            c[6, s] = up_z * scaled
            c[7, s] = diagonal
            c[8, s] = inverse

        slots(lo, hi, body)

    def scaled_residual(c, v, a, s, step, rows=16, off=0):
        at = pl.ds(8 + off, rows)
        centre = v[a, s + 1, at]
        k = pl.ds(off, rows)
        total = c[0, s, k] - centre
        along_x = c[1, s, k] * v[a, s, at] + c[2, s, k] * v[a, s + 2, at]
        along_y = c[3, s, k] * v[a, s + 1, pl.ds(7 + off, rows)] + c[4, s, k] * v[a, s + 1, pl.ds(9 + off, rows)]
        along_z = c[5, s, k] * roll(centre, step) + c[6, s, k] * roll(centre, -step)
        return centre, total + (along_x + along_y) + along_z

    def sweep(c, v, a, s, step, k, first):
        keep, gain = TABLE[k]
        centre, r = scaled_residual(c, v, a, s, step)
        change = gain * r
        if not first:
            change = change + keep * (centre - v[1 - a, s + 1, pl.ds(8, 16)])
        return centre + change

    def smooth_up(b, c, v, row, step, lo, hi, more=0):
        def begin(s):
            g = b[0, s, pl.ds(row, 16)] * c[8, s]
            c[0, s] = g
            v[0, s + 1, pl.ds(8, 16)] = TABLE[0][1] * g

        slots(lo - more, hi + more, begin)

        def second(s):
            keep, gain = TABLE[1]
            centre, r = scaled_residual(c, v, 0, s, step)
            v[1, s + 1, pl.ds(8, 16)] = centre + gain * r + keep * centre

        slots(lo + 1, hi - 1, second)
        for k in (2, 3):
            a = (k - 1) % 2

            def body(s, k=k, a=a):
                v[1 - a, s + 1, pl.ds(8, 16)] = sweep(c, v, a, s, step, k, False)

            slots(lo + k, hi - k, body)

    arrive(send_b0)
    prepare(b0, c0, 0, 1.0, 1, 16, 8, 4, 0, 24)
    smooth_up(b0, c0, v0, 0, 1, 0, 24)

    def resid0(i):
        total = None
        for j in range(2):
            s = 4 + 2 * i + j
            centre, r = scaled_residual(c0, v0, 1, s, 1, 8, 4)
            x0[s, 4:12] = centre
            r = r * c0[7, s, 4:12]
            total = r if total is None else total + r
        t0[i] = total

    slots(0, 8, resid0)
    both = t0[:, pl.ds(0, 4, stride=2)] + t0[:, pl.ds(1, 4, stride=2)]
    b1[0, 8:16, 8:12] = pair_sum(both, 1) * 0.125
    start(send_f1)
    start(send_x0)

    arrive(send_c1)
    prepare(b1, c1, 2, 0.25, 2, 8, 4, 8, 2, 22)
    arrive(send_f1)

    smooth_up(b1, c1, v1, 2, 2, 4, 20, 1)

    def resid1(i):
        total = None
        for j in range(2):
            s = 8 + 2 * i + j
            centre, r = scaled_residual(c1, v1, 1, s, 2, 4, 6)
            x1[s, 8:12] = centre
            r = r * c1[7, s, 6:10]
            total = r if total is None else total + r
        t1[i, 0:4] = total

    slots(0, 4, resid1)
    both = t1[:, pl.ds(0, 2, stride=2)] + t1[:, pl.ds(1, 2, stride=2)]
    g2[gx, own_rows(2)] = pack(pair_sum(both, 2) * 0.125)
    send_r2a(lambda copy: copy.start())
    start(send_x1)

    shape = (GX, 16, 128)
    lane = lanes(shape)
    lane4 = lane % 4

    def get(ref, lead, q, dx=0, dy=0):
        planes = ref.shape[1]
        row = 8
        if q + dy >= planes:
            q, row = 0, 9
        elif q + dy < 0:
            q, row = planes - 1, 7
        else:
            q = q + dy
        return ref[lead, q, pl.ds(1 + dx, GX), pl.ds(row, 16)]

    def x_next(ref, lead, q, level):
        if level == 4:
            return get(ref, lead, q, 1)
        centre, beyond = get(ref, lead, q), get(ref, lead, q, 1)
        if level == 2:
            return jnp.where(lane4 < 3, roll(centre, -1), roll(beyond, 3))
        return jnp.where(lane4 < 2, roll(centre, -2), roll(beyond, 2))

    def x_last(ref, lead, q, level):
        if level == 4:
            return get(ref, lead, q, -1)
        centre, beyond = get(ref, lead, q), get(ref, lead, q, -1)
        if level == 2:
            return jnp.where(lane4 > 0, roll(centre, 1), roll(beyond, -3))
        return jnp.where(lane4 >= 2, roll(centre, 2), roll(beyond, -2))

    def prepare_whole(a, c, level):
        scale = 0.25**level
        step = 2**level
        for q in range(a.shape[1]):
            low_x, low_y, low_z = get(a, 1, q), get(a, 2, q), get(a, 3, q)
            up_x = x_next(a, 1, q, level)
            up_y = get(a, 2, q, 0, 1)
            up_z = jnp.where(lane >= 128 - step, 0.0, roll(low_z, -step))
            diagonal = SHIFT * get(a, 0, q) + scale * (low_x + up_x + low_y + up_y + low_z + up_z)
            inverse = 1.0 / diagonal
            scaled = scale * inverse
            c[1, q] = low_x * scaled
            c[2, q] = up_x * scaled
            c[3, q] = low_y * scaled
            c[4, q] = up_y * scaled
            c[5, q] = jnp.where(lane < step, 0.0, low_z * scaled)
            c[6, q] = up_z * scaled
            c[7, q] = diagonal
            c[8, q] = inverse

    def inner(ref, lead, q, value):
        ref[lead, q, pl.ds(1, GX), pl.ds(8, 16)] = value

    def coarsen_whole(fine, coarse, z_step, x_step):
        for p in range(coarse.shape[1]):
            for name in range(4):
                value = get(fine, name, 2 * p)
                if name != 2:
                    value = value + get(fine, name, 2 * p + 1)
                value = pair_first(value, z_step) if name == 3 else pair_sum(value, z_step)
                value = pair_first(value, x_step) if name == 1 else pair_sum(value, x_step)
                inner(coarse, name, p, value * (0.125 if name == 0 else 0.25))

    def whole_residual(c, v, a, q, level):
        step = 2**level
        centre = get(v, a, q)
        total = c[0, q] - centre
        along_x = c[1, q] * x_last(v, a, q, level) + c[2, q] * x_next(v, a, q, level)
        along_y = c[3, q] * get(v, a, q, 0, -1) + c[4, q] * get(v, a, q, 0, 1)
        along_z = c[5, q] * roll(centre, step) + c[6, q] * roll(centre, -step)
        return centre, total + (along_x + along_y) + along_z

    def sweeps_whole(c, v, level, table, lo, hi):
        def body(k, carry):
            keep = choose(k, [entry[0] for entry in table])
            gain = choose(k, [entry[1] for entry in table])
            new = lax.rem(k, 2)
            old = 1 - new
            for q in range(v.shape[1]):
                centre, r = whole_residual(c, v, old, q, level)
                inner(v, new, q, centre + (gain * r + keep * (centre - get(v, new, q))))
            return carry

        lax.fori_loop(lo, hi, body, 0)

    def begin_whole(c, v, table, q, f):
        g = f * c[8, q]
        c[0, q] = g
        inner(v, 0, q, table[0][1] * g)
        inner(v, 1, q, jnp.zeros(shape, F32))

    def down(c, v, coarse_c, coarse_v, level, coarse_table):
        sweeps_whole(c, v, level, TABLE, 1, SWEEPS)
        for p in range(coarse_v.shape[1]):
            total = None
            for q in (2 * p, 2 * p + 1):
                _, r = whole_residual(c, v, 1, q, level)
                r = r * c[7, q]
                total = r if total is None else total + r
            total = pair_sum(pair_sum(total, 2**level), level - 1) * 0.125
            begin_whole(coarse_c, coarse_v, coarse_table, p, total)

    def up(c, v, coarse_v, level):
        for q in range(v.shape[1]):
            inner(v, 1, q, get(v, 1, q) + get(coarse_v, 1, q // 2))
        sweeps_whole(c, v, level, TABLE, 0, SWEEPS)

    send_c2b(lambda copy: copy.wait_recv())
    for q in range(4):
        for name in range(4):
            inner(a2, name, q, gc[:, pl.ds(8 * (q // 2) + 2 * name + q % 2, 16, stride=16)])
    prepare_whole(a2, k2, 2)
    send_r2a(lambda copy: copy.wait_recv())
    send_r2b(lambda copy: copy.start())
    coarsen_whole(a2, a3, 4, 1)
    prepare_whole(a3, k3, 3)
    coarsen_whole(a3, a4, 8, 2)
    prepare_whole(a4, k4, 4)
    send_r2b(lambda copy: copy.wait_recv())

    for q in range(4):
        begin_whole(k2, v2, TABLE, q, g2[:, pl.ds(8 * (q // 2) + q % 2, 16, stride=16)])
    down(k2, v2, k3, v3, 2, TABLE)
    down(k3, v3, k4, v4, 3, COARSE)
    sweeps_whole(k4, v4, 4, COARSE, 1, COARSE_SWEEPS)
    up(k3, v3, v4, 3)
    up(k2, v2, v3, 2)

    for q in range(4):
        lin[pl.ds(1, GX), pl.ds(8 + q, 16, stride=4)] = get(v2, 1, q)
    arrive(send_x1)
    lane_row = lanes((8, 128)) % 4

    def spread(block):
        value = lin[gx + block, pl.ds(8 + 2 * gy - 3, 8)]
        for x in range(4):
            one = jnp.where(lane_row == x, value, 0.0)
            one = pair_sum(pair_sum(one, 1), 2)
            pr[4 * block + x, pl.ds(0, 8, stride=2)] = one
            pr[4 * block + x, pl.ds(1, 8, stride=2)] = one

    slots(0, 3, spread, 1)

    def correct1(s):
        ok, _, _ = valid(s, 2, 8, 8, 8, 4)
        v1[0, s + 1, pl.ds(8, 16)] = jnp.where(ok, x1[s, pl.ds(2, 16)] + pr[s // 2], 0.0)

    slots(2, 22, correct1)

    def smooth_down(c, v, step, lo, hi, last):
        for k in range(SWEEPS):
            a = k % 2

            def body(s, k=k, a=a):
                value = sweep(c, v, a, s, step, k, k == 0)
                if k == SWEEPS - 1:
                    last(s, value)
                else:
                    v[1 - a, s + 1, pl.ds(8, 16)] = value

            slots(lo + k, hi - k, body)

    def spread0(s, value):
        t1[s - 6] = value[4:12]

    smooth_down(c1, v1, 2, 3, 21, spread0)

    def widen(i):
        pr[i, pl.ds(0, 8, stride=2)] = t1[i]
        pr[i, pl.ds(1, 8, stride=2)] = t1[i]

    slots(0, 12, widen)
    arrive(send_x0)

    def correct0(s):
        ok, _, _ = valid(s, 0, 4, 16, 4, 8)
        v0[0, s + 1, pl.ds(8, 16)] = jnp.where(ok, x0[s] + pr[s // 2], 0.0)

    slots(0, 24, correct0)

    def finish(s, value):
        out[s - 4] = value[4:12]

    smooth_down(c0, v0, 1, 1, 23, finish)

    for copy in send_b0 + send_c1 + send_f1 + send_x0 + send_x1:
        copy.wait_send()
    for each in (send_c2a, send_c2b, send_r2a, send_r2b):
        each(lambda copy: copy.wait_send())


def step(right_side, alpha, beta_x, beta_y, beta_z):
    copies = 8 + 14 + 14 + 8 + 14 + 2 * (GX - 1 + GY - 1)
    vmem = [
        (5, 25, 24, 128),
        (9, 24, 16, 128),
        (2, 26, 32, 128),
        (24, 16, 128),
        (8, 8, 128),
        (5, 25, 24, 128),
        (9, 24, 16, 128),
        (2, 26, 32, 128),
        (24, 24, 128),
        (12, 8, 128),
        (12, 16, 128),
        (GX, 8 * GY, 128),
        (GX, 8 * GY, 128),
        (GX + 2, 80, 128),
    ]
    for planes in (4, 2, 1):
        vmem += [(4, planes, GX + 2, 32, 128), (9, planes, GX, 16, 128), (2, planes, GX + 2, 32, 128)]
    return pl.pallas_call(
        kernel,
        out_shape=jax.ShapeDtypeStruct((16, 8, 128), F32),
        in_specs=[pl.BlockSpec(memory_space=pl.ANY)] * 5,
        out_specs=pl.BlockSpec(memory_space=pltpu.VMEM),
        scratch_shapes=[pltpu.VMEM(shape, F32) for shape in vmem]
        + [
            pltpu.SemaphoreType.DMA((5,)),
            pltpu.SemaphoreType.DMA((copies,)),
            pltpu.SemaphoreType.DMA((copies,)),
        ],
        compiler_params=pltpu.CompilerParams(
            collective_id=0, has_side_effects=True, vmem_limit_bytes=48 * 1024 * 1024
        ),
        name="vcycle",
    )(right_side, alpha, beta_x, beta_y, beta_z)


def solution(mesh):
    spec = P("gx", "gy", None)
    return jax.shard_map(step, mesh=mesh, in_specs=(spec,) * 5, out_specs=spec, check_vma=False)
```

```python
import functools

import jax
import jax.numpy as jnp
from jax import lax
from jax.experimental import pallas as pl
from jax.experimental.pallas import tpu as pltpu
from jax.sharding import PartitionSpec as P

MESH = pl.DeviceIdType.MESH
F32 = jnp.float32

SHIFT = 0.002
LOW = 0.25
HIGH = 2.0
COARSE_LOW = 0.1
SWEEPS = 4
COARSE_SWEEPS = 12
GX = 8
GY = 32


def chebyshev_table(count, lower, upper):
    theta = (upper + lower) / 2.0
    delta = (upper - lower) / 2.0
    sigma = theta / delta
    rho_prev = 1.0 / sigma
    table = []
    for sweep in range(count):
        if sweep == 0:
            table.append((0.0, 1.0 / theta))
        else:
            rho_next = 1.0 / (2.0 * sigma - rho_prev)
            table.append((rho_next * rho_prev, 2.0 * rho_next / delta))
            rho_prev = rho_next
    return table


TABLE = chebyshev_table(SWEEPS, LOW, HIGH)
COARSE = chebyshev_table(COARSE_SWEEPS, COARSE_LOW, HIGH)

NEAR = [(-1, 0), (1, 0), (0, -1), (0, 1), (-1, -1), (-1, 1), (1, -1), (1, 1)]
FAR_Y = [(0, -2), (0, 2)]
FAR_XY = [(-1, -2), (-1, 2), (1, -2), (1, 2)]


def lanes(shape):
    return lax.broadcasted_iota(jnp.int32, shape, len(shape) - 1)


def roll(value, shift):
    shape = value.shape
    if len(shape) == 3:
        value = value.reshape(shape[0] * shape[1], shape[2])
    out = pltpu.roll(value, shift % 128, 1)
    return out.reshape(shape)


def partner(value, step):
    lane = lanes(value.shape)
    return jnp.where((lane // step) % 2 == 0, roll(value, -step), roll(value, step))


def pair_sum(value, step):
    return value + partner(value, step)


def pair_first(value, step):
    lane = lanes(value.shape)
    return jnp.where((lane // step) % 2 == 0, value, roll(value, step))


def choose(index, values):
    out = jnp.float32(values[-1])
    for i in range(len(values) - 2, -1, -1):
        out = jnp.where(index == i, jnp.float32(values[i]), out)
    return out


def kernel(
    f_in, al_in, bx_in, by_in, bz_in, out,
    b0, c0, v0, x0, t0, b1, c1, v1, x1, t1, pr,
    gc, g2, lin, a2, k2, v2, a3, k3, v3, a4, k4, v4,
    in_sem, ss, rs,
):
    gx = lax.axis_index("gx")
    gy = lax.axis_index("gy")
    counter = [0]

    def near(dx, dy):
        return (lax.rem(gx + dx + GX, GX), lax.rem(gy + dy + GY, GY))

    def gx_peer(i):
        return (lax.rem(gx + i, GX), gy)

    def gy_peer(i):
        return (gx, lax.rem(gy + i, GY))

    def remote(src, dst, index, device):
        return pltpu.make_async_remote_copy(
            src_ref=src, dst_ref=dst, send_sem=ss.at[index], recv_sem=rs.at[index],
            device_id=device, device_id_type=MESH,
        )

    def halo(view, sides, off_x, n_x, off_y, n_y, widths):
        copies = []
        for dx, dy in sides:
            first_x, last_x, first_y, last_y = widths(dx, dy)
            lo_x, w_x = (off_x, n_x) if dx == 0 else (off_x, first_x) if dx < 0 else (off_x + n_x - last_x, last_x)
            lo_y, w_y = (off_y, n_y) if dy == 0 else (off_y, first_y) if dy < 0 else (off_y + n_y - last_y, last_y)
            src = view(pl.ds(lo_x, w_x), pl.ds(lo_y, w_y))
            dst = view(pl.ds(lo_x - dx * n_x, w_x), pl.ds(lo_y - dy * n_y, w_y))
            copies.append(remote(src, dst, counter[0], near(dx, dy)))
            counter[0] += 1
        return copies

    def start(copies):
        for copy in copies:
            copy.start()

    def arrive(copies):
        for copy in copies:
            copy.wait_recv()

    def many(count, make):
        base = counter[0]
        counter[0] += count

        def each(what):
            def body(i, carry):
                what(make(i, base + i - 1))
                return carry

            lax.fori_loop(1, count + 1, body, 0)

        return each

    def own_rows(rows):
        return pl.ds(pl.multiple_of(8 * gy, 8), rows)

    def c2_gx(i, s):
        return remote(gc.at[gx, own_rows(8)], gc.at[gx, own_rows(8)], s, gx_peer(i))

    def c2_gy(i, s):
        return remote(gc.at[:, own_rows(8)], gc.at[:, own_rows(8)], s, gy_peer(2 * i))

    def c2_core(i, s):
        rows = pl.ds(pl.multiple_of(8 * lax.rem(gy - 2 * (i - 1) + GY, GY), 8), 8)
        return remote(gc.at[:, rows], gc.at[:, rows], s, (gx, gy + 1 - 2 * lax.rem(gy, 2)))

    def r2_gx(i, s):
        return remote(g2.at[gx, own_rows(2)], g2.at[gx, own_rows(2)], s, gx_peer(i))

    send_b0 = halo(
        lambda x, y: b0.at[:, x, y], NEAR, 4, 16, 4, 8,
        lambda dx, dy: (5, 4, 5, 4) if dx == 0 or dy == 0 else (4, 4, 4, 4),
    )
    send_c1 = halo(
        lambda x, y: b1.at[pl.ds(1, 4), x, y], NEAR + FAR_Y + FAR_XY, 8, 8, 8, 4,
        lambda dx, dy: (2, 2, 2, 1) if abs(dy) == 2 else (6, 5, 4, 4),
    )
    send_f1 = halo(
        lambda x, y: b1.at[0, x, y], NEAR, 8, 8, 8, 4,
        lambda dx, dy: (4, 4, 4, 4) if dx == 0 or dy == 0 else (3, 3, 3, 3),
    )
    send_x0 = halo(
        lambda x, y: x0.at[x, y], NEAR, 4, 16, 4, 8,
        lambda dx, dy: (4, 4, 4, 4) if dx == 0 or dy == 0 else (3, 3, 3, 3),
    )
    send_x1 = halo(
        lambda x, y: x1.at[:, x, y], NEAR + FAR_Y + FAR_XY, 8, 8, 8, 4,
        lambda dx, dy: (2, 2, 2, 2) if abs(dy) == 2 else (6, 6, 4, 4),
    )
    send_c2a = many(GX - 1, c2_gx)
    c2b_base = counter[0]
    send_c2b = many(GY // 2 - 1, c2_gy)
    send_c2c = many(GY // 2, c2_core)
    send_r2a = many(GX - 1, r2_gx)
    send_r2b = []
    for a, b, e in sorted(
        [(a, b, e) for a in range(4) for b in range(4) for e in range(2) if a + b + e],
        key=lambda t: -(2 * min(t[0], 4 - t[0]) + 2 * min(t[1], 4 - t[1]) + t[2]),
    ):
        x, y, core = lax.rem(gy // 8 + a, 4), lax.rem(gy // 2 + b, 4), lax.rem(gy + e, 2)
        own = g2.at[:, own_rows(2)]
        send_r2b.append(remote(own, own, counter[0], (gx, 8 * x + 2 * y + core)))
        counter[0] += 1

    inputs = [
        pltpu.make_async_copy(ref, b0.at[i, pl.ds(4, 16), pl.ds(4, 8)], in_sem.at[i])
        for i, ref in enumerate((f_in, al_in, bx_in, by_in, bz_in))
    ]
    start(inputs)
    barrier = pltpu.get_barrier_semaphore()

    def greet(device):
        pl.semaphore_signal(barrier, inc=1, device_id=device, device_id_type=MESH)

    def greet_gx(i, carry):
        greet(gx_peer(i))
        return carry

    def greet_gy(i, carry):
        greet(gy_peer(i))
        return carry

    diagonal = [side for side in NEAR + FAR_XY if side[0] and side[1]]
    lax.fori_loop(1, GX, greet_gx, 0)
    lax.fori_loop(1, GY, greet_gy, 0)
    for dx, dy in diagonal:
        greet(near(dx, dy))

    edge = jnp.zeros((32, 128), F32)
    side = jnp.zeros((GX, 8, 128), F32)
    for ref in (a2, a3, a4, v2, v3, v4):

        def clear(i, carry, ref=ref):
            p, q = i // ref.shape[1], i % ref.shape[1]
            ref[p, q, 0] = edge
            ref[p, q, GX + 1] = edge
            ref[p, q, 1 : GX + 1, 0:8] = side
            ref[p, q, 1 : GX + 1, 24:32] = side
            return carry

        lax.fori_loop(0, ref.shape[0] * ref.shape[1], clear, 0)
    for copy in inputs:
        copy.wait()

    def split_slots(value):
        pairs = value.reshape(value.shape[0] // 2, 2, *value.shape[1:])
        return pairs[:, 0], pairs[:, 1]

    def coarsen(ref, lo, n, off, rows, step, first):
        def take(i, odd):
            return split_slots(ref[i, pl.ds(lo, n), pl.ds(off + odd, rows // 2, stride=2)])

        result = []
        for name in range(4):
            i = first + name
            even_a, even_b = take(i, 0)
            if name == 2:
                value = pair_sum(even_a + even_b, step) * 0.25
            else:
                odd_a, odd_b = take(i, 1)
                if name == 0:
                    value = pair_sum((even_a + even_b) + (odd_a + odd_b), step) * 0.125
                elif name == 1:
                    value = pair_sum(even_a + odd_a, step) * 0.25
                else:
                    value = pair_first((even_a + even_b) + (odd_a + odd_b), step) * 0.25
            result.append(value)
        return result

    for i, value in enumerate(coarsen(b0, 4, 16, 4, 8, 1, 1)):
        b1[1 + i, 8:16, 8:12] = value

    def pack(value):
        lane = lanes(value.shape[1:]) % 4
        packed = value[3]
        for i in range(2, -1, -1):
            packed = jnp.where(lane == i, value[i], packed)
        return packed

    packed = [pack(value) for value in coarsen(b1, 8, 8, 8, 4, 2, 1)]
    for i in range(4):
        gc[gx, pl.ds(8 * gy + 2 * i, 2)] = packed[i]

    pl.semaphore_wait(barrier, GX - 1 + GY - 1 + len(diagonal))

    start(send_b0)
    send_c2a(lambda copy: copy.start())
    start(send_c1)
    send_c2a(lambda copy: copy.wait_recv())
    send_c2b(lambda copy: copy.start())

    def valid(s, rows, off_x, n_x, off_y, n_y):
        x = gx * n_x + s - off_x
        y = gy * n_y + lax.broadcasted_iota(jnp.int32, (16, 128), 0) + rows - off_y
        inside = jnp.logical_and(y >= 0, y < GY * n_y)
        return jnp.logical_and(inside, jnp.logical_and(x >= 0, x < GX * n_x)), x, y

    def slots(lo, hi, body, unroll=4):
        def run(s, carry):
            body(s)
            return carry

        lax.fori_loop(lo, hi, run, 0, unroll=unroll)

    def prepare(b, c, row, scale, step, n_x, n_y, off, lo, hi):
        lane = lanes((16, 128))

        def body(s):
            ok, x, y = valid(s, row, off, n_x, off, n_y)
            low_x, low_y, low_z = b[2, s, pl.ds(row, 16)], b[3, s, pl.ds(row, 16)], b[4, s, pl.ds(row, 16)]
            up_x = jnp.where(x + 1 < GX * n_x, b[2, s + 1, pl.ds(row, 16)], 0.0)
            up_y = jnp.where(y + 1 < GY * n_y, b[3, s, pl.ds(row + 1, 16)], 0.0)
            up_z = jnp.where(lane >= 128 - step, 0.0, roll(low_z, -step))
            diagonal = SHIFT * b[1, s, pl.ds(row, 16)] + scale * (low_x + up_x + low_y + up_y + low_z + up_z)
            inverse = jnp.where(ok, 1.0 / diagonal, 0.0)
            scaled = scale * inverse
            c[1, s] = low_x * scaled
            c[2, s] = up_x * scaled
            c[3, s] = low_y * scaled
            c[4, s] = up_y * scaled
            c[5, s] = jnp.where(lane < step, 0.0, low_z * scaled)
            c[6, s] = up_z * scaled
            c[7, s] = diagonal
            c[8, s] = inverse

        slots(lo, hi, body)

    def scaled_residual(c, v, a, s, step, rows=16, off=0):
        at = pl.ds(8 + off, rows)
        centre = v[a, s + 1, at]
        k = pl.ds(off, rows)
        total = c[0, s, k] - centre
        along_x = c[1, s, k] * v[a, s, at] + c[2, s, k] * v[a, s + 2, at]
        along_y = c[3, s, k] * v[a, s + 1, pl.ds(7 + off, rows)] + c[4, s, k] * v[a, s + 1, pl.ds(9 + off, rows)]
        along_z = c[5, s, k] * roll(centre, step) + c[6, s, k] * roll(centre, -step)
        return centre, total + (along_x + along_y) + along_z

    def sweep(c, v, a, s, step, k, first):
        keep, gain = TABLE[k]
        centre, r = scaled_residual(c, v, a, s, step)
        change = gain * r
        if not first:
            change = change + keep * (centre - v[1 - a, s + 1, pl.ds(8, 16)])
        return centre + change

    def smooth_up(b, c, v, row, step, lo, hi):
        def begin(s):
            g = b[0, s, pl.ds(row, 16)] * c[8, s]
            c[0, s] = g
            v[0, s + 1, pl.ds(8, 16)] = TABLE[0][1] * g

        slots(lo, hi, begin)

        def second(s):
            keep, gain = TABLE[1]
            centre, r = scaled_residual(c, v, 0, s, step)
            v[1, s + 1, pl.ds(8, 16)] = centre + gain * r + keep * centre

        slots(lo + 1, hi - 1, second)
        for k in (2, 3):
            a = (k - 1) % 2

            def body(s, k=k, a=a):
                v[1 - a, s + 1, pl.ds(8, 16)] = sweep(c, v, a, s, step, k, False)

            slots(lo + k, hi - k, body)

    arrive(send_b0)
    prepare(b0, c0, 0, 1.0, 1, 16, 8, 4, 0, 24)
    smooth_up(b0, c0, v0, 0, 1, 0, 24)

    def resid0(i):
        total = None
        for j in range(2):
            s = 4 + 2 * i + j
            centre, r = scaled_residual(c0, v0, 1, s, 1, 8, 4)
            x0[s, 4:12] = centre
            r = r * c0[7, s, 4:12]
            total = r if total is None else total + r
        t0[i] = total

    slots(0, 8, resid0)
    both = t0[:, pl.ds(0, 4, stride=2)] + t0[:, pl.ds(1, 4, stride=2)]
    f1 = pair_sum(both, 1) * 0.125
    b1[0, 8:16, 8:12] = f1
    x1[1, 8:16, 8:12] = f1
    start(send_f1)
    start(send_x0)

    arrive(send_c1)
    prepare(b1, c1, 2, 0.25, 2, 8, 4, 8, 2, 22)

    def forward(i, carry):
        @pl.when(i > 1)
        def _():
            c2_gy(i - 1, c2b_base + i - 2).wait_recv()

        c2_core(i, c2b_base + GY // 2 + i - 2).start()
        return carry

    lax.fori_loop(1, GY // 2 + 1, forward, 0)
    arrive(send_f1)

    smooth_up(b1, c1, v1, 2, 2, 4, 20)

    def resid1(i):
        total = None
        for j in range(2):
            s = 8 + 2 * i + j
            centre, r = scaled_residual(c1, v1, 1, s, 2, 4, 6)
            x1[0, s, 8:12] = centre
            r = r * c1[7, s, 6:10]
            total = r if total is None else total + r
        t1[i, 0:4] = total

    slots(0, 4, resid1)
    both = t1[:, pl.ds(0, 2, stride=2)] + t1[:, pl.ds(1, 2, stride=2)]
    g2[gx, own_rows(2)] = pack(pair_sum(both, 2) * 0.125)
    send_r2a(lambda copy: copy.start())
    start(send_x1)

    HALVES = [(0, GX, 0, 8), (0, GX, 8, 8)]

    def lane_of(value):
        return lanes(value.shape)

    def get(ref, lead, q, win, dy=0, wide=False):
        planes = ref.shape[1]
        row = 8
        if q + dy >= planes:
            q, row = 0, 9
        elif q + dy < 0:
            q, row = planes - 1, 7
        else:
            q = q + dy
        x0, nx, r0, nr = win
        start, count = (x0, nx + 2) if wide else (x0 + 1, nx)
        return ref[lead, q, pl.ds(start, count), pl.ds(row + r0, nr)]

    def put(ref, lead, q, win, value):
        x0, nx, r0, nr = win
        ref[lead, q, pl.ds(x0 + 1, nx), pl.ds(8 + r0, nr)] = value

    def x_next(wide, level):
        if level == 4:
            return wide[2:]
        lane4 = lane_of(wide[1:-1]) % 4
        if level == 2:
            return roll(jnp.where(lane4 == 0, roll(wide[2:], 4), wide[1:-1]), -1)
        return jnp.where(lane4 < 2, roll(wide[1:-1], -2), roll(wide[2:], 2))

    def around(wide, level):
        step = 2**level
        centre = wide[1:-1]
        lane4 = lane_of(centre) % 4
        if level == 4:
            return wide[:-2], wide[2:], roll(centre, step), roll(centre, -step)
        if level == 2:
            low, high = roll(wide[1:], 4), roll(wide[:-1], -4)
            x_low = roll(jnp.where(lane4 == 3, high[:-1], centre), 1)
            x_high = roll(jnp.where(lane4 == 0, low[1:], centre), -1)
            return x_low, x_high, low[:-1], high[1:]
        other = jnp.where(lane_of(wide) % 4 < 2, roll(wide, -2), roll(wide, 2))
        x_low = jnp.where(lane4 >= 2, other[1:-1], other[:-2])
        x_high = jnp.where(lane4 < 2, other[1:-1], other[2:])
        return x_low, x_high, roll(centre, step), roll(centre, -step)

    def prepare_whole(a, c, level):
        scale = 0.25**level
        step = 2**level
        for q in range(a.shape[1]):
            for win in HALVES:
                low_x, low_y, low_z = get(a, 1, q, win), get(a, 2, q, win), get(a, 3, q, win)
                up_x = x_next(get(a, 1, q, win, wide=True), level)
                up_y = get(a, 2, q, win, 1)
                lane = lane_of(low_z)
                up_z = jnp.where(lane >= 128 - step, 0.0, roll(low_z, -step))
                diagonal = SHIFT * get(a, 0, q, win) + scale * (low_x + up_x + low_y + up_y + low_z + up_z)
                inverse = 1.0 / diagonal
                scaled = scale * inverse
                put_c(c, 1, q, win, low_x * scaled)
                put_c(c, 2, q, win, up_x * scaled)
                put_c(c, 3, q, win, low_y * scaled)
                put_c(c, 4, q, win, up_y * scaled)
                put_c(c, 5, q, win, jnp.where(lane < step, 0.0, low_z * scaled))
                put_c(c, 6, q, win, up_z * scaled)
                put_c(c, 7, q, win, diagonal)
                put_c(c, 8, q, win, inverse)

    def put_c(c, i, q, win, value):
        x0, nx, r0, nr = win
        c[i, q, pl.ds(x0, nx), pl.ds(r0, nr)] = value

    def get_c(c, i, q, win):
        x0, nx, r0, nr = win
        return c[i, q, pl.ds(x0, nx), pl.ds(r0, nr)]

    def coarsen_whole(fine, coarse, z_step, x_step):
        for p in range(coarse.shape[1]):
            for win in HALVES:
                for name in range(4):
                    value = get(fine, name, 2 * p, win)
                    if name != 2:
                        value = value + get(fine, name, 2 * p + 1, win)
                    value = pair_first(value, z_step) if name == 3 else pair_sum(value, z_step)
                    value = pair_first(value, x_step) if name == 1 else pair_sum(value, x_step)
                    put(coarse, name, p, win, value * (0.125 if name == 0 else 0.25))

    def whole_residual(c, v, a, q, win, level):
        wide = get(v, a, q, win, wide=True)
        centre = wide[1:-1]
        x_low, x_high, z_low, z_high = around(wide, level)
        along_x = get_c(c, 1, q, win) * x_low + get_c(c, 2, q, win) * x_high
        along_y = get_c(c, 3, q, win) * get(v, a, q, win, -1) + get_c(c, 4, q, win) * get(v, a, q, win, 1)
        along_z = get_c(c, 5, q, win) * z_low + get_c(c, 6, q, win) * z_high
        return centre, (get_c(c, 0, q, win) - centre) + (along_x + along_y) + along_z

    def sweeps_whole(c, v, level, table, lo, hi, wins):
        def body(k, carry):
            keep = choose(k, [entry[0] for entry in table])
            gain = choose(k, [entry[1] for entry in table])
            new = lax.rem(k, 2)
            old = 1 - new
            for q in range(v.shape[1]):
                for win in wins:
                    centre, r = whole_residual(c, v, old, q, win, level)
                    change = gain * r + keep * (centre - get(v, new, q, win))
                    put(v, new, q, win, centre + change)
            return carry

        lax.fori_loop(lo, hi, body, 0)

    def begin_whole(c, v, table, q, win, f):
        g = f * get_c(c, 8, q, win)
        put_c(c, 0, q, win, g)
        put(v, 0, q, win, table[0][1] * g)
        put(v, 1, q, win, jnp.zeros_like(g))

    def down(c, v, coarse_c, coarse_v, level, coarse_table):
        sweeps_whole(c, v, level, TABLE, 1, SWEEPS, HALVES)
        for p in range(coarse_v.shape[1]):
            for win in HALVES:
                total = None
                for q in (2 * p, 2 * p + 1):
                    _, r = whole_residual(c, v, 1, q, win, level)
                    r = r * get_c(c, 7, q, win)
                    total = r if total is None else total + r
                total = pair_sum(pair_sum(total, 2**level), level - 1) * 0.125
                begin_whole(coarse_c, coarse_v, coarse_table, p, win, total)

    def up(c, v, coarse_v, level, wins):
        for q in range(v.shape[1]):
            for win in wins:
                put(v, 1, q, win, get(v, 1, q, win) + get(coarse_v, 1, q // 2, win))
        sweeps_whole(c, v, level, TABLE, 0, SWEEPS, wins)

    send_c2c(lambda copy: copy.wait_recv())
    for q in range(4):
        for name in range(4):
            a2[name, q, pl.ds(1, GX), pl.ds(8, 16)] = gc[:, pl.ds(8 * (q // 2) + 2 * name + q % 2, 16, stride=16)]
    prepare_whole(a2, k2, 2)
    send_r2a(lambda copy: copy.wait_recv())
    start(send_r2b)
    coarsen_whole(a2, a3, 4, 1)
    prepare_whole(a3, k3, 3)
    coarsen_whole(a3, a4, 8, 2)
    prepare_whole(a4, k4, 4)
    arrive(send_r2b)

    for q in range(4):
        begin_whole(k2, v2, TABLE, q, (0, GX, 0, 16), g2[:, pl.ds(8 * (q // 2) + q % 2, 16, stride=16)])
    down(k2, v2, k3, v3, 2, TABLE)
    down(k3, v3, k4, v4, 3, COARSE)
    sweeps_whole(k4, v4, 4, COARSE, 1, COARSE_SWEEPS, HALVES)
    up(k3, v3, v4, 3, HALVES)
    near_x = jnp.clip(gx - 2, 0, GX - 5)
    near_row = jnp.clip((2 * gy + 1) // 4 - 2, 0, 8)
    near2 = (near_x, 5, near_row, 8)
    up(k2, v2, v3, 2, [near2])

    for q in range(4):
        lin[pl.ds(1, 5), pl.ds(8 + q, 8, stride=4)] = get(v2, 1, q, near2)
    arrive(send_x1)
    lane_row = lanes((8, 128)) % 4

    def spread(block):
        value = lin[gx - near_x + block, pl.ds(8 + 2 * gy - 3 - 4 * near_row, 8)]
        for x in range(4):
            one = jnp.where(lane_row == x, value, 0.0)
            one = pair_sum(pair_sum(one, 1), 2)
            pr[4 * block + x, pl.ds(0, 8, stride=2)] = one
            pr[4 * block + x, pl.ds(1, 8, stride=2)] = one

    slots(0, 3, spread, 1)

    def correct1(s):
        ok, _, _ = valid(s, 2, 8, 8, 8, 4)
        v1[0, s + 1, pl.ds(8, 16)] = jnp.where(ok, x1[0, s, pl.ds(2, 16)] + pr[s // 2], 0.0)
        c1[0, s] = jnp.where(ok, x1[1, s, pl.ds(2, 16)] * c1[8, s], 0.0)

    slots(2, 22, correct1)

    def smooth_down(c, v, step, lo, hi, last):
        for k in range(SWEEPS):
            a = k % 2

            def body(s, k=k, a=a):
                value = sweep(c, v, a, s, step, k, k == 0)
                if k == SWEEPS - 1:
                    last(s, value)
                else:
                    v[1 - a, s + 1, pl.ds(8, 16)] = value

            slots(lo + k, hi - k, body)

    def spread0(s, value):
        t1[s - 6] = value[4:12]

    smooth_down(c1, v1, 2, 3, 21, spread0)

    def widen(i):
        pr[i, pl.ds(0, 8, stride=2)] = t1[i]
        pr[i, pl.ds(1, 8, stride=2)] = t1[i]

    slots(0, 12, widen)
    arrive(send_x0)

    def correct0(s):
        ok, _, _ = valid(s, 0, 4, 16, 4, 8)
        v0[0, s + 1, pl.ds(8, 16)] = jnp.where(ok, x0[s] + pr[s // 2], 0.0)

    slots(0, 24, correct0)

    def finish(s, value):
        out[s - 4] = value[4:12]

    smooth_down(c0, v0, 1, 1, 23, finish)

    for copy in send_b0 + send_c1 + send_f1 + send_x0 + send_x1 + send_r2b:
        copy.wait_send()
    for each in (send_c2a, send_c2b, send_c2c, send_r2a):
        each(lambda copy: copy.wait_send())


def step(right_side, alpha, beta_x, beta_y, beta_z):
    copies = 8 + 14 + 8 + 8 + 14 + 2 * (GX - 1 + GY - 1)
    vmem = [
        (5, 25, 24, 128),
        (9, 24, 16, 128),
        (2, 26, 32, 128),
        (24, 16, 128),
        (8, 8, 128),
        (5, 25, 24, 128),
        (9, 24, 16, 128),
        (2, 26, 32, 128),
        (2, 24, 24, 128),
        (12, 8, 128),
        (12, 16, 128),
        (GX, 8 * GY, 128),
        (GX, 8 * GY, 128),
        (7, 48, 128),
    ]
    for planes in (4, 2, 1):
        vmem += [(4, planes, GX + 2, 32, 128), (9, planes, GX, 16, 128), (2, planes, GX + 2, 32, 128)]
    return pl.pallas_call(
        kernel,
        out_shape=jax.ShapeDtypeStruct((16, 8, 128), F32),
        in_specs=[pl.BlockSpec(memory_space=pl.ANY)] * 5,
        out_specs=pl.BlockSpec(memory_space=pltpu.VMEM),
        scratch_shapes=[pltpu.VMEM(shape, F32) for shape in vmem]
        + [
            pltpu.SemaphoreType.DMA((5,)),
            pltpu.SemaphoreType.DMA((copies,)),
            pltpu.SemaphoreType.DMA((copies,)),
        ],
        compiler_params=pltpu.CompilerParams(
            collective_id=0, has_side_effects=True, vmem_limit_bytes=60 * 1024 * 1024
        ),
        name="vcycle",
    )(right_side, alpha, beta_x, beta_y, beta_z)


def solution(mesh):
    spec = P("gx", "gy", None)
    return jax.shard_map(step, mesh=mesh, in_specs=(spec,) * 5, out_specs=spec, check_vma=False)
```

```python
import functools

import jax
import jax.numpy as jnp
from jax import lax
from jax.experimental import pallas as pl
from jax.experimental.pallas import tpu as pltpu
from jax.sharding import PartitionSpec as P

MESH = pl.DeviceIdType.MESH
F32 = jnp.float32

SHIFT = 0.002
LOW = 0.25
HIGH = 2.0
COARSE_LOW = 0.1
SWEEPS = 4
COARSE_SWEEPS = 12
GX = 8
GY = 32


def chebyshev_table(count, lower, upper):
    theta = (upper + lower) / 2.0
    delta = (upper - lower) / 2.0
    sigma = theta / delta
    rho_prev = 1.0 / sigma
    table = []
    for sweep in range(count):
        if sweep == 0:
            table.append((0.0, 1.0 / theta))
        else:
            rho_next = 1.0 / (2.0 * sigma - rho_prev)
            table.append((rho_next * rho_prev, 2.0 * rho_next / delta))
            rho_prev = rho_next
    return table


TABLE = chebyshev_table(SWEEPS, LOW, HIGH)
COARSE = chebyshev_table(COARSE_SWEEPS, COARSE_LOW, HIGH)

NEAR = [(-1, 0), (1, 0), (0, -1), (0, 1), (-1, -1), (-1, 1), (1, -1), (1, 1)]
FAR_Y = [(0, -2), (0, 2)]
FAR_XY = [(-1, -2), (-1, 2), (1, -2), (1, 2)]


def lanes(shape):
    return lax.broadcasted_iota(jnp.int32, shape, len(shape) - 1)


def roll(value, shift):
    shape = value.shape
    if len(shape) == 3:
        value = value.reshape(shape[0] * shape[1], shape[2])
    out = pltpu.roll(value, shift % 128, 1)
    return out.reshape(shape)


def partner(value, step):
    lane = lanes(value.shape)
    return jnp.where((lane // step) % 2 == 0, roll(value, -step), roll(value, step))


def pair_sum(value, step):
    return value + partner(value, step)


def pair_first(value, step):
    lane = lanes(value.shape)
    return jnp.where((lane // step) % 2 == 0, value, roll(value, step))


def kernel(
    f_in, al_in, bx_in, by_in, bz_in, out,
    b0, c0, w0, v0a, v0b, x0, t0, b1, c1, w1, v1a, v1b, x1, t1, pr,
    gc, g2, turn, lin, a2, k2, w2, v2a, v2b, a3, k3, a4, k4,
    in_sem, ss, rs,
):
    v0, v1 = (v0a, v0b), (v1a, v1b)
    gx = lax.axis_index("gx")
    gy = lax.axis_index("gy")
    counter = [0]

    def near(dx, dy):
        return (lax.rem(gx + dx + GX, GX), lax.rem(gy + dy + GY, GY))

    def gx_peer(i):
        return (lax.rem(gx + i, GX), gy)

    def gy_peer(i):
        return (gx, lax.rem(gy + i, GY))

    def remote(src, dst, index, device):
        return pltpu.make_async_remote_copy(
            src_ref=src, dst_ref=dst, send_sem=ss.at[index], recv_sem=rs.at[index],
            device_id=device, device_id_type=MESH,
        )

    def halo(view, sides, off_x, n_x, off_y, n_y, widths):
        copies = []
        for dx, dy in sides:
            first_x, last_x, first_y, last_y = widths(dx, dy)
            lo_x, w_x = (off_x, n_x) if dx == 0 else (off_x, first_x) if dx < 0 else (off_x + n_x - last_x, last_x)
            lo_y, w_y = (off_y, n_y) if dy == 0 else (off_y, first_y) if dy < 0 else (off_y + n_y - last_y, last_y)
            src = view(pl.ds(lo_x, w_x), pl.ds(lo_y, w_y))
            dst = view(pl.ds(lo_x - dx * n_x, w_x), pl.ds(lo_y - dy * n_y, w_y))
            copies.append(remote(src, dst, counter[0], near(dx, dy)))
            counter[0] += 1
        return copies

    def start(copies):
        for copy in copies:
            copy.start()

    def arrive(copies):
        for copy in copies:
            copy.wait_recv()

    def many(count, make):
        base = counter[0]
        counter[0] += count

        def each(what):
            def body(i, carry):
                what(make(i, base + i - 1))
                return carry

            lax.fori_loop(1, count + 1, body, 0)

        return each

    def own_rows(rows):
        return pl.ds(pl.multiple_of(8 * gy, 8), rows)

    def c2_gx(i, s):
        return remote(gc.at[gx, own_rows(8)], gc.at[gx, own_rows(8)], s, gx_peer(i))

    def c2_gy(i, s):
        return remote(gc.at[:, own_rows(8)], gc.at[:, own_rows(8)], s, gy_peer(2 * i))

    def c2_core(i, s):
        rows = pl.ds(pl.multiple_of(8 * lax.rem(gy - 2 * (i - 1) + GY, GY), 8), 8)
        return remote(gc.at[:, rows], gc.at[:, rows], s, (gx, gy + 1 - 2 * lax.rem(gy, 2)))

    def r2_gx(i, s):
        return remote(g2.at[gx, own_rows(2)], g2.at[gx, own_rows(2)], s, gx_peer(i))

    send_b0 = halo(
        lambda x, y: b0.at[:, x, y], NEAR, 4, 16, 4, 8,
        lambda dx, dy: (5, 4, 5, 4) if dx == 0 or dy == 0 else (4, 4, 4, 4),
    )
    send_c1 = halo(
        lambda x, y: b1.at[pl.ds(1, 4), x, y], NEAR + FAR_Y + FAR_XY, 8, 8, 8, 4,
        lambda dx, dy: (2, 2, 2, 1) if abs(dy) == 2 else (6, 5, 4, 4),
    )
    send_f1 = halo(
        lambda x, y: b1.at[0, x, y], NEAR, 8, 8, 8, 4,
        lambda dx, dy: (4, 4, 4, 4) if dx == 0 or dy == 0 else (3, 3, 3, 3),
    )
    send_x0 = halo(
        lambda x, y: x0.at[x, y], NEAR, 4, 16, 4, 8,
        lambda dx, dy: (4, 4, 4, 4) if dx == 0 or dy == 0 else (3, 3, 3, 3),
    )
    send_x1 = halo(
        lambda x, y: x1.at[:, x, y], NEAR + FAR_Y + FAR_XY, 8, 8, 8, 4,
        lambda dx, dy: (2, 2, 2, 2) if abs(dy) == 2 else (6, 6, 4, 4),
    )
    send_c2a = many(GX - 1, c2_gx)
    c2b_base = counter[0]
    send_c2b = many(GY // 2 - 1, c2_gy)
    send_c2c = many(GY // 2, c2_core)
    send_r2a = many(GX - 1, r2_gx)
    send_r2b = []
    for a, b, e in sorted(
        [(a, b, e) for a in range(4) for b in range(4) for e in range(2) if a + b + e],
        key=lambda t: -(2 * min(t[0], 4 - t[0]) + 2 * min(t[1], 4 - t[1]) + t[2]),
    ):
        x, y, core = lax.rem(gy // 8 + a, 4), lax.rem(gy // 2 + b, 4), lax.rem(gy + e, 2)
        own = g2.at[:, own_rows(2)]
        send_r2b.append(remote(own, own, counter[0], (gx, 8 * x + 2 * y + core)))
        counter[0] += 1

    inputs = [
        pltpu.make_async_copy(ref, b0.at[i, pl.ds(4, 16), pl.ds(4, 8)], in_sem.at[i])
        for i, ref in enumerate((f_in, al_in, bx_in, by_in, bz_in))
    ]
    start(inputs)
    barrier = pltpu.get_barrier_semaphore()

    def greet(device):
        pl.semaphore_signal(barrier, inc=1, device_id=device, device_id_type=MESH)

    def greet_gx(i, carry):
        greet(gx_peer(i))
        return carry

    def greet_gy(i, carry):
        greet(gy_peer(i))
        return carry

    diagonal = [side for side in NEAR + FAR_XY if side[0] and side[1]]
    lax.fori_loop(1, GX, greet_gx, 0)
    lax.fori_loop(1, GY, greet_gy, 0)
    for dx, dy in diagonal:
        greet(near(dx, dy))

    for copy in inputs:
        copy.wait()

    def split_slots(value):
        pairs = value.reshape(value.shape[0] // 2, 2, *value.shape[1:])
        return pairs[:, 0], pairs[:, 1]

    def coarsen(ref, lo, n, off, rows, step, first):
        def take(i, odd):
            return split_slots(ref[i, pl.ds(lo, n), pl.ds(off + odd, rows // 2, stride=2)])

        result = []
        for name in range(4):
            i = first + name
            even_a, even_b = take(i, 0)
            if name == 2:
                value = pair_sum(even_a + even_b, step) * 0.25
            else:
                odd_a, odd_b = take(i, 1)
                if name == 0:
                    value = pair_sum((even_a + even_b) + (odd_a + odd_b), step) * 0.125
                elif name == 1:
                    value = pair_sum(even_a + odd_a, step) * 0.25
                else:
                    value = pair_first((even_a + even_b) + (odd_a + odd_b), step) * 0.25
            result.append(value)
        return result

    for i, value in enumerate(coarsen(b0, 4, 16, 4, 8, 1, 1)):
        b1[1 + i, 8:16, 8:12] = value

    def pack(value):
        lane = lanes(value.shape[1:]) % 4
        packed = value[3]
        for i in range(2, -1, -1):
            packed = jnp.where(lane == i, value[i], packed)
        return packed

    packed = [pack(value) for value in coarsen(b1, 8, 8, 8, 4, 2, 1)]
    for i in range(4):
        gc[gx, pl.ds(8 * gy + 2 * i, 2)] = packed[i]

    pl.semaphore_wait(barrier, GX - 1 + GY - 1 + len(diagonal))

    start(send_b0)
    send_c2a(lambda copy: copy.start())
    start(send_c1)
    send_c2a(lambda copy: copy.wait_recv())
    send_c2b(lambda copy: copy.start())

    def valid(s, rows, off_x, n_x, off_y, n_y):
        x = gx * n_x + s - off_x
        y = gy * n_y + lax.broadcasted_iota(jnp.int32, (16, 128), 0) + rows - off_y
        inside = jnp.logical_and(y >= 0, y < GY * n_y)
        return jnp.logical_and(inside, jnp.logical_and(x >= 0, x < GX * n_x)), x, y

    def slots(lo, hi, body, unroll=4):
        def run(s, carry):
            body(s)
            return carry

        lax.fori_loop(lo, hi, run, 0, unroll=unroll)

    def prepare(b, c, row, scale, step, n_x, n_y, off, lo, hi):
        lane = lanes((16, 128))

        def body(s):
            ok, x, y = valid(s, row, off, n_x, off, n_y)
            low_x, low_y, low_z = b[2, s, pl.ds(row, 16)], b[3, s, pl.ds(row, 16)], b[4, s, pl.ds(row, 16)]
            up_x = jnp.where(x + 1 < GX * n_x, b[2, s + 1, pl.ds(row, 16)], 0.0)
            up_y = jnp.where(y + 1 < GY * n_y, b[3, s, pl.ds(row + 1, 16)], 0.0)
            up_z = jnp.where(lane >= 128 - step, 0.0, roll(low_z, -step))
            diagonal = SHIFT * b[1, s, pl.ds(row, 16)] + scale * (low_x + up_x + low_y + up_y + low_z + up_z)
            inverse = jnp.where(ok, 1.0 / diagonal, 0.0)
            scaled = scale * inverse
            c[1, s] = low_x * scaled
            c[2, s] = up_x * scaled
            c[3, s] = low_y * scaled
            c[4, s] = up_y * scaled
            c[5, s] = jnp.where(lane < step, 0.0, low_z * scaled)
            c[6, s] = up_z * scaled
            c[7, s] = diagonal
            c[8, s] = inverse

        slots(lo, hi, body)

    def scaled_residual(c, w, v, s, step, rows=16, off=0):
        at = pl.ds(8 + off, rows)
        centre = v[s + 1, at]
        k = pl.ds(off, rows)
        total = w[s, k] - centre
        along_x = c[1, s, k] * v[s, at] + c[2, s, k] * v[s + 2, at]
        along_y = c[3, s, k] * v[s + 1, pl.ds(7 + off, rows)] + c[4, s, k] * v[s + 1, pl.ds(9 + off, rows)]
        along_z = c[5, s, k] * roll(centre, step) + c[6, s, k] * roll(centre, -step)
        return centre, total + (along_x + along_y) + along_z

    def sweep(c, w, v, a, s, step, k, first, rows=16, off=0):
        keep, gain = TABLE[k]
        centre, r = scaled_residual(c, w, v[a], s, step, rows, off)
        change = gain * r
        if not first:
            change = change + keep * (centre - v[1 - a][s + 1, pl.ds(8 + off, rows)])
        return centre + change

    def smooth_up(b, c, w, v, row, step, lo, hi, rows, off):
        def begin(s):
            g = b[0, s, pl.ds(row, 16)] * c[8, s]
            w[s] = g
            v[0][s + 1, pl.ds(8, 16)] = TABLE[0][1] * g

        slots(lo, hi, begin)

        def second(s):
            keep, gain = TABLE[1]
            centre, r = scaled_residual(c, w, v[0], s, step)
            v[1][s + 1, pl.ds(8, 16)] = centre + gain * r + keep * centre

        slots(lo + 1, hi - 1, second)
        for k in (2, 3):
            a = (k - 1) % 2

            def body(s, k=k, a=a):
                v[1 - a][s + 1, pl.ds(8 + off, rows)] = sweep(c, w, v, a, s, step, k, False, rows, off)

            slots(lo + k, hi - k, body)

    arrive(send_b0)
    prepare(b0, c0, 0, 1.0, 1, 16, 8, 4, 0, 24)
    smooth_up(b0, c0, w0, v0, 0, 1, 0, 24, 16, 0)

    def resid0(i):
        total = None
        for j in range(2):
            s = 4 + 2 * i + j
            centre, r = scaled_residual(c0, w0, v0[1], s, 1, 8, 4)
            x0[s, 4:12] = centre
            r = r * c0[7, s, 4:12]
            total = r if total is None else total + r
        t0[i] = total

    slots(0, 8, resid0)
    both = t0[:, pl.ds(0, 4, stride=2)] + t0[:, pl.ds(1, 4, stride=2)]
    f1 = pair_sum(both, 1) * 0.125
    b1[0, 8:16, 8:12] = f1
    x1[1, 8:16, 8:12] = f1
    start(send_f1)
    start(send_x0)

    arrive(send_c1)
    prepare(b1, c1, 2, 0.25, 2, 8, 4, 8, 2, 22)

    def forward(i, carry):
        @pl.when(i > 1)
        def _():
            c2_gy(i - 1, c2b_base + i - 2).wait_recv()

        c2_core(i, c2b_base + GY // 2 + i - 2).start()
        return carry

    lax.fori_loop(1, GY // 2 + 1, forward, 0)
    arrive(send_f1)

    smooth_up(b1, c1, w1, v1, 2, 2, 4, 20, 8, 4)

    def resid1(i):
        total = None
        for j in range(2):
            s = 8 + 2 * i + j
            centre, r = scaled_residual(c1, w1, v1[1], s, 2, 4, 6)
            x1[0, s, 8:12] = centre
            r = r * c1[7, s, 6:10]
            total = r if total is None else total + r
        t1[i, 0:4] = total

    slots(0, 4, resid1)
    both = t1[:, pl.ds(0, 2, stride=2)] + t1[:, pl.ds(1, 2, stride=2)]
    g2[gx, own_rows(2)] = pack(pair_sum(both, 2) * 0.125)
    send_r2a(lambda copy: copy.start())
    start(send_x1)

    tile = (1, 8, 128)
    sub = lax.broadcasted_iota(jnp.int32, tile, 1)
    lane = lanes(tile)
    ENDS = {"x": (lane // 16 == 0, lane // 16 == 7), "y": (lane % 16 == 0, lane % 16 == 15), "z": (sub == 0, sub == 7)}

    def turned(value, shift):
        return pltpu.roll(value, shift % 8, 1)

    def high(get, n, j, k, axis):
        if axis == "x":
            value = get(j, k)
            last = roll(value[:1], -16)
            return last if n == 1 else jnp.concatenate([value[1:], last], axis=0)
        if axis == "y":
            return get(j + 1, k) if j + 1 < n else roll(get(0, k), -1)
        return get(j, k + 1) if k + 1 < n else turned(get(j, 0), -1)

    def low(get, n, j, k, axis):
        if axis == "x":
            value = get(j, k)
            first = roll(value[n - 1 :], 16)
            return first if n == 1 else jnp.concatenate([first, value[: n - 1]], axis=0)
        if axis == "y":
            return get(j - 1, k) if j > 0 else roll(get(n - 1, k), 1)
        return get(j, k - 1) if k > 0 else turned(get(j, n - 1), 1)

    def without(value, n, j, k, axis, end):
        edge = (n - 1) * end
        mask = ENDS[axis][end]
        if axis == "x":
            parts = [value[i : i + 1] for i in range(n)]
            parts[edge] = jnp.where(mask, 0.0, parts[edge])
            return parts[0] if n == 1 else jnp.concatenate(parts, axis=0)
        if (j if axis == "y" else k) != edge:
            return value
        return jnp.where(mask, 0.0, value)

    def blocks(n):
        return [(j, k) for j in range(n) for k in range(n)]

    def prepare_whole(a, c, level):
        scale = 0.25**level
        n = a.shape[1]
        for j, k in blocks(n):
            diagonal = SHIFT * a[0, j, k]
            faces = []
            for i, axis in enumerate("xyz"):
                below = a[1 + i, j, k]
                above = high(lambda j, k, i=i: a[1 + i, j, k], n, j, k, axis)
                above = without(above, n, j, k, axis, 1)
                faces.append((without(below, n, j, k, axis, 0), above))
                diagonal = diagonal + scale * (below + above)
            inverse = 1.0 / diagonal
            scaled = scale * inverse
            for i, (below, above) in enumerate(faces):
                c[1 + 2 * i, j, k] = below * scaled
                c[2 + 2 * i, j, k] = above * scaled
            c[7, j, k] = diagonal
            c[8, j, k] = inverse

    def coarser(take, n, j, k, skip=""):
        total = None
        for fine_j in (2 * j, 2 * j + 1)[: 1 if skip == "y" else 2]:
            for fine_k in (2 * k, 2 * k + 1)[: 1 if skip == "z" else 2]:
                value = take(fine_j, fine_k)
                total = value if total is None else total + value
        pairs = total.reshape(n // 2, 2, 8, 128)
        return pairs[:, 0] if skip == "x" else pairs[:, 0] + pairs[:, 1]

    def coarsen_whole(fine, coarse):
        n = fine.shape[1]
        for j, k in blocks(n // 2):
            for i, skip in enumerate(("", "x", "y", "z")):
                value = coarser(lambda j, k, i=i: fine[i, j, k], n, j, k, skip)
                coarse[i, j, k] = value * (0.25 if skip else 0.125)

    def whole_residual(c, w, get, n, j, k):
        centre = get(j, k)
        parts = []
        for i, axis in enumerate("xyz"):
            parts.append(c[1 + 2 * i, j, k] * low(get, n, j, k, axis) + c[2 + 2 * i, j, k] * high(get, n, j, k, axis))
        return centre, (w(j, k) - centre) + (parts[0] + parts[1]) + parts[2]

    class InRefs:
        def __init__(self, ref):
            self.ref = ref

        def __call__(self, j, k):
            return self.ref[j, k]

        def put(self, j, k, value):
            self.ref[j, k] = value

    class InValues:
        def __init__(self):
            self.values = {}

        def __call__(self, j, k):
            return self.values[j, k]

        def put(self, j, k, value):
            self.values[j, k] = value

    def sweeps_whole(c, w, old, new, n, table, lo, hi):
        for sweep_index in range(lo, hi):
            keep, gain = table[sweep_index]
            results = []
            for j, k in blocks(n):
                centre, r = whole_residual(c, w, old, n, j, k)
                change = gain * r
                if sweep_index == 1 and lo == 1:
                    change = change + keep * centre
                elif sweep_index:
                    change = change + keep * (centre - new(j, k))
                if isinstance(new, InRefs):
                    new.put(j, k, centre + change)
                else:
                    results.append((j, k, centre + change))
            if results:
                new = InValues()
                for j, k, value in results:
                    new.put(j, k, value)
            old, new = new, old
        return old, new

    def start_whole(c, w, v, n, table, f):
        for j, k in blocks(n):
            g = f(j, k) * c[8, j, k]
            w.put(j, k, g)
            v.put(j, k, table[0][1] * g)

    def restricted(c, w, v, n):
        result = InValues()
        scaled = InValues()
        for j, k in blocks(n):
            _, r = whole_residual(c, w, v, n, j, k)
            scaled.put(j, k, r * c[7, j, k])
        for j, k in blocks(n // 2):
            result.put(j, k, coarser(scaled, n, j, k) * 0.125)
        return result

    def corrected(v, coarse, n, into):
        for j, k in blocks(n):
            value = coarse(j // 2, k // 2)
            value = jnp.broadcast_to(value[:, None], (n // 2, 2, 8, 128)).reshape(n, 8, 128)
            into.put(j, k, v(j, k) + value)

    send_c2c(lambda copy: copy.wait_recv())
    for j in range(4):
        for name in range(4):
            rows = gc[:, pl.ds(8 * (j // 2) + 2 * name + j % 2, 16, stride=16)]
            turn[name, j] = rows.reshape(128, 128).T
    for j in range(4):
        for name in range(4):
            for k in range(4):
                for i in range(4):
                    a2[name, j, k, i] = turn[name, j, pl.ds(4 * k + i, 8, stride=16)]
    prepare_whole(a2, k2, 2)
    send_r2a(lambda copy: copy.wait_recv())
    start(send_r2b)
    coarsen_whole(a2, a3)
    prepare_whole(a3, k3, 3)
    coarsen_whole(a3, a4)
    prepare_whole(a4, k4, 4)
    arrive(send_r2b)

    for j in range(4):
        rows = g2[:, pl.ds(8 * (j // 2) + j % 2, 16, stride=16)]
        turn[4, j] = rows.reshape(128, 128).T

    def f2(j, k):
        return jnp.stack([turn[4, j, pl.ds(4 * k + i, 8, stride=16)] for i in range(4)])

    field2, before2, source2 = InRefs(v2a), InRefs(v2b), InRefs(w2)
    start_whole(k2, source2, field2, 4, TABLE, f2)
    field2, before2 = sweeps_whole(k2, source2, field2, before2, 4, TABLE, 1, SWEEPS)
    field3, source3 = InValues(), InValues()
    start_whole(k3, source3, field3, 2, TABLE, restricted(k2, source2, field2, 4))
    field3, _ = sweeps_whole(k3, source3, field3, InValues(), 2, TABLE, 1, SWEEPS)
    field4, source4 = InValues(), InValues()
    start_whole(k4, source4, field4, 1, COARSE, restricted(k3, source3, field3, 2))
    field4, _ = sweeps_whole(k4, source4, field4, InValues(), 1, COARSE, 1, COARSE_SWEEPS)
    next3 = InValues()
    corrected(field3, field4, 2, next3)
    field3, _ = sweeps_whole(k3, source3, next3, InValues(), 2, TABLE, 0, SWEEPS)
    corrected(field2, field3, 4, field2)
    field2, _ = sweeps_whole(k2, source2, field2, before2, 4, TABLE, 0, SWEEPS)

    for j in range(4):
        for k in range(4):
            value = field2(j, k)
            for i in range(4):
                turn[4, j, pl.ds(4 * k + i, 8, stride=16)] = value[i]
    for j in range(4):
        lin[pl.ds(1, GX), pl.ds(8 + j, 16, stride=4)] = turn[4, j].T.reshape(GX, 16, 128)
    arrive(send_x1)
    lane_row = lanes((8, 128)) % 4

    def spread(block):
        value = lin[gx + block, pl.ds(8 + 2 * gy - 3, 8)]
        for x in range(4):
            one = jnp.where(lane_row == x, value, 0.0)
            one = pair_sum(pair_sum(one, 1), 2)
            pr[4 * block + x, pl.ds(0, 8, stride=2)] = one
            pr[4 * block + x, pl.ds(1, 8, stride=2)] = one

    slots(0, 3, spread, 1)

    def correct1(s):
        ok, _, _ = valid(s, 2, 8, 8, 8, 4)
        v1[0][s + 1, pl.ds(8, 16)] = jnp.where(ok, x1[0, s, pl.ds(2, 16)] + pr[s // 2], 0.0)
        w1[s] = jnp.where(ok, x1[1, s, pl.ds(2, 16)] * c1[8, s], 0.0)

    slots(2, 22, correct1)

    def smooth_down(c, w, v, step, lo, hi, last):
        for k in range(SWEEPS):
            a = k % 2

            def body(s, k=k, a=a):
                if k == SWEEPS - 1:
                    last(s, sweep(c, w, v, a, s, step, k, False, 8, 4))
                    return
                value = sweep(c, w, v, a, s, step, k, k == 0)
                v[1 - a][s + 1, pl.ds(8, 16)] = value

            slots(lo + k, hi - k, body)

    def spread0(s, value):
        t1[s - 6] = value

    smooth_down(c1, w1, v1, 2, 3, 21, spread0)

    def widen(i):
        pr[i, pl.ds(0, 8, stride=2)] = t1[i]
        pr[i, pl.ds(1, 8, stride=2)] = t1[i]

    slots(0, 12, widen)
    arrive(send_x0)

    def correct0(s):
        ok, _, _ = valid(s, 0, 4, 16, 4, 8)
        v0[0][s + 1, pl.ds(8, 16)] = jnp.where(ok, x0[s] + pr[s // 2], 0.0)

    slots(0, 24, correct0)

    def finish(s, value):
        out[s - 4] = value

    smooth_down(c0, w0, v0, 1, 1, 23, finish)

    for copy in send_b0 + send_c1 + send_f1 + send_x0 + send_x1 + send_r2b:
        copy.wait_send()
    for each in (send_c2a, send_c2b, send_c2c, send_r2a):
        each(lambda copy: copy.wait_send())


def step(right_side, alpha, beta_x, beta_y, beta_z):
    copies = 8 + 14 + 8 + 8 + 14 + 2 * (GX - 1 + GY - 1)
    vmem = [
        (5, 25, 24, 128),
        (9, 24, 16, 128),
        (24, 16, 128),
        (26, 32, 128),
        (26, 32, 128),
        (24, 16, 128),
        (8, 8, 128),
        (5, 25, 24, 128),
        (9, 24, 16, 128),
        (24, 16, 128),
        (26, 32, 128),
        (26, 32, 128),
        (2, 24, 24, 128),
        (12, 8, 128),
        (12, 16, 128),
        (GX, 8 * GY, 128),
        (GX, 8 * GY, 128),
        (5, 4, 128, 128),
        (GX + 2, 80, 128),
    ]
    for n in (4, 2, 1):
        vmem += [(4, n, n, n, 8, 128), (9, n, n, n, 8, 128)]
        if n == 4:
            vmem += [(n, n, n, 8, 128)] * 3
    return pl.pallas_call(
        kernel,
        out_shape=jax.ShapeDtypeStruct((16, 8, 128), F32),
        in_specs=[pl.BlockSpec(memory_space=pl.ANY)] * 5,
        out_specs=pl.BlockSpec(memory_space=pltpu.VMEM),
        scratch_shapes=[pltpu.VMEM(shape, F32) for shape in vmem]
        + [
            pltpu.SemaphoreType.DMA((5,)),
            pltpu.SemaphoreType.DMA((copies,)),
            pltpu.SemaphoreType.DMA((copies,)),
        ],
        compiler_params=pltpu.CompilerParams(
            collective_id=0, has_side_effects=True, vmem_limit_bytes=60 * 1024 * 1024
        ),
        name="vcycle",
    )(right_side, alpha, beta_x, beta_y, beta_z)


def solution(mesh):
    spec = P("gx", "gy", None)
    return jax.shard_map(step, mesh=mesh, in_specs=(spec,) * 5, out_specs=spec, check_vma=False)
```

```python
import functools

import jax
import jax.numpy as jnp
from jax import lax
from jax.experimental import pallas as pl
from jax.experimental.pallas import tpu as pltpu
from jax.sharding import PartitionSpec as P

MESH = pl.DeviceIdType.MESH
F32 = jnp.float32

SHIFT = 0.002
LOW = 0.25
HIGH = 2.0
COARSE_LOW = 0.1
SWEEPS = 4
COARSE_SWEEPS = 12
GX = 8
GY = 32
CHUNK = 4
FAR_FIRST = [4, 3, 5, 2, 6, 1, 7]
LINE = sorted(
    [(a, b, e) for a in range(4) for b in range(4) for e in range(2) if a + b + e],
    key=lambda t: -(2 * min(t[0], 4 - t[0]) + 2 * min(t[1], 4 - t[1]) + t[2]),
)


def chebyshev_table(count, lower, upper):
    theta = (upper + lower) / 2.0
    delta = (upper - lower) / 2.0
    sigma = theta / delta
    rho_prev = 1.0 / sigma
    table = []
    for sweep in range(count):
        if sweep == 0:
            table.append((0.0, 1.0 / theta))
        else:
            rho_next = 1.0 / (2.0 * sigma - rho_prev)
            table.append((rho_next * rho_prev, 2.0 * rho_next / delta))
            rho_prev = rho_next
    return table


TABLE = chebyshev_table(SWEEPS, LOW, HIGH)
COARSE = chebyshev_table(COARSE_SWEEPS, COARSE_LOW, HIGH)

NEAR = [(-1, 0), (1, 0), (0, -1), (0, 1), (-1, -1), (-1, 1), (1, -1), (1, 1)]
FAR_Y = [(0, -2), (0, 2)]
FAR_XY = [(-1, -2), (-1, 2), (1, -2), (1, 2)]


def lanes(shape):
    return lax.broadcasted_iota(jnp.int32, shape, len(shape) - 1)


def roll(value, shift):
    shape = value.shape
    if len(shape) == 3:
        value = value.reshape(shape[0] * shape[1], shape[2])
    out = pltpu.roll(value, shift % 128, 1)
    return out.reshape(shape)


def partner(value, step):
    lane = lanes(value.shape)
    return jnp.where((lane // step) % 2 == 0, roll(value, -step), roll(value, step))


def pair_sum(value, step):
    return value + partner(value, step)


def pair_first(value, step):
    lane = lanes(value.shape)
    return jnp.where((lane // step) % 2 == 0, value, roll(value, step))


def kernel(
    f_in, al_in, bx_in, by_in, bz_in, out,
    b0, c0, w0, v0a, v0b, x0, t0, b1, c1, w1, v1a, v1b, x1, t1, pr,
    gc, g2, turn, lin, a2, k2, w2, v2a, v2b, a3, k3, a4, k4,
    in_sem, ss, rs,
):
    v0, v1 = (v0a, v0b), (v1a, v1b)
    gx = lax.axis_index("gx")
    gy = lax.axis_index("gy")
    counter = [0]

    def near(dx, dy):
        return (lax.rem(gx + dx + GX, GX), lax.rem(gy + dy + GY, GY))

    def gx_peer(i):
        return (lax.rem(gx + i, GX), gy)

    def gy_peer(i):
        return (gx, lax.rem(gy + i, GY))

    def remote(src, dst, index, device):
        return pltpu.make_async_remote_copy(
            src_ref=src, dst_ref=dst, send_sem=ss.at[index], recv_sem=rs.at[index],
            device_id=device, device_id_type=MESH,
        )

    def halo(view, sides, off_x, n_x, off_y, n_y, widths):
        copies = []
        for dx, dy in sides:
            first_x, last_x, first_y, last_y = widths(dx, dy)
            lo_x, w_x = (off_x, n_x) if dx == 0 else (off_x, first_x) if dx < 0 else (off_x + n_x - last_x, last_x)
            lo_y, w_y = (off_y, n_y) if dy == 0 else (off_y, first_y) if dy < 0 else (off_y + n_y - last_y, last_y)
            src = view(pl.ds(lo_x, w_x), pl.ds(lo_y, w_y))
            dst = view(pl.ds(lo_x - dx * n_x, w_x), pl.ds(lo_y - dy * n_y, w_y))
            copies.append(remote(src, dst, counter[0], near(dx, dy)))
            counter[0] += 1
        return copies

    def start(copies):
        for copy in copies:
            copy.start()

    def arrive(copies):
        for copy in copies:
            copy.wait_recv()

    def many(count, make):
        base = counter[0]
        counter[0] += count

        def each(what):
            def body(i, carry):
                what(make(i, base + i - 1))
                return carry

            lax.fori_loop(1, count + 1, body, 0)

        return each

    def own_rows(rows):
        return pl.ds(pl.multiple_of(8 * gy, 8), rows)

    def c2_gx(i, s):
        return remote(gc.at[gx, own_rows(8)], gc.at[gx, own_rows(8)], s, gx_peer(i))

    def c2_gy(i, s):
        return remote(gc.at[:, own_rows(8)], gc.at[:, own_rows(8)], s, gy_peer(2 * i))

    def c2_core(i, s):
        rows = pl.ds(pl.multiple_of(8 * lax.rem(gy - 2 * (i - 1) + GY, GY), 8), 8)
        return remote(gc.at[:, rows], gc.at[:, rows], s, (gx, gy + 1 - 2 * lax.rem(gy, 2)))

    def r2_gx(i):
        counter[0] += 1
        return remote(g2.at[gx, own_rows(2)], g2.at[gx, own_rows(2)], counter[0] - 1, gx_peer(i))

    send_b0 = halo(
        lambda x, y: b0.at[:, x, y], NEAR, 4, 16, 4, 8,
        lambda dx, dy: (5, 4, 5, 4) if dx == 0 or dy == 0 else (4, 4, 4, 4),
    )
    send_c1 = halo(
        lambda x, y: b1.at[pl.ds(1, 4), x, y], NEAR + FAR_Y + FAR_XY, 8, 8, 8, 4,
        lambda dx, dy: (2, 2, 2, 1) if abs(dy) == 2 else (6, 5, 4, 4),
    )
    send_f1 = halo(
        lambda x, y: b1.at[0, x, y], NEAR, 8, 8, 8, 4,
        lambda dx, dy: (4, 4, 4, 4) if dx == 0 or dy == 0 else (3, 3, 3, 3),
    )
    send_x0 = halo(
        lambda x, y: x0.at[x, y], NEAR, 4, 16, 4, 8,
        lambda dx, dy: (4, 4, 4, 4) if dx == 0 or dy == 0 else (3, 3, 3, 3),
    )
    send_x1 = halo(
        lambda x, y: x1.at[:, x, y], NEAR + FAR_Y + FAR_XY, 8, 8, 8, 4,
        lambda dx, dy: (2, 2, 2, 2) if abs(dy) == 2 else (6, 6, 4, 4),
    )
    send_c2a = many(GX - 1, c2_gx)
    c2b_base = counter[0]
    send_c2b = many(GY // 2 - 1, c2_gy)
    send_c2c = many(GY // 2, c2_core)
    send_r2a = [r2_gx(i) for i in FAR_FIRST]
    along_x = [8 * lax.rem(gy // 8 + a, 4) for a in range(4)]
    along_y = [2 * lax.rem(gy // 2 + b, 4) for b in range(4)]
    core = [lax.rem(gy + e, 2) for e in range(2)]
    line = [(gx, along_x[a] + along_y[b] + core[e]) for a, b, e in LINE]
    send_r2b = []
    for device in line:
        own = g2.at[:, own_rows(2)]
        send_r2b.append(remote(own, own, counter[0], device))
        counter[0] += 1

    inputs = [
        pltpu.make_async_copy(ref, b0.at[i, pl.ds(4, 16), pl.ds(4, 8)], in_sem.at[i])
        for i, ref in enumerate((f_in, al_in, bx_in, by_in, bz_in))
    ]
    start(inputs)
    barrier = pltpu.get_barrier_semaphore()

    def greet(device):
        pl.semaphore_signal(barrier, inc=1, device_id=device, device_id_type=MESH)

    diagonal = [side for side in NEAR + FAR_XY if side[0] and side[1]]
    for device in line[:18]:
        greet(device)
    for i in FAR_FIRST:
        greet(gx_peer(i))
    for dx, dy in diagonal:
        greet(near(dx, dy))
    for device in line[18:]:
        greet(device)

    for copy in inputs:
        copy.wait()

    def split_slots(value):
        pairs = value.reshape(value.shape[0] // 2, 2, *value.shape[1:])
        return pairs[:, 0], pairs[:, 1]

    def coarsen(ref, lo, n, off, rows, step, first):
        def take(i, odd):
            return split_slots(ref[i, pl.ds(lo, n), pl.ds(off + odd, rows // 2, stride=2)])

        result = []
        for name in range(4):
            i = first + name
            even_a, even_b = take(i, 0)
            if name == 2:
                value = pair_sum(even_a + even_b, step) * 0.25
            else:
                odd_a, odd_b = take(i, 1)
                if name == 0:
                    value = pair_sum((even_a + even_b) + (odd_a + odd_b), step) * 0.125
                elif name == 1:
                    value = pair_sum(even_a + odd_a, step) * 0.25
                else:
                    value = pair_first((even_a + even_b) + (odd_a + odd_b), step) * 0.25
            result.append(value)
        return result

    for i, value in enumerate(coarsen(b0, 4, 16, 4, 8, 1, 1)):
        b1[1 + i, 8:16, 8:12] = value

    def pack(value):
        lane = lanes(value.shape[1:]) % 4
        packed = value[3]
        for i in range(2, -1, -1):
            packed = jnp.where(lane == i, value[i], packed)
        return packed

    packed = [pack(value) for value in coarsen(b1, 8, 8, 8, 4, 2, 1)]
    for i in range(4):
        gc[gx, pl.ds(8 * gy + 2 * i, 2)] = packed[i]

    pl.semaphore_wait(barrier, GX - 1 + GY - 1 + len(diagonal))

    start(send_b0)
    send_c2a(lambda copy: copy.start())
    start(send_c1)
    send_c2a(lambda copy: copy.wait_recv())
    send_c2b(lambda copy: copy.start())

    def valid(s, rows, off_x, n_x, off_y, n_y):
        shape = (CHUNK, 16, 128)
        x = gx * n_x + s - off_x + lax.broadcasted_iota(jnp.int32, shape, 0)
        y = gy * n_y + rows - off_y + lax.broadcasted_iota(jnp.int32, shape, 1)
        inside = jnp.logical_and(y >= 0, y < GY * n_y)
        return jnp.logical_and(inside, jnp.logical_and(x >= 0, x < GX * n_x)), x, y

    def slots(lo, hi, body):
        runs = -(-(hi - lo) // CHUNK)
        first = lo - (runs * CHUNK - (hi - lo)) // 2

        def run(i, carry):
            body(first + CHUNK * i)
            return carry

        lax.fori_loop(0, runs, run, 0, unroll=2)

    def some(s):
        return pl.ds(s, CHUNK)

    def prepare(b, c, row, scale, step, n_x, n_y, off, lo, hi):
        def body(s):
            at = pl.ds(row, 16)
            ok, x, y = valid(s, row, off, n_x, off, n_y)
            lane = lanes(ok.shape)
            low_x, low_y, low_z = b[2, some(s), at], b[3, some(s), at], b[4, some(s), at]
            up_x = jnp.where(x + 1 < GX * n_x, b[2, some(s + 1), at], 0.0)
            up_y = jnp.where(y + 1 < GY * n_y, b[3, some(s), pl.ds(row + 1, 16)], 0.0)
            up_z = jnp.where(lane >= 128 - step, 0.0, roll(low_z, -step))
            diagonal = SHIFT * b[1, some(s), at] + scale * (low_x + up_x + low_y + up_y + low_z + up_z)
            inverse = jnp.where(ok, 1.0 / diagonal, 0.0)
            scaled = scale * inverse
            c[1, some(s)] = low_x * scaled
            c[2, some(s)] = up_x * scaled
            c[3, some(s)] = low_y * scaled
            c[4, some(s)] = up_y * scaled
            c[5, some(s)] = jnp.where(lane < step, 0.0, low_z * scaled)
            c[6, some(s)] = up_z * scaled
            c[7, some(s)] = diagonal
            c[8, some(s)] = inverse

        slots(lo, hi, body)

    def scaled_residual(c, w, v, s, step, rows=16, off=0):
        at = pl.ds(8 + off, rows)
        centre = v[some(s + 1), at]
        k = pl.ds(off, rows)
        t = some(s)
        total = w[t, k] - centre
        along_x = c[1, t, k] * v[t, at] + c[2, t, k] * v[some(s + 2), at]
        before, after = v[some(s + 1), pl.ds(7 + off, rows)], v[some(s + 1), pl.ds(9 + off, rows)]
        along_y = c[3, t, k] * before + c[4, t, k] * after
        along_z = c[5, t, k] * roll(centre, step) + c[6, t, k] * roll(centre, -step)
        return centre, total + (along_x + along_y) + along_z

    def sweep(c, w, v, a, s, step, k, first, rows=16, off=0):
        keep, gain = TABLE[k]
        centre, r = scaled_residual(c, w, v[a], s, step, rows, off)
        change = gain * r
        if not first:
            change = change + keep * (centre - v[1 - a][some(s + 1), pl.ds(8 + off, rows)])
        return centre + change

    def smooth_up(b, c, w, v, row, step, lo, hi, rows, off):
        def begin(s):
            g = b[0, some(s), pl.ds(row, 16)] * c[8, some(s)]
            w[some(s)] = g
            v[0][some(s + 1), pl.ds(8, 16)] = TABLE[0][1] * g

        slots(lo, hi, begin)

        def second(s):
            keep, gain = TABLE[1]
            centre, r = scaled_residual(c, w, v[0], s, step)
            v[1][some(s + 1), pl.ds(8, 16)] = centre + gain * r + keep * centre

        slots(lo + 1, hi - 1, second)
        for k in (2, 3):
            a = (k - 1) % 2

            def body(s, k=k, a=a):
                v[1 - a][some(s + 1), pl.ds(8 + off, rows)] = sweep(c, w, v, a, s, step, k, False, rows, off)

            slots(lo + k, hi - k, body)

    def pair_slots(value):
        first, second = split_slots(value)
        return first + second

    arrive(send_b0)
    prepare(b0, c0, 0, 1.0, 1, 16, 8, 4, 0, 24)
    smooth_up(b0, c0, w0, v0, 0, 1, 0, 24, 16, 0)

    def resid0(s):
        centre, r = scaled_residual(c0, w0, v0[1], s, 1, 8, 4)
        x0[some(s), 4:12] = centre
        t0[pl.ds((s - 4) // 2, CHUNK // 2)] = pair_slots(r * c0[7, some(s), 4:12])

    slots(4, 20, resid0)
    both = t0[:, pl.ds(0, 4, stride=2)] + t0[:, pl.ds(1, 4, stride=2)]
    f1 = pair_sum(both, 1) * 0.125
    b1[0, 8:16, 8:12] = f1
    x1[1, 8:16, 8:12] = f1
    start(send_f1)
    start(send_x0)

    arrive(send_c1)
    prepare(b1, c1, 2, 0.25, 2, 8, 4, 8, 2, 22)

    def forward(i, carry):
        @pl.when(i > 1)
        def _():
            c2_gy(i - 1, c2b_base + i - 2).wait_recv()

        c2_core(i, c2b_base + GY // 2 + i - 2).start()
        return carry

    lax.fori_loop(1, GY // 2 + 1, forward, 0)
    arrive(send_f1)

    smooth_up(b1, c1, w1, v1, 2, 2, 4, 20, 8, 4)

    def resid1(s):
        centre, r = scaled_residual(c1, w1, v1[1], s, 2, 4, 6)
        x1[0, some(s), 8:12] = centre
        t1[pl.ds((s - 8) // 2, CHUNK // 2), 0:4] = pair_slots(r * c1[7, some(s), 6:10])

    slots(8, 16, resid1)
    both = t1[0:4, pl.ds(0, 2, stride=2)] + t1[0:4, pl.ds(1, 2, stride=2)]
    g2[gx, own_rows(2)] = pack(pair_sum(both, 2) * 0.125)
    start(send_r2a)
    start(send_x1)

    tile = (1, 8, 128)
    sub = lax.broadcasted_iota(jnp.int32, tile, 1)
    lane = lanes(tile)
    ENDS = {"x": (lane // 16 == 0, lane // 16 == 7), "y": (lane % 16 == 0, lane % 16 == 15), "z": (sub == 0, sub == 7)}

    def turned(value, shift):
        return pltpu.roll(value, shift % 8, 1)

    def high(get, n, j, k, axis):
        if axis == "x":
            value = get(j, k)
            last = roll(value[:1], -16)
            return last if n == 1 else jnp.concatenate([value[1:], last], axis=0)
        if axis == "y":
            return get(j + 1, k) if j + 1 < n else roll(get(0, k), -1)
        return get(j, k + 1) if k + 1 < n else turned(get(j, 0), -1)

    def low(get, n, j, k, axis):
        if axis == "x":
            value = get(j, k)
            first = roll(value[n - 1 :], 16)
            return first if n == 1 else jnp.concatenate([first, value[: n - 1]], axis=0)
        if axis == "y":
            return get(j - 1, k) if j > 0 else roll(get(n - 1, k), 1)
        return get(j, k - 1) if k > 0 else turned(get(j, n - 1), 1)

    def without(value, n, j, k, axis, end):
        edge = (n - 1) * end
        mask = ENDS[axis][end]
        if axis == "x":
            parts = [value[i : i + 1] for i in range(n)]
            parts[edge] = jnp.where(mask, 0.0, parts[edge])
            return parts[0] if n == 1 else jnp.concatenate(parts, axis=0)
        if (j if axis == "y" else k) != edge:
            return value
        return jnp.where(mask, 0.0, value)

    def blocks(n):
        return [(j, k) for j in range(n) for k in range(n)]

    def prepare_whole(a, c, level):
        scale = 0.25**level
        n = a.shape[1]
        for j, k in blocks(n):
            diagonal = SHIFT * a[0, j, k]
            faces = []
            for i, axis in enumerate("xyz"):
                below = a[1 + i, j, k]
                above = high(lambda j, k, i=i: a[1 + i, j, k], n, j, k, axis)
                above = without(above, n, j, k, axis, 1)
                faces.append((without(below, n, j, k, axis, 0), above))
                diagonal = diagonal + scale * (below + above)
            inverse = 1.0 / diagonal
            scaled = scale * inverse
            for i, (below, above) in enumerate(faces):
                c[1 + 2 * i, j, k] = below * scaled
                c[2 + 2 * i, j, k] = above * scaled
            c[7, j, k] = diagonal
            c[8, j, k] = inverse

    def coarser(take, n, j, k, skip=""):
        total = None
        for fine_j in (2 * j, 2 * j + 1)[: 1 if skip == "y" else 2]:
            for fine_k in (2 * k, 2 * k + 1)[: 1 if skip == "z" else 2]:
                value = take(fine_j, fine_k)
                total = value if total is None else total + value
        pairs = total.reshape(n // 2, 2, 8, 128)
        return pairs[:, 0] if skip == "x" else pairs[:, 0] + pairs[:, 1]

    def coarsen_whole(fine, coarse):
        n = fine.shape[1]
        for j, k in blocks(n // 2):
            for i, skip in enumerate(("", "x", "y", "z")):
                value = coarser(lambda j, k, i=i: fine[i, j, k], n, j, k, skip)
                coarse[i, j, k] = value * (0.25 if skip else 0.125)

    def whole_residual(c, w, get, n, j, k):
        centre = get(j, k)
        parts = []
        for i, axis in enumerate("xyz"):
            parts.append(c[1 + 2 * i, j, k] * low(get, n, j, k, axis) + c[2 + 2 * i, j, k] * high(get, n, j, k, axis))
        return centre, (w(j, k) - centre) + (parts[0] + parts[1]) + parts[2]

    class InRefs:
        def __init__(self, ref):
            self.ref = ref

        def __call__(self, j, k):
            return self.ref[j, k]

        def put(self, j, k, value):
            self.ref[j, k] = value

    class InValues:
        def __init__(self):
            self.values = {}

        def __call__(self, j, k):
            return self.values[j, k]

        def put(self, j, k, value):
            self.values[j, k] = value

    def sweeps_whole(c, w, old, new, n, table, lo, hi):
        for sweep_index in range(lo, hi):
            keep, gain = table[sweep_index]
            results = []
            for j, k in blocks(n):
                centre, r = whole_residual(c, w, old, n, j, k)
                change = gain * r
                if sweep_index == 1 and lo == 1:
                    change = change + keep * centre
                elif sweep_index:
                    change = change + keep * (centre - new(j, k))
                if isinstance(new, InRefs):
                    new.put(j, k, centre + change)
                else:
                    results.append((j, k, centre + change))
            if results:
                new = InValues()
                for j, k, value in results:
                    new.put(j, k, value)
            old, new = new, old
        return old, new

    def start_whole(c, w, v, n, table, f):
        for j, k in blocks(n):
            g = f(j, k) * c[8, j, k]
            w.put(j, k, g)
            v.put(j, k, table[0][1] * g)

    def restricted(c, w, v, n):
        result = InValues()
        scaled = InValues()
        for j, k in blocks(n):
            _, r = whole_residual(c, w, v, n, j, k)
            scaled.put(j, k, r * c[7, j, k])
        for j, k in blocks(n // 2):
            result.put(j, k, coarser(scaled, n, j, k) * 0.125)
        return result

    def corrected(v, coarse, n, into):
        for j, k in blocks(n):
            value = coarse(j // 2, k // 2)
            value = jnp.broadcast_to(value[:, None], (n // 2, 2, 8, 128)).reshape(n, 8, 128)
            into.put(j, k, v(j, k) + value)

    send_c2c(lambda copy: copy.wait_recv())
    for j in range(4):
        for name in range(4):
            rows = gc[:, pl.ds(8 * (j // 2) + 2 * name + j % 2, 16, stride=16)]
            turn[name, j] = rows.reshape(128, 128).T
    for j in range(4):
        for name in range(4):
            for k in range(4):
                for i in range(4):
                    a2[name, j, k, i] = turn[name, j, pl.ds(4 * k + i, 8, stride=16)]
    prepare_whole(a2, k2, 2)
    arrive(send_r2a)
    start(send_r2b)
    coarsen_whole(a2, a3)
    prepare_whole(a3, k3, 3)
    coarsen_whole(a3, a4)
    prepare_whole(a4, k4, 4)
    arrive(send_r2b)

    for j in range(4):
        rows = g2[:, pl.ds(8 * (j // 2) + j % 2, 16, stride=16)]
        turn[4, j] = rows.reshape(128, 128).T

    def f2(j, k):
        return jnp.stack([turn[4, j, pl.ds(4 * k + i, 8, stride=16)] for i in range(4)])

    field2, before2, source2 = InRefs(v2a), InRefs(v2b), InRefs(w2)
    start_whole(k2, source2, field2, 4, TABLE, f2)
    field2, before2 = sweeps_whole(k2, source2, field2, before2, 4, TABLE, 1, SWEEPS)
    field3, source3 = InValues(), InValues()
    start_whole(k3, source3, field3, 2, TABLE, restricted(k2, source2, field2, 4))
    field3, _ = sweeps_whole(k3, source3, field3, InValues(), 2, TABLE, 1, SWEEPS)
    field4, source4 = InValues(), InValues()
    start_whole(k4, source4, field4, 1, COARSE, restricted(k3, source3, field3, 2))
    field4, _ = sweeps_whole(k4, source4, field4, InValues(), 1, COARSE, 1, COARSE_SWEEPS)
    next3 = InValues()
    corrected(field3, field4, 2, next3)
    field3, _ = sweeps_whole(k3, source3, next3, InValues(), 2, TABLE, 0, SWEEPS)
    corrected(field2, field3, 4, field2)
    field2, _ = sweeps_whole(k2, source2, field2, before2, 4, TABLE, 0, SWEEPS)

    for j in range(4):
        for k in range(4):
            value = field2(j, k)
            for i in range(4):
                turn[4, j, pl.ds(4 * k + i, 8, stride=16)] = value[i]
    for j in range(4):
        lin[pl.ds(1, GX), pl.ds(8 + j, 16, stride=4)] = turn[4, j].T.reshape(GX, 16, 128)
    arrive(send_x1)
    lane_row = lanes((8, 128)) % 4

    def spread(block):
        value = lin[gx + block, pl.ds(8 + 2 * gy - 3, 8)]
        for x in range(4):
            one = jnp.where(lane_row == x, value, 0.0)
            one = pair_sum(pair_sum(one, 1), 2)
            pr[4 * block + x, pl.ds(0, 8, stride=2)] = one
            pr[4 * block + x, pl.ds(1, 8, stride=2)] = one

    for block in range(3):
        spread(block)

    def twice(value):
        count = value.shape[0]
        return jnp.broadcast_to(value[:, None], (count, 2, 16, 128)).reshape(2 * count, 16, 128)

    def correct1(s):
        ok, _, _ = valid(s, 2, 8, 8, 8, 4)
        added = twice(pr[pl.ds(s // 2, CHUNK // 2)])
        v1[0][some(s + 1), pl.ds(8, 16)] = jnp.where(ok, x1[0, some(s), pl.ds(2, 16)] + added, 0.0)
        w1[some(s)] = jnp.where(ok, x1[1, some(s), pl.ds(2, 16)] * c1[8, some(s)], 0.0)

    slots(2, 22, correct1)

    def smooth_down(c, w, v, step, lo, hi, last):
        for k in range(SWEEPS):
            a = k % 2

            def body(s, k=k, a=a):
                if k == SWEEPS - 1:
                    last(s, sweep(c, w, v, a, s, step, k, False, 8, 4))
                    return
                value = sweep(c, w, v, a, s, step, k, k == 0)
                v[1 - a][some(s + 1), pl.ds(8, 16)] = value

            slots(lo + k, hi - k, body)

    def spread0(s, value):
        t1[some(s - 6)] = value

    smooth_down(c1, w1, v1, 2, 3, 21, spread0)

    for odd in range(2):
        pr[:, pl.ds(odd, 8, stride=2)] = t1[...]
    arrive(send_x0)

    def correct0(s):
        ok, _, _ = valid(s, 0, 4, 16, 4, 8)
        added = twice(pr[pl.ds(s // 2, CHUNK // 2)])
        v0[0][some(s + 1), pl.ds(8, 16)] = jnp.where(ok, x0[some(s)] + added, 0.0)

    slots(0, 24, correct0)

    def finish(s, value):
        out[some(s - 4)] = value

    smooth_down(c0, w0, v0, 1, 1, 23, finish)

    for copy in send_b0 + send_c1 + send_f1 + send_x0 + send_x1 + send_r2a + send_r2b:
        copy.wait_send()
    for each in (send_c2a, send_c2b, send_c2c):
        each(lambda copy: copy.wait_send())


def step(right_side, alpha, beta_x, beta_y, beta_z):
    copies = 8 + 14 + 8 + 8 + 14 + 2 * (GX - 1 + GY - 1)
    vmem = [
        (5, 25, 24, 128),
        (9, 24, 16, 128),
        (24, 16, 128),
        (26, 32, 128),
        (26, 32, 128),
        (24, 16, 128),
        (8, 8, 128),
        (5, 25, 24, 128),
        (9, 24, 16, 128),
        (24, 16, 128),
        (26, 32, 128),
        (26, 32, 128),
        (2, 24, 24, 128),
        (12, 8, 128),
        (12, 16, 128),
        (GX, 8 * GY, 128),
        (GX, 8 * GY, 128),
        (5, 4, 128, 128),
        (GX + 2, 80, 128),
    ]
    for n in (4, 2, 1):
        vmem += [(4, n, n, n, 8, 128), (9, n, n, n, 8, 128)]
        if n == 4:
            vmem += [(n, n, n, 8, 128)] * 3
    return pl.pallas_call(
        kernel,
        out_shape=jax.ShapeDtypeStruct((16, 8, 128), F32),
        in_specs=[pl.BlockSpec(memory_space=pl.ANY)] * 5,
        out_specs=pl.BlockSpec(memory_space=pltpu.VMEM),
        scratch_shapes=[pltpu.VMEM(shape, F32) for shape in vmem]
        + [
            pltpu.SemaphoreType.DMA((5,)),
            pltpu.SemaphoreType.DMA((copies,)),
            pltpu.SemaphoreType.DMA((copies,)),
        ],
        compiler_params=pltpu.CompilerParams(
            collective_id=0, has_side_effects=True, vmem_limit_bytes=60 * 1024 * 1024
        ),
        name="vcycle",
    )(right_side, alpha, beta_x, beta_y, beta_z)


def solution(mesh):
    spec = P("gx", "gy", None)
    return jax.shard_map(step, mesh=mesh, in_specs=(spec,) * 5, out_specs=spec, check_vma=False)
```

```python
import functools

import jax
import jax.numpy as jnp
from jax import lax
from jax.experimental import pallas as pl
from jax.experimental.pallas import tpu as pltpu
from jax.sharding import PartitionSpec as P

MESH = pl.DeviceIdType.MESH
F32 = jnp.float32

SHIFT = 0.002
LOW = 0.25
HIGH = 2.0
COARSE_LOW = 0.1
SWEEPS = 4
COARSE_SWEEPS = 12
GX = 8
GY = 32
CHUNK = 4
FAR_FIRST = [4, 3, 5, 2, 6, 1, 7]
LINE = sorted(
    [(a, b, e) for a in range(4) for b in range(4) for e in range(2) if a + b + e],
    key=lambda t: -(2 * min(t[0], 4 - t[0]) + 2 * min(t[1], 4 - t[1]) + t[2]),
)


def chebyshev_table(count, lower, upper):
    theta = (upper + lower) / 2.0
    delta = (upper - lower) / 2.0
    sigma = theta / delta
    rho_prev = 1.0 / sigma
    table = []
    for sweep in range(count):
        if sweep == 0:
            table.append((0.0, 1.0 / theta))
        else:
            rho_next = 1.0 / (2.0 * sigma - rho_prev)
            table.append((rho_next * rho_prev, 2.0 * rho_next / delta))
            rho_prev = rho_next
    return table


TABLE = chebyshev_table(SWEEPS, LOW, HIGH)
COARSE = chebyshev_table(COARSE_SWEEPS, COARSE_LOW, HIGH)

NEAR = [(-1, 0), (1, 0), (0, -1), (0, 1), (-1, -1), (-1, 1), (1, -1), (1, 1)]
FAR_Y = [(0, -2), (0, 2)]
FAR_XY = [(-1, -2), (-1, 2), (1, -2), (1, 2)]


def lanes(shape):
    return lax.broadcasted_iota(jnp.int32, shape, len(shape) - 1)


def roll(value, shift):
    shape = value.shape
    if len(shape) == 3:
        value = value.reshape(shape[0] * shape[1], shape[2])
    out = pltpu.roll(value, shift % 128, 1)
    return out.reshape(shape)


def partner(value, step):
    lane = lanes(value.shape)
    return jnp.where((lane // step) % 2 == 0, roll(value, -step), roll(value, step))


def pair_sum(value, step):
    return value + partner(value, step)


def pair_first(value, step):
    lane = lanes(value.shape)
    return jnp.where((lane // step) % 2 == 0, value, roll(value, step))


def kernel(
    f_in, al_in, bx_in, by_in, bz_in, out,
    b0, c0, w0, v0a, v0b, x0, t0, b1, c1, w1, v1a, v1b, x1, t1, pr,
    gc, g2, turn, lin, a2, k2, w2, v2a, v2b, a3, k3, a4, k4,
    in_sem, ss, rs,
):
    v0, v1 = (v0a, v0b), (v1a, v1b)
    gx = lax.axis_index("gx")
    gy = lax.axis_index("gy")
    counter = [0]

    def near(dx, dy):
        return (lax.rem(gx + dx + GX, GX), lax.rem(gy + dy + GY, GY))

    def gx_peer(i):
        return (lax.rem(gx + i, GX), gy)

    def gy_peer(i):
        return (gx, lax.rem(gy + i, GY))

    def remote(src, dst, index, device):
        return pltpu.make_async_remote_copy(
            src_ref=src, dst_ref=dst, send_sem=ss.at[index], recv_sem=rs.at[index],
            device_id=device, device_id_type=MESH,
        )

    def halo(view, sides, off_x, n_x, off_y, n_y, widths):
        copies = []
        for dx, dy in sides:
            first_x, last_x, first_y, last_y = widths(dx, dy)
            lo_x, w_x = (off_x, n_x) if dx == 0 else (off_x, first_x) if dx < 0 else (off_x + n_x - last_x, last_x)
            lo_y, w_y = (off_y, n_y) if dy == 0 else (off_y, first_y) if dy < 0 else (off_y + n_y - last_y, last_y)
            src = view(pl.ds(lo_x, w_x), pl.ds(lo_y, w_y))
            dst = view(pl.ds(lo_x - dx * n_x, w_x), pl.ds(lo_y - dy * n_y, w_y))
            copies.append(remote(src, dst, counter[0], near(dx, dy)))
            counter[0] += 1
        return copies

    def start(copies):
        for copy in copies:
            copy.start()

    def arrive(copies):
        for copy in copies:
            copy.wait_recv()

    def many(count, make):
        base = counter[0]
        counter[0] += count

        def each(what):
            def body(i, carry):
                what(make(i, base + i - 1))
                return carry

            lax.fori_loop(1, count + 1, body, 0)

        return each

    def own_rows(rows):
        return pl.ds(pl.multiple_of(8 * gy, 8), rows)

    def c2_gx(i, s):
        return remote(gc.at[gx, own_rows(8)], gc.at[gx, own_rows(8)], s, gx_peer(i))

    def c2_gy(i, s):
        return remote(gc.at[:, own_rows(8)], gc.at[:, own_rows(8)], s, gy_peer(2 * i))

    def c2_core(i, s):
        rows = pl.ds(pl.multiple_of(8 * lax.rem(gy - 2 * (i - 1) + GY, GY), 8), 8)
        return remote(gc.at[:, rows], gc.at[:, rows], s, (gx, gy + 1 - 2 * lax.rem(gy, 2)))

    def r2_gx(i):
        counter[0] += 1
        return remote(g2.at[gx, own_rows(2)], g2.at[gx, own_rows(2)], counter[0] - 1, gx_peer(i))

    send_b0 = halo(
        lambda x, y: b0.at[:, x, y], NEAR, 4, 16, 4, 8,
        lambda dx, dy: (5, 4, 5, 4) if dx == 0 or dy == 0 else (4, 4, 4, 4),
    )
    send_c1 = halo(
        lambda x, y: b1.at[pl.ds(1, 4), x, y], NEAR + FAR_Y + FAR_XY, 8, 8, 8, 4,
        lambda dx, dy: (2, 2, 2, 1) if abs(dy) == 2 else (6, 5, 4, 4),
    )
    send_f1 = halo(
        lambda x, y: b1.at[0, x, y], NEAR, 8, 8, 8, 4,
        lambda dx, dy: (4, 4, 4, 4) if dx == 0 or dy == 0 else (3, 3, 3, 3),
    )
    send_x0 = halo(
        lambda x, y: x0.at[x, y], NEAR, 4, 16, 4, 8,
        lambda dx, dy: (4, 4, 4, 4) if dx == 0 or dy == 0 else (3, 3, 3, 3),
    )
    send_x1 = halo(
        lambda x, y: x1.at[:, x, y], NEAR + FAR_Y + FAR_XY, 8, 8, 8, 4,
        lambda dx, dy: (2, 2, 2, 2) if abs(dy) == 2 else (6, 6, 4, 4),
    )
    send_c2a = many(GX - 1, c2_gx)
    c2b_base = counter[0]
    send_c2b = many(GY // 2 - 1, c2_gy)
    send_c2c = many(GY // 2, c2_core)
    send_r2a = [r2_gx(i) for i in FAR_FIRST]
    along_x = [8 * lax.rem(gy // 8 + a, 4) for a in range(4)]
    along_y = [2 * lax.rem(gy // 2 + b, 4) for b in range(4)]
    core = [lax.rem(gy + e, 2) for e in range(2)]
    line = [(gx, along_x[a] + along_y[b] + core[e]) for a, b, e in LINE]
    send_r2b = []
    for device in line:
        own = g2.at[:, own_rows(2)]
        send_r2b.append(remote(own, own, counter[0], device))
        counter[0] += 1

    inputs = [
        pltpu.make_async_copy(ref, b0.at[i, pl.ds(4, 16), pl.ds(4, 8)], in_sem.at[i])
        for i, ref in enumerate((f_in, al_in, bx_in, by_in, bz_in))
    ]
    start(inputs)
    barrier = pltpu.get_barrier_semaphore()

    def greet(device):
        pl.semaphore_signal(barrier, inc=1, device_id=device, device_id_type=MESH)

    diagonal = [side for side in NEAR + FAR_XY if side[0] and side[1]]
    for device in line[:18]:
        greet(device)
    for i in FAR_FIRST:
        greet(gx_peer(i))
    for dx, dy in diagonal:
        greet(near(dx, dy))
    for device in line[18:]:
        greet(device)

    for copy in inputs:
        copy.wait()

    def split_slots(value):
        pairs = value.reshape(value.shape[0] // 2, 2, *value.shape[1:])
        return pairs[:, 0], pairs[:, 1]

    def coarsen(ref, lo, n, off, rows, step, first):
        def take(i, odd):
            return split_slots(ref[i, pl.ds(lo, n), pl.ds(off + odd, rows // 2, stride=2)])

        result = []
        for name in range(4):
            i = first + name
            even_a, even_b = take(i, 0)
            if name == 2:
                value = pair_sum(even_a + even_b, step) * 0.25
            else:
                odd_a, odd_b = take(i, 1)
                if name == 0:
                    value = pair_sum((even_a + even_b) + (odd_a + odd_b), step) * 0.125
                elif name == 1:
                    value = pair_sum(even_a + odd_a, step) * 0.25
                else:
                    value = pair_first((even_a + even_b) + (odd_a + odd_b), step) * 0.25
            result.append(value)
        return result

    for i, value in enumerate(coarsen(b0, 4, 16, 4, 8, 1, 1)):
        b1[1 + i, 8:16, 8:12] = value

    def pack(value):
        lane = lanes(value.shape[1:]) % 4
        packed = value[3]
        for i in range(2, -1, -1):
            packed = jnp.where(lane == i, value[i], packed)
        return packed

    packed = [pack(value) for value in coarsen(b1, 8, 8, 8, 4, 2, 1)]
    for i in range(4):
        gc[gx, pl.ds(8 * gy + 2 * i, 2)] = packed[i]

    pl.semaphore_wait(barrier, GX - 1 + GY - 1 + len(diagonal))

    start(send_b0)
    send_c2a(lambda copy: copy.start())
    start(send_c1)
    send_c2a(lambda copy: copy.wait_recv())
    send_c2b(lambda copy: copy.start())

    def valid(s, rows, off_x, n_x, off_y, n_y):
        shape = (CHUNK, 16, 128)
        x = gx * n_x + s - off_x + lax.broadcasted_iota(jnp.int32, shape, 0)
        y = gy * n_y + rows - off_y + lax.broadcasted_iota(jnp.int32, shape, 1)
        inside = jnp.logical_and(y >= 0, y < GY * n_y)
        return jnp.logical_and(inside, jnp.logical_and(x >= 0, x < GX * n_x)), x, y

    def slots(lo, hi, body):
        runs = -(-(hi - lo) // CHUNK)
        first = lo - (runs * CHUNK - (hi - lo)) // 2

        def run(i, carry):
            body(first + CHUNK * i)
            return carry

        lax.fori_loop(0, runs, run, 0, unroll=3)

    def some(s):
        return pl.ds(s, CHUNK)

    def prepare(b, c, row, scale, step, n_x, n_y, off, lo, hi):
        def body(s):
            at = pl.ds(row, 16)
            ok, x, y = valid(s, row, off, n_x, off, n_y)
            lane = lanes(ok.shape)
            low_x, low_y, low_z = b[2, some(s), at], b[3, some(s), at], b[4, some(s), at]
            up_x = jnp.where(x + 1 < GX * n_x, b[2, some(s + 1), at], 0.0)
            up_y = jnp.where(y + 1 < GY * n_y, b[3, some(s), pl.ds(row + 1, 16)], 0.0)
            up_z = jnp.where(lane >= 128 - step, 0.0, roll(low_z, -step))
            diagonal = SHIFT * b[1, some(s), at] + scale * (low_x + up_x + low_y + up_y + low_z + up_z)
            inverse = jnp.where(ok, 1.0 / diagonal, 0.0)
            scaled = scale * inverse
            c[1, some(s)] = low_x * scaled
            c[2, some(s)] = up_x * scaled
            c[3, some(s)] = low_y * scaled
            c[4, some(s)] = up_y * scaled
            c[5, some(s)] = jnp.where(lane < step, 0.0, low_z * scaled)
            c[6, some(s)] = up_z * scaled
            c[7, some(s)] = diagonal
            c[8, some(s)] = inverse

        slots(lo, hi, body)

    def scaled_residual(c, w, v, s, step, rows=16, off=0):
        at = pl.ds(8 + off, rows)
        centre = v[some(s + 1), at]
        k = pl.ds(off, rows)
        t = some(s)
        total = w[t, k] - centre
        along_x = c[1, t, k] * v[t, at] + c[2, t, k] * v[some(s + 2), at]
        before, after = v[some(s + 1), pl.ds(7 + off, rows)], v[some(s + 1), pl.ds(9 + off, rows)]
        along_y = c[3, t, k] * before + c[4, t, k] * after
        along_z = c[5, t, k] * roll(centre, step) + c[6, t, k] * roll(centre, -step)
        return centre, total + (along_x + along_y) + along_z

    def sweep(c, w, v, a, s, step, k, first, rows=16, off=0):
        keep, gain = TABLE[k]
        centre, r = scaled_residual(c, w, v[a], s, step, rows, off)
        change = gain * r
        if not first:
            change = change + keep * (centre - v[1 - a][some(s + 1), pl.ds(8 + off, rows)])
        return centre + change

    def smooth_up(b, c, w, v, row, step, lo, hi, rows, off):
        def begin(s):
            g = b[0, some(s), pl.ds(row, 16)] * c[8, some(s)]
            w[some(s)] = g
            v[0][some(s + 1), pl.ds(8, 16)] = TABLE[0][1] * g

        slots(lo, hi, begin)

        def second(s):
            keep, gain = TABLE[1]
            centre, r = scaled_residual(c, w, v[0], s, step)
            v[1][some(s + 1), pl.ds(8, 16)] = centre + gain * r + keep * centre

        slots(lo + 1, hi - 1, second)
        for k in (2, 3):
            a = (k - 1) % 2

            def body(s, k=k, a=a):
                v[1 - a][some(s + 1), pl.ds(8 + off, rows)] = sweep(c, w, v, a, s, step, k, False, rows, off)

            slots(lo + k, hi - k, body)

    def pair_slots(value):
        first, second = split_slots(value)
        return first + second

    arrive(send_b0)
    prepare(b0, c0, 0, 1.0, 1, 16, 8, 4, 0, 24)
    smooth_up(b0, c0, w0, v0, 0, 1, 0, 24, 16, 0)

    def resid0(s):
        centre, r = scaled_residual(c0, w0, v0[1], s, 1, 8, 4)
        x0[some(s), 4:12] = centre
        t0[pl.ds((s - 4) // 2, CHUNK // 2)] = pair_slots(r * c0[7, some(s), 4:12])

    slots(4, 20, resid0)
    both = t0[:, pl.ds(0, 4, stride=2)] + t0[:, pl.ds(1, 4, stride=2)]
    f1 = pair_sum(both, 1) * 0.125
    b1[0, 8:16, 8:12] = f1
    x1[1, 8:16, 8:12] = f1
    start(send_f1)
    start(send_x0)

    arrive(send_c1)
    prepare(b1, c1, 2, 0.25, 2, 8, 4, 8, 2, 22)
    arrive(send_f1)

    smooth_up(b1, c1, w1, v1, 2, 2, 4, 20, 8, 4)

    def resid1(s):
        centre, r = scaled_residual(c1, w1, v1[1], s, 2, 4, 6)
        x1[0, some(s), 8:12] = centre
        t1[pl.ds((s - 8) // 2, CHUNK // 2), 0:4] = pair_slots(r * c1[7, some(s), 6:10])

    slots(8, 16, resid1)
    both = t1[0:4, pl.ds(0, 2, stride=2)] + t1[0:4, pl.ds(1, 2, stride=2)]
    g2[gx, own_rows(2)] = pack(pair_sum(both, 2) * 0.125)
    start(send_r2a)
    start(send_x1)

    def forward(i, carry):
        @pl.when(i > 1)
        def _():
            c2_gy(i - 1, c2b_base + i - 2).wait_recv()

        c2_core(i, c2b_base + GY // 2 + i - 2).start()
        return carry

    lax.fori_loop(1, GY // 2 + 1, forward, 0)


    tile = (1, 8, 128)
    sub = lax.broadcasted_iota(jnp.int32, tile, 1)
    lane = lanes(tile)
    ENDS = {"x": (lane // 16 == 0, lane // 16 == 7), "y": (lane % 16 == 0, lane % 16 == 15), "z": (sub == 0, sub == 7)}

    def turned(value, shift):
        return pltpu.roll(value, shift % 8, 1)

    def high(get, n, j, k, axis):
        if axis == "x":
            value = get(j, k)
            last = roll(value[:1], -16)
            return last if n == 1 else jnp.concatenate([value[1:], last], axis=0)
        if axis == "y":
            return get(j + 1, k) if j + 1 < n else roll(get(0, k), -1)
        return get(j, k + 1) if k + 1 < n else turned(get(j, 0), -1)

    def low(get, n, j, k, axis):
        if axis == "x":
            value = get(j, k)
            first = roll(value[n - 1 :], 16)
            return first if n == 1 else jnp.concatenate([first, value[: n - 1]], axis=0)
        if axis == "y":
            return get(j - 1, k) if j > 0 else roll(get(n - 1, k), 1)
        return get(j, k - 1) if k > 0 else turned(get(j, n - 1), 1)

    def without(value, n, j, k, axis, end):
        edge = (n - 1) * end
        mask = ENDS[axis][end]
        if axis == "x":
            parts = [value[i : i + 1] for i in range(n)]
            parts[edge] = jnp.where(mask, 0.0, parts[edge])
            return parts[0] if n == 1 else jnp.concatenate(parts, axis=0)
        if (j if axis == "y" else k) != edge:
            return value
        return jnp.where(mask, 0.0, value)

    def blocks(n):
        return [(j, k) for j in range(n) for k in range(n)]

    def prepare_whole(a, c, level):
        scale = 0.25**level
        n = a.shape[1]
        for j, k in blocks(n):
            diagonal = SHIFT * a[0, j, k]
            faces = []
            for i, axis in enumerate("xyz"):
                below = a[1 + i, j, k]
                above = high(lambda j, k, i=i: a[1 + i, j, k], n, j, k, axis)
                above = without(above, n, j, k, axis, 1)
                faces.append((without(below, n, j, k, axis, 0), above))
                diagonal = diagonal + scale * (below + above)
            inverse = 1.0 / diagonal
            scaled = scale * inverse
            for i, (below, above) in enumerate(faces):
                c[1 + 2 * i, j, k] = below * scaled
                c[2 + 2 * i, j, k] = above * scaled
            c[7, j, k] = diagonal
            c[8, j, k] = inverse

    def coarser(take, n, j, k, skip=""):
        total = None
        for fine_j in (2 * j, 2 * j + 1)[: 1 if skip == "y" else 2]:
            for fine_k in (2 * k, 2 * k + 1)[: 1 if skip == "z" else 2]:
                value = take(fine_j, fine_k)
                total = value if total is None else total + value
        pairs = total.reshape(n // 2, 2, 8, 128)
        return pairs[:, 0] if skip == "x" else pairs[:, 0] + pairs[:, 1]

    def coarsen_whole(fine, coarse):
        n = fine.shape[1]
        for j, k in blocks(n // 2):
            for i, skip in enumerate(("", "x", "y", "z")):
                value = coarser(lambda j, k, i=i: fine[i, j, k], n, j, k, skip)
                coarse[i, j, k] = value * (0.25 if skip else 0.125)

    def whole_residual(c, w, get, n, j, k):
        centre = get(j, k)
        parts = []
        for i, axis in enumerate("xyz"):
            parts.append(c[1 + 2 * i, j, k] * low(get, n, j, k, axis) + c[2 + 2 * i, j, k] * high(get, n, j, k, axis))
        return centre, (w(j, k) - centre) + (parts[0] + parts[1]) + parts[2]

    class InRefs:
        def __init__(self, ref):
            self.ref = ref

        def __call__(self, j, k):
            return self.ref[j, k]

        def put(self, j, k, value):
            self.ref[j, k] = value

    class InValues:
        def __init__(self):
            self.values = {}

        def __call__(self, j, k):
            return self.values[j, k]

        def put(self, j, k, value):
            self.values[j, k] = value

    def sweeps_whole(c, w, old, new, n, table, lo, hi):
        for sweep_index in range(lo, hi):
            keep, gain = table[sweep_index]
            results = []
            for j, k in blocks(n):
                centre, r = whole_residual(c, w, old, n, j, k)
                change = gain * r
                if sweep_index == 1 and lo == 1:
                    change = change + keep * centre
                elif sweep_index:
                    change = change + keep * (centre - new(j, k))
                if isinstance(new, InRefs):
                    new.put(j, k, centre + change)
                else:
                    results.append((j, k, centre + change))
            if results:
                new = InValues()
                for j, k, value in results:
                    new.put(j, k, value)
            old, new = new, old
        return old, new

    def start_whole(c, w, v, n, table, f):
        for j, k in blocks(n):
            g = f(j, k) * c[8, j, k]
            w.put(j, k, g)
            v.put(j, k, table[0][1] * g)

    def restricted(c, w, v, n):
        result = InValues()
        scaled = InValues()
        for j, k in blocks(n):
            _, r = whole_residual(c, w, v, n, j, k)
            scaled.put(j, k, r * c[7, j, k])
        for j, k in blocks(n // 2):
            result.put(j, k, coarser(scaled, n, j, k) * 0.125)
        return result

    def corrected(v, coarse, n, into):
        for j, k in blocks(n):
            value = coarse(j // 2, k // 2)
            value = jnp.broadcast_to(value[:, None], (n // 2, 2, 8, 128)).reshape(n, 8, 128)
            into.put(j, k, v(j, k) + value)

    send_c2c(lambda copy: copy.wait_recv())
    for j in range(4):
        for name in range(4):
            rows = gc[:, pl.ds(8 * (j // 2) + 2 * name + j % 2, 16, stride=16)]
            turn[name, j] = rows.reshape(128, 128).T
    for j in range(4):
        for name in range(4):
            for k in range(4):
                for i in range(4):
                    a2[name, j, k, i] = turn[name, j, pl.ds(4 * k + i, 8, stride=16)]
    prepare_whole(a2, k2, 2)
    arrive(send_r2a)
    start(send_r2b)
    coarsen_whole(a2, a3)
    prepare_whole(a3, k3, 3)
    coarsen_whole(a3, a4)
    prepare_whole(a4, k4, 4)
    arrive(send_r2b)

    for j in range(4):
        rows = g2[:, pl.ds(8 * (j // 2) + j % 2, 16, stride=16)]
        turn[4, j] = rows.reshape(128, 128).T

    def f2(j, k):
        return jnp.stack([turn[4, j, pl.ds(4 * k + i, 8, stride=16)] for i in range(4)])

    field2, before2, source2 = InRefs(v2a), InRefs(v2b), InRefs(w2)
    start_whole(k2, source2, field2, 4, TABLE, f2)
    field2, before2 = sweeps_whole(k2, source2, field2, before2, 4, TABLE, 1, SWEEPS)
    field3, source3 = InValues(), InValues()
    start_whole(k3, source3, field3, 2, TABLE, restricted(k2, source2, field2, 4))
    field3, _ = sweeps_whole(k3, source3, field3, InValues(), 2, TABLE, 1, SWEEPS)
    field4, source4 = InValues(), InValues()
    start_whole(k4, source4, field4, 1, COARSE, restricted(k3, source3, field3, 2))
    field4, _ = sweeps_whole(k4, source4, field4, InValues(), 1, COARSE, 1, COARSE_SWEEPS)
    next3 = InValues()
    corrected(field3, field4, 2, next3)
    field3, _ = sweeps_whole(k3, source3, next3, InValues(), 2, TABLE, 0, SWEEPS)
    corrected(field2, field3, 4, field2)
    field2, _ = sweeps_whole(k2, source2, field2, before2, 4, TABLE, 0, SWEEPS)

    for j in range(4):
        for k in range(4):
            value = field2(j, k)
            for i in range(4):
                turn[4, j, pl.ds(4 * k + i, 8, stride=16)] = value[i]
    for j in range(4):
        lin[pl.ds(1, GX), pl.ds(8 + j, 16, stride=4)] = turn[4, j].T.reshape(GX, 16, 128)
    arrive(send_x1)
    lane_row = lanes((8, 128)) % 4

    def spread(block):
        value = lin[gx + block, pl.ds(8 + 2 * gy - 3, 8)]
        for x in range(4):
            one = jnp.where(lane_row == x, value, 0.0)
            one = pair_sum(pair_sum(one, 1), 2)
            pr[4 * block + x, pl.ds(0, 8, stride=2)] = one
            pr[4 * block + x, pl.ds(1, 8, stride=2)] = one

    for block in range(3):
        spread(block)

    def twice(value):
        count = value.shape[0]
        return jnp.broadcast_to(value[:, None], (count, 2, 16, 128)).reshape(2 * count, 16, 128)

    def correct1(s):
        ok, _, _ = valid(s, 2, 8, 8, 8, 4)
        added = twice(pr[pl.ds(s // 2, CHUNK // 2)])
        v1[0][some(s + 1), pl.ds(8, 16)] = jnp.where(ok, x1[0, some(s), pl.ds(2, 16)] + added, 0.0)
        w1[some(s)] = jnp.where(ok, x1[1, some(s), pl.ds(2, 16)] * c1[8, some(s)], 0.0)

    slots(2, 22, correct1)

    def smooth_down(c, w, v, step, lo, hi, last):
        for k in range(SWEEPS):
            a = k % 2

            def body(s, k=k, a=a):
                if k == SWEEPS - 1:
                    last(s, sweep(c, w, v, a, s, step, k, False, 8, 4))
                    return
                value = sweep(c, w, v, a, s, step, k, k == 0)
                v[1 - a][some(s + 1), pl.ds(8, 16)] = value

            slots(lo + k, hi - k, body)

    def spread0(s, value):
        t1[some(s - 6)] = value

    smooth_down(c1, w1, v1, 2, 3, 21, spread0)

    for odd in range(2):
        pr[:, pl.ds(odd, 8, stride=2)] = t1[...]
    arrive(send_x0)

    def correct0(s):
        ok, _, _ = valid(s, 0, 4, 16, 4, 8)
        added = twice(pr[pl.ds(s // 2, CHUNK // 2)])
        v0[0][some(s + 1), pl.ds(8, 16)] = jnp.where(ok, x0[some(s)] + added, 0.0)

    slots(0, 24, correct0)

    def finish(s, value):
        out[some(s - 4)] = value

    smooth_down(c0, w0, v0, 1, 1, 23, finish)

    for copy in send_b0 + send_c1 + send_f1 + send_x0 + send_x1 + send_r2a + send_r2b:
        copy.wait_send()
    for each in (send_c2a, send_c2b, send_c2c):
        each(lambda copy: copy.wait_send())


def step(right_side, alpha, beta_x, beta_y, beta_z):
    copies = 8 + 14 + 8 + 8 + 14 + 2 * (GX - 1 + GY - 1)
    vmem = [
        (5, 25, 24, 128),
        (9, 24, 16, 128),
        (24, 16, 128),
        (26, 32, 128),
        (26, 32, 128),
        (24, 16, 128),
        (8, 8, 128),
        (5, 25, 24, 128),
        (9, 24, 16, 128),
        (24, 16, 128),
        (26, 32, 128),
        (26, 32, 128),
        (2, 24, 24, 128),
        (12, 8, 128),
        (12, 16, 128),
        (GX, 8 * GY, 128),
        (GX, 8 * GY, 128),
        (5, 4, 128, 128),
        (GX + 2, 80, 128),
    ]
    for n in (4, 2, 1):
        vmem += [(4, n, n, n, 8, 128), (9, n, n, n, 8, 128)]
        if n == 4:
            vmem += [(n, n, n, 8, 128)] * 3
    return pl.pallas_call(
        kernel,
        out_shape=pltpu.VMEM((16, 8, 128), F32),
        in_specs=[pl.BlockSpec(memory_space=pl.ANY)] * 5,
        out_specs=pl.BlockSpec(memory_space=pltpu.VMEM),
        scratch_shapes=[pltpu.VMEM(shape, F32) for shape in vmem]
        + [
            pltpu.SemaphoreType.DMA((5,)),
            pltpu.SemaphoreType.DMA((copies,)),
            pltpu.SemaphoreType.DMA((copies,)),
        ],
        compiler_params=pltpu.CompilerParams(
            collective_id=0, has_side_effects=True, vmem_limit_bytes=60 * 1024 * 1024
        ),
        name="vcycle",
    )(right_side, alpha, beta_x, beta_y, beta_z)


def solution(mesh):
    spec = P("gx", "gy", None)
    return jax.shard_map(step, mesh=mesh, in_specs=(spec,) * 5, out_specs=spec, check_vma=False)
```

```python
import functools

import jax
import jax.numpy as jnp
from jax import lax
from jax.experimental import pallas as pl
from jax.experimental.pallas import tpu as pltpu
from jax.sharding import PartitionSpec as P

MESH = pl.DeviceIdType.MESH
F32 = jnp.float32

SHIFT = 0.002
LOW = 0.25
HIGH = 2.0
COARSE_LOW = 0.1
SWEEPS = 4
COARSE_SWEEPS = 12
GX = 8
GY = 32
CHUNK = 4
FAR_FIRST = [4, 3, 5, 2, 6, 1, 7]
LINE = sorted(
    [(a, b, e) for a in range(4) for b in range(4) for e in range(2) if a + b + e],
    key=lambda t: -(2 * min(t[0], 4 - t[0]) + 2 * min(t[1], 4 - t[1]) + t[2]),
)


def chebyshev_table(count, lower, upper):
    theta = (upper + lower) / 2.0
    delta = (upper - lower) / 2.0
    sigma = theta / delta
    rho_prev = 1.0 / sigma
    table = []
    for sweep in range(count):
        if sweep == 0:
            table.append((0.0, 1.0 / theta))
        else:
            rho_next = 1.0 / (2.0 * sigma - rho_prev)
            table.append((rho_next * rho_prev, 2.0 * rho_next / delta))
            rho_prev = rho_next
    return table


TABLE = chebyshev_table(SWEEPS, LOW, HIGH)
COARSE = chebyshev_table(COARSE_SWEEPS, COARSE_LOW, HIGH)

NEAR = [(-1, 0), (1, 0), (0, -1), (0, 1), (-1, -1), (-1, 1), (1, -1), (1, 1)]
FAR_Y = [(0, -2), (0, 2)]
FAR_XY = [(-1, -2), (-1, 2), (1, -2), (1, 2)]


def lanes(shape):
    return lax.broadcasted_iota(jnp.int32, shape, len(shape) - 1)


def roll(value, shift):
    shape = value.shape
    if len(shape) == 3:
        value = value.reshape(shape[0] * shape[1], shape[2])
    out = pltpu.roll(value, shift % 128, 1)
    return out.reshape(shape)


def partner(value, step):
    lane = lanes(value.shape)
    return jnp.where((lane // step) % 2 == 0, roll(value, -step), roll(value, step))


def pair_sum(value, step):
    return value + partner(value, step)


def pair_first(value, step):
    lane = lanes(value.shape)
    return jnp.where((lane // step) % 2 == 0, value, roll(value, step))


def kernel(
    f_in, al_in, bx_in, by_in, bz_in, out,
    b0, c0, w0, v0a, v0b, x0, t0, b1, c1, w1, v1a, v1b, x1, t1, pr,
    gc, g2, turn, lin, a2, k2, w2, v2a, v2b, a3, k3, a4, k4,
    in_sem, ss, rs,
):
    v0, v1 = (v0a, v0b), (v1a, v1b)
    gx = lax.axis_index("gx")
    gy = lax.axis_index("gy")
    counter = [0]

    def near(dx, dy):
        return (lax.rem(gx + dx + GX, GX), lax.rem(gy + dy + GY, GY))

    def gx_peer(i):
        return (lax.rem(gx + i, GX), gy)

    def gy_peer(i):
        return (gx, lax.rem(gy + i, GY))

    def remote(src, dst, index, device):
        return pltpu.make_async_remote_copy(
            src_ref=src, dst_ref=dst, send_sem=ss.at[index], recv_sem=rs.at[index],
            device_id=device, device_id_type=MESH,
        )

    def halo(view, sides, off_x, n_x, off_y, n_y, widths):
        copies = []
        for dx, dy in sides:
            first_x, last_x, first_y, last_y = widths(dx, dy)
            lo_x, w_x = (off_x, n_x) if dx == 0 else (off_x, first_x) if dx < 0 else (off_x + n_x - last_x, last_x)
            lo_y, w_y = (off_y, n_y) if dy == 0 else (off_y, first_y) if dy < 0 else (off_y + n_y - last_y, last_y)
            src = view(pl.ds(lo_x, w_x), pl.ds(lo_y, w_y))
            dst = view(pl.ds(lo_x - dx * n_x, w_x), pl.ds(lo_y - dy * n_y, w_y))
            copies.append(remote(src, dst, counter[0], near(dx, dy)))
            counter[0] += 1
        return copies

    def start(copies):
        for copy in copies:
            copy.start()

    def arrive(copies):
        for copy in copies:
            copy.wait_recv()

    def many(count, make):
        base = counter[0]
        counter[0] += count

        def each(what):
            def body(i, carry):
                what(make(i, base + i - 1))
                return carry

            lax.fori_loop(1, count + 1, body, 0)

        return each

    def own_rows(rows):
        return pl.ds(pl.multiple_of(8 * gy, 8), rows)

    def c2_gx(i, s):
        return remote(gc.at[gx, own_rows(8)], gc.at[gx, own_rows(8)], s, gx_peer(i))

    def c2_gy(i, s):
        return remote(gc.at[:, own_rows(8)], gc.at[:, own_rows(8)], s, gy_peer(2 * i))

    def c2_core(i, s):
        rows = pl.ds(pl.multiple_of(8 * lax.rem(gy - 2 * (i - 1) + GY, GY), 8), 8)
        return remote(gc.at[:, rows], gc.at[:, rows], s, (gx, gy + 1 - 2 * lax.rem(gy, 2)))

    def r2_gx(i):
        counter[0] += 1
        return remote(g2.at[gx, own_rows(2)], g2.at[gx, own_rows(2)], counter[0] - 1, gx_peer(i))

    send_b0 = []
    for dx, dy in NEAR[4:]:
        for from_x, to_x, to_y in [(0, 1, 3), (1, 3, 2)] if dx > 0 and dy > 0 else [(0, 2, 4), (2, 4, 2)]:
            lo_x = 4 + from_x if dx < 0 else 20 - to_x
            lo_y = 4 if dy < 0 else 12 - to_y
            w_x = to_x - from_x
            src = b0.at[:, pl.ds(lo_x, w_x), pl.ds(lo_y, to_y)]
            dst = b0.at[:, pl.ds(lo_x - 16 * dx, w_x), pl.ds(lo_y - 8 * dy, to_y)]
            send_b0.append(remote(src, dst, counter[0], near(dx, dy)))
            counter[0] += 1
    send_b0 += halo(lambda x, y: b0.at[:, x, y], NEAR[:4], 4, 16, 4, 8, lambda dx, dy: (5, 4, 5, 4))
    send_c1 = halo(
        lambda x, y: b1.at[pl.ds(1, 4), x, y], NEAR + FAR_Y + FAR_XY, 8, 8, 8, 4,
        lambda dx, dy: (2, 2, 2, 1) if abs(dy) == 2 else (6, 5, 4, 4),
    )
    send_f1 = halo(
        lambda x, y: b1.at[0, x, y], NEAR, 8, 8, 8, 4,
        lambda dx, dy: (4, 4, 4, 4) if dx == 0 or dy == 0 else (3, 3, 3, 3),
    )
    send_x0 = halo(
        lambda x, y: x0.at[x, y], NEAR, 4, 16, 4, 8,
        lambda dx, dy: (4, 4, 4, 4) if dx == 0 or dy == 0 else (3, 3, 3, 3),
    )
    send_x1 = halo(
        lambda x, y: x1.at[:, x, y], NEAR + FAR_Y + FAR_XY, 8, 8, 8, 4,
        lambda dx, dy: (2, 2, 2, 2) if abs(dy) == 2 else (6, 6, 4, 4),
    )
    send_c2a = many(GX - 1, c2_gx)
    c2b_base = counter[0]
    send_c2b = many(GY // 2 - 1, c2_gy)
    send_c2c = many(GY // 2, c2_core)
    send_r2a = [r2_gx(i) for i in FAR_FIRST]
    along_x = [8 * lax.rem(gy // 8 + a, 4) for a in range(4)]
    along_y = [2 * lax.rem(gy // 2 + b, 4) for b in range(4)]
    core = [lax.rem(gy + e, 2) for e in range(2)]
    line = [(gx, along_x[a] + along_y[b] + core[e]) for a, b, e in LINE]
    send_r2b = []
    for device in line:
        own = g2.at[:, own_rows(2)]
        send_r2b.append(remote(own, own, counter[0], device))
        counter[0] += 1

    inputs = [
        pltpu.make_async_copy(ref, b0.at[i, pl.ds(4, 16), pl.ds(4, 8)], in_sem.at[i])
        for i, ref in enumerate((f_in, al_in, bx_in, by_in, bz_in))
    ]
    start(inputs)
    barrier = pltpu.get_barrier_semaphore()

    def greet(device):
        pl.semaphore_signal(barrier, inc=1, device_id=device, device_id_type=MESH)

    diagonal = [side for side in NEAR + FAR_XY if side[0] and side[1]]
    for device in line[:18]:
        greet(device)
    for i in FAR_FIRST:
        greet(gx_peer(i))
    for dx, dy in diagonal:
        greet(near(dx, dy))
    for device in line[18:]:
        greet(device)

    for copy in inputs:
        copy.wait()

    def split_slots(value):
        pairs = value.reshape(value.shape[0] // 2, 2, *value.shape[1:])
        return pairs[:, 0], pairs[:, 1]

    def coarsen(ref, lo, n, off, rows, step, first):
        def take(i, odd):
            return split_slots(ref[i, pl.ds(lo, n), pl.ds(off + odd, rows // 2, stride=2)])

        result = []
        for name in range(4):
            i = first + name
            even_a, even_b = take(i, 0)
            if name == 2:
                value = pair_sum(even_a + even_b, step) * 0.25
            else:
                odd_a, odd_b = take(i, 1)
                if name == 0:
                    value = pair_sum((even_a + even_b) + (odd_a + odd_b), step) * 0.125
                elif name == 1:
                    value = pair_sum(even_a + odd_a, step) * 0.25
                else:
                    value = pair_first((even_a + even_b) + (odd_a + odd_b), step) * 0.25
            result.append(value)
        return result

    for i, value in enumerate(coarsen(b0, 4, 16, 4, 8, 1, 1)):
        b1[1 + i, 8:16, 8:12] = value

    def pack(value):
        lane = lanes(value.shape[1:]) % 4
        packed = value[3]
        for i in range(2, -1, -1):
            packed = jnp.where(lane == i, value[i], packed)
        return packed

    packed = [pack(value) for value in coarsen(b1, 8, 8, 8, 4, 2, 1)]
    for i in range(4):
        gc[gx, pl.ds(8 * gy + 2 * i, 2)] = packed[i]

    pl.semaphore_wait(barrier, GX - 1 + GY - 1 + len(diagonal))

    start(send_b0)
    send_c2a(lambda copy: copy.start())
    start(send_c1)

    def valid(s, rows, off_x, n_x, off_y, n_y):
        shape = (CHUNK, 16, 128)
        x = gx * n_x + s - off_x + lax.broadcasted_iota(jnp.int32, shape, 0)
        y = gy * n_y + rows - off_y + lax.broadcasted_iota(jnp.int32, shape, 1)
        inside = jnp.logical_and(y >= 0, y < GY * n_y)
        return jnp.logical_and(inside, jnp.logical_and(x >= 0, x < GX * n_x)), x, y

    def slots(lo, hi, body):
        runs = -(-(hi - lo) // CHUNK)
        first = lo - (runs * CHUNK - (hi - lo)) // 2

        def run(i, carry):
            body(first + CHUNK * i)
            return carry

        lax.fori_loop(0, runs, run, 0, unroll=3)

    def some(s):
        return pl.ds(s, CHUNK)

    def prepare(b, c, row, scale, step, n_x, n_y, off, lo, hi):
        def body(s):
            at = pl.ds(row, 16)
            ok, x, y = valid(s, row, off, n_x, off, n_y)
            lane = lanes(ok.shape)
            low_x, low_y, low_z = b[2, some(s), at], b[3, some(s), at], b[4, some(s), at]
            up_x = jnp.where(x + 1 < GX * n_x, b[2, some(s + 1), at], 0.0)
            up_y = jnp.where(y + 1 < GY * n_y, b[3, some(s), pl.ds(row + 1, 16)], 0.0)
            up_z = jnp.where(lane >= 128 - step, 0.0, roll(low_z, -step))
            diagonal = SHIFT * b[1, some(s), at] + scale * (low_x + up_x + low_y + up_y + low_z + up_z)
            inverse = jnp.where(ok, 1.0 / diagonal, 0.0)
            scaled = scale * inverse
            c[1, some(s)] = low_x * scaled
            c[2, some(s)] = up_x * scaled
            c[3, some(s)] = low_y * scaled
            c[4, some(s)] = up_y * scaled
            c[5, some(s)] = jnp.where(lane < step, 0.0, low_z * scaled)
            c[6, some(s)] = up_z * scaled
            c[7, some(s)] = diagonal
            c[8, some(s)] = inverse

        slots(lo, hi, body)

    def scaled_residual(c, w, v, s, step, rows=16, off=0):
        at = pl.ds(8 + off, rows)
        centre = v[some(s + 1), at]
        k = pl.ds(off, rows)
        t = some(s)
        total = w[t, k] - centre
        along_x = c[1, t, k] * v[t, at] + c[2, t, k] * v[some(s + 2), at]
        before, after = v[some(s + 1), pl.ds(7 + off, rows)], v[some(s + 1), pl.ds(9 + off, rows)]
        along_y = c[3, t, k] * before + c[4, t, k] * after
        along_z = c[5, t, k] * roll(centre, step) + c[6, t, k] * roll(centre, -step)
        return centre, total + (along_x + along_y) + along_z

    def sweep(c, w, v, a, s, step, k, first, rows=16, off=0):
        keep, gain = TABLE[k]
        centre, r = scaled_residual(c, w, v[a], s, step, rows, off)
        change = gain * r
        if not first:
            change = change + keep * (centre - v[1 - a][some(s + 1), pl.ds(8 + off, rows)])
        return centre + change

    def smooth_up(b, c, w, v, row, step, lo, hi, rows, off):
        def begin(s):
            g = b[0, some(s), pl.ds(row, 16)] * c[8, some(s)]
            w[some(s)] = g
            v[0][some(s + 1), pl.ds(8, 16)] = TABLE[0][1] * g

        slots(lo, hi, begin)

        def second(s):
            keep, gain = TABLE[1]
            centre, r = scaled_residual(c, w, v[0], s, step)
            v[1][some(s + 1), pl.ds(8, 16)] = centre + gain * r + keep * centre

        slots(lo + 1, hi - 1, second)
        for k in (2, 3):
            a = (k - 1) % 2

            def body(s, k=k, a=a):
                v[1 - a][some(s + 1), pl.ds(8 + off, rows)] = sweep(c, w, v, a, s, step, k, False, rows, off)

            slots(lo + k, hi - k, body)

    def pair_slots(value):
        first, second = split_slots(value)
        return first + second

    arrive(send_b0)
    prepare(b0, c0, 0, 1.0, 1, 16, 8, 4, 0, 24)
    smooth_up(b0, c0, w0, v0, 0, 1, 0, 24, 16, 0)

    def resid0(s):
        centre, r = scaled_residual(c0, w0, v0[1], s, 1, 8, 4)
        x0[some(s), 4:12] = centre
        t0[pl.ds((s - 4) // 2, CHUNK // 2)] = pair_slots(r * c0[7, some(s), 4:12])

    slots(4, 20, resid0)
    both = t0[:, pl.ds(0, 4, stride=2)] + t0[:, pl.ds(1, 4, stride=2)]
    f1 = pair_sum(both, 1) * 0.125
    b1[0, 8:16, 8:12] = f1
    x1[1, 8:16, 8:12] = f1
    start(send_f1)
    send_c2a(lambda copy: copy.wait_recv())
    send_c2b(lambda copy: copy.start())
    start(send_x0)

    arrive(send_c1)
    prepare(b1, c1, 2, 0.25, 2, 8, 4, 8, 2, 22)
    arrive(send_f1)

    smooth_up(b1, c1, w1, v1, 2, 2, 4, 20, 8, 4)

    def resid1(s):
        centre, r = scaled_residual(c1, w1, v1[1], s, 2, 4, 6)
        x1[0, some(s), 8:12] = centre
        t1[pl.ds((s - 8) // 2, CHUNK // 2), 0:4] = pair_slots(r * c1[7, some(s), 6:10])

    slots(8, 16, resid1)
    both = t1[0:4, pl.ds(0, 2, stride=2)] + t1[0:4, pl.ds(1, 2, stride=2)]
    g2[gx, own_rows(2)] = pack(pair_sum(both, 2) * 0.125)
    start(send_r2a)
    start(send_x1)

    def forward(i, carry):
        @pl.when(i > 1)
        def _():
            c2_gy(i - 1, c2b_base + i - 2).wait_recv()

        c2_core(i, c2b_base + GY // 2 + i - 2).start()
        return carry

    lax.fori_loop(1, GY // 2 + 1, forward, 0)


    tile = (1, 8, 128)
    sub = lax.broadcasted_iota(jnp.int32, tile, 1)
    lane = lanes(tile)
    ENDS = {"x": (lane // 16 == 0, lane // 16 == 7), "y": (lane % 16 == 0, lane % 16 == 15), "z": (sub == 0, sub == 7)}

    def turned(value, shift):
        return pltpu.roll(value, shift % 8, 1)

    def high(get, n, j, k, axis):
        if axis == "x":
            value = get(j, k)
            last = roll(value[:1], -16)
            return last if n == 1 else jnp.concatenate([value[1:], last], axis=0)
        if axis == "y":
            return get(j + 1, k) if j + 1 < n else roll(get(0, k), -1)
        return get(j, k + 1) if k + 1 < n else turned(get(j, 0), -1)

    def low(get, n, j, k, axis):
        if axis == "x":
            value = get(j, k)
            first = roll(value[n - 1 :], 16)
            return first if n == 1 else jnp.concatenate([first, value[: n - 1]], axis=0)
        if axis == "y":
            return get(j - 1, k) if j > 0 else roll(get(n - 1, k), 1)
        return get(j, k - 1) if k > 0 else turned(get(j, n - 1), 1)

    def without(value, n, j, k, axis, end):
        edge = (n - 1) * end
        mask = ENDS[axis][end]
        if axis == "x":
            parts = [value[i : i + 1] for i in range(n)]
            parts[edge] = jnp.where(mask, 0.0, parts[edge])
            return parts[0] if n == 1 else jnp.concatenate(parts, axis=0)
        if (j if axis == "y" else k) != edge:
            return value
        return jnp.where(mask, 0.0, value)

    def blocks(n):
        return [(j, k) for j in range(n) for k in range(n)]

    def prepare_whole(a, c, level):
        scale = 0.25**level
        n = a.shape[1]
        for j, k in blocks(n):
            diagonal = SHIFT * a[0, j, k]
            faces = []
            for i, axis in enumerate("xyz"):
                below = a[1 + i, j, k]
                above = high(lambda j, k, i=i: a[1 + i, j, k], n, j, k, axis)
                above = without(above, n, j, k, axis, 1)
                faces.append((without(below, n, j, k, axis, 0), above))
                diagonal = diagonal + scale * (below + above)
            inverse = 1.0 / diagonal
            scaled = scale * inverse
            for i, (below, above) in enumerate(faces):
                c[1 + 2 * i, j, k] = below * scaled
                c[2 + 2 * i, j, k] = above * scaled
            c[7, j, k] = diagonal
            c[8, j, k] = inverse

    def coarser(take, n, j, k, skip=""):
        total = None
        for fine_j in (2 * j, 2 * j + 1)[: 1 if skip == "y" else 2]:
            for fine_k in (2 * k, 2 * k + 1)[: 1 if skip == "z" else 2]:
                value = take(fine_j, fine_k)
                total = value if total is None else total + value
        pairs = total.reshape(n // 2, 2, 8, 128)
        return pairs[:, 0] if skip == "x" else pairs[:, 0] + pairs[:, 1]

    def coarsen_whole(fine, coarse):
        n = fine.shape[1]
        for j, k in blocks(n // 2):
            for i, skip in enumerate(("", "x", "y", "z")):
                value = coarser(lambda j, k, i=i: fine[i, j, k], n, j, k, skip)
                coarse[i, j, k] = value * (0.25 if skip else 0.125)

    def whole_residual(c, w, get, n, j, k):
        centre = get(j, k)
        parts = []
        for i, axis in enumerate("xyz"):
            parts.append(c[1 + 2 * i, j, k] * low(get, n, j, k, axis) + c[2 + 2 * i, j, k] * high(get, n, j, k, axis))
        return centre, (w(j, k) - centre) + (parts[0] + parts[1]) + parts[2]

    class InRefs:
        def __init__(self, ref):
            self.ref = ref

        def __call__(self, j, k):
            return self.ref[j, k]

        def put(self, j, k, value):
            self.ref[j, k] = value

    class InValues:
        def __init__(self):
            self.values = {}

        def __call__(self, j, k):
            return self.values[j, k]

        def put(self, j, k, value):
            self.values[j, k] = value

    def sweeps_whole(c, w, old, new, n, table, lo, hi):
        for sweep_index in range(lo, hi):
            keep, gain = table[sweep_index]
            results = []
            for j, k in blocks(n):
                centre, r = whole_residual(c, w, old, n, j, k)
                change = gain * r
                if sweep_index == 1 and lo == 1:
                    change = change + keep * centre
                elif sweep_index:
                    change = change + keep * (centre - new(j, k))
                if isinstance(new, InRefs):
                    new.put(j, k, centre + change)
                else:
                    results.append((j, k, centre + change))
            if results:
                new = InValues()
                for j, k, value in results:
                    new.put(j, k, value)
            old, new = new, old
        return old, new

    def start_whole(c, w, v, n, table, f):
        for j, k in blocks(n):
            g = f(j, k) * c[8, j, k]
            w.put(j, k, g)
            v.put(j, k, table[0][1] * g)

    def restricted(c, w, v, n):
        result = InValues()
        scaled = InValues()
        for j, k in blocks(n):
            _, r = whole_residual(c, w, v, n, j, k)
            scaled.put(j, k, r * c[7, j, k])
        for j, k in blocks(n // 2):
            result.put(j, k, coarser(scaled, n, j, k) * 0.125)
        return result

    def corrected(v, coarse, n, into):
        for j, k in blocks(n):
            value = coarse(j // 2, k // 2)
            value = jnp.broadcast_to(value[:, None], (n // 2, 2, 8, 128)).reshape(n, 8, 128)
            into.put(j, k, v(j, k) + value)

    send_c2c(lambda copy: copy.wait_recv())
    for j in range(4):
        for name in range(4):
            rows = gc[:, pl.ds(8 * (j // 2) + 2 * name + j % 2, 16, stride=16)]
            turn[name, j] = rows.reshape(128, 128).T
    for j in range(4):
        for name in range(4):
            for k in range(4):
                for i in range(4):
                    a2[name, j, k, i] = turn[name, j, pl.ds(4 * k + i, 8, stride=16)]
    prepare_whole(a2, k2, 2)
    arrive(send_r2a)
    start(send_r2b)
    coarsen_whole(a2, a3)
    prepare_whole(a3, k3, 3)
    coarsen_whole(a3, a4)
    prepare_whole(a4, k4, 4)
    arrive(send_r2b)

    for j in range(4):
        rows = g2[:, pl.ds(8 * (j // 2) + j % 2, 16, stride=16)]
        turn[4, j] = rows.reshape(128, 128).T

    def f2(j, k):
        return jnp.stack([turn[4, j, pl.ds(4 * k + i, 8, stride=16)] for i in range(4)])

    field2, before2, source2 = InRefs(v2a), InRefs(v2b), InRefs(w2)
    start_whole(k2, source2, field2, 4, TABLE, f2)
    field2, before2 = sweeps_whole(k2, source2, field2, before2, 4, TABLE, 1, SWEEPS)
    field3, source3 = InValues(), InValues()
    start_whole(k3, source3, field3, 2, TABLE, restricted(k2, source2, field2, 4))
    field3, _ = sweeps_whole(k3, source3, field3, InValues(), 2, TABLE, 1, SWEEPS)
    field4, source4 = InValues(), InValues()
    start_whole(k4, source4, field4, 1, COARSE, restricted(k3, source3, field3, 2))
    field4, _ = sweeps_whole(k4, source4, field4, InValues(), 1, COARSE, 1, COARSE_SWEEPS)
    next3 = InValues()
    corrected(field3, field4, 2, next3)
    field3, _ = sweeps_whole(k3, source3, next3, InValues(), 2, TABLE, 0, SWEEPS)
    corrected(field2, field3, 4, field2)
    field2, _ = sweeps_whole(k2, source2, field2, before2, 4, TABLE, 0, SWEEPS)

    for j in range(4):
        for k in range(4):
            value = field2(j, k)
            for i in range(4):
                turn[4, j, pl.ds(4 * k + i, 8, stride=16)] = value[i]
    for j in range(4):
        lin[pl.ds(1, GX), pl.ds(8 + j, 16, stride=4)] = turn[4, j].T.reshape(GX, 16, 128)
    arrive(send_x1)
    lane_row = lanes((8, 128)) % 4

    def spread(block):
        value = lin[gx + block, pl.ds(8 + 2 * gy - 3, 8)]
        for x in range(4):
            one = jnp.where(lane_row == x, value, 0.0)
            one = pair_sum(pair_sum(one, 1), 2)
            pr[4 * block + x, pl.ds(0, 8, stride=2)] = one
            pr[4 * block + x, pl.ds(1, 8, stride=2)] = one

    for block in range(3):
        spread(block)

    def twice(value):
        count = value.shape[0]
        return jnp.broadcast_to(value[:, None], (count, 2, 16, 128)).reshape(2 * count, 16, 128)

    def correct1(s):
        ok, _, _ = valid(s, 2, 8, 8, 8, 4)
        added = twice(pr[pl.ds(s // 2, CHUNK // 2)])
        v1[0][some(s + 1), pl.ds(8, 16)] = jnp.where(ok, x1[0, some(s), pl.ds(2, 16)] + added, 0.0)
        w1[some(s)] = jnp.where(ok, x1[1, some(s), pl.ds(2, 16)] * c1[8, some(s)], 0.0)

    slots(2, 22, correct1)

    def smooth_down(c, w, v, step, lo, hi, last):
        for k in range(SWEEPS):
            a = k % 2

            def body(s, k=k, a=a):
                if k == SWEEPS - 1:
                    last(s, sweep(c, w, v, a, s, step, k, False, 8, 4))
                    return
                value = sweep(c, w, v, a, s, step, k, k == 0)
                v[1 - a][some(s + 1), pl.ds(8, 16)] = value

            slots(lo + k, hi - k, body)

    def spread0(s, value):
        t1[some(s - 6)] = value

    smooth_down(c1, w1, v1, 2, 3, 21, spread0)

    for odd in range(2):
        pr[:, pl.ds(odd, 8, stride=2)] = t1[...]
    arrive(send_x0)

    def correct0(s):
        ok, _, _ = valid(s, 0, 4, 16, 4, 8)
        added = twice(pr[pl.ds(s // 2, CHUNK // 2)])
        v0[0][some(s + 1), pl.ds(8, 16)] = jnp.where(ok, x0[some(s)] + added, 0.0)

    slots(0, 24, correct0)

    def finish(s, value):
        out[some(s - 4)] = value

    smooth_down(c0, w0, v0, 1, 1, 23, finish)

    for copy in send_b0 + send_c1 + send_f1 + send_x0 + send_x1 + send_r2a + send_r2b:
        copy.wait_send()
    for each in (send_c2a, send_c2b, send_c2c):
        each(lambda copy: copy.wait_send())


def step(right_side, alpha, beta_x, beta_y, beta_z):
    copies = 12 + 14 + 8 + 8 + 14 + 2 * (GX - 1 + GY - 1)
    vmem = [
        (5, 25, 24, 128),
        (9, 24, 16, 128),
        (24, 16, 128),
        (26, 32, 128),
        (26, 32, 128),
        (24, 16, 128),
        (8, 8, 128),
        (5, 25, 24, 128),
        (9, 24, 16, 128),
        (24, 16, 128),
        (26, 32, 128),
        (26, 32, 128),
        (2, 24, 24, 128),
        (12, 8, 128),
        (12, 16, 128),
        (GX, 8 * GY, 128),
        (GX, 8 * GY, 128),
        (5, 4, 128, 128),
        (GX + 2, 80, 128),
    ]
    for n in (4, 2, 1):
        vmem += [(4, n, n, n, 8, 128), (9, n, n, n, 8, 128)]
        if n == 4:
            vmem += [(n, n, n, 8, 128)] * 3
    return pl.pallas_call(
        kernel,
        out_shape=pltpu.VMEM((16, 8, 128), F32),
        in_specs=[pl.BlockSpec(memory_space=pl.ANY)] * 5,
        out_specs=pl.BlockSpec(memory_space=pltpu.VMEM),
        scratch_shapes=[pltpu.VMEM(shape, F32) for shape in vmem]
        + [
            pltpu.SemaphoreType.DMA((5,)),
            pltpu.SemaphoreType.DMA((copies,)),
            pltpu.SemaphoreType.DMA((copies,)),
        ],
        compiler_params=pltpu.CompilerParams(
            collective_id=0, has_side_effects=True, vmem_limit_bytes=60 * 1024 * 1024
        ),
        name="vcycle",
    )(right_side, alpha, beta_x, beta_y, beta_z)


def solution(mesh):
    spec = P("gx", "gy", None)
    return jax.shard_map(step, mesh=mesh, in_specs=(spec,) * 5, out_specs=spec, check_vma=False)
```

```python
import functools

import jax
import jax.numpy as jnp
from jax import lax
from jax.experimental import pallas as pl
from jax.experimental.pallas import tpu as pltpu
from jax.sharding import PartitionSpec as P

MESH = pl.DeviceIdType.MESH
F32 = jnp.float32

SHIFT = 0.002
LOW = 0.25
HIGH = 2.0
COARSE_LOW = 0.1
SWEEPS = 4
COARSE_SWEEPS = 12
GX = 8
GY = 32
CHUNK = 4
FAR_FIRST = [4, 3, 5, 2, 6, 1, 7]
LINE = sorted(
    [(a, b, e) for a in range(4) for b in range(4) for e in range(2) if a + b + e],
    key=lambda t: -(2 * min(t[0], 4 - t[0]) + 2 * min(t[1], 4 - t[1]) + t[2]),
)


def chebyshev_table(count, lower, upper):
    theta = (upper + lower) / 2.0
    delta = (upper - lower) / 2.0
    sigma = theta / delta
    rho_prev = 1.0 / sigma
    table = []
    for sweep in range(count):
        if sweep == 0:
            table.append((0.0, 1.0 / theta))
        else:
            rho_next = 1.0 / (2.0 * sigma - rho_prev)
            table.append((rho_next * rho_prev, 2.0 * rho_next / delta))
            rho_prev = rho_next
    return table


TABLE = chebyshev_table(SWEEPS, LOW, HIGH)
COARSE = chebyshev_table(COARSE_SWEEPS, COARSE_LOW, HIGH)

NEAR = [(-1, 0), (1, 0), (0, -1), (0, 1), (-1, -1), (-1, 1), (1, -1), (1, 1)]
FAR_Y = [(0, -2), (0, 2)]
FAR_XY = [(-1, -2), (-1, 2), (1, -2), (1, 2)]


def lanes(shape):
    return lax.broadcasted_iota(jnp.int32, shape, len(shape) - 1)


def roll(value, shift):
    shape = value.shape
    if len(shape) == 3:
        value = value.reshape(shape[0] * shape[1], shape[2])
    out = pltpu.roll(value, shift % 128, 1)
    return out.reshape(shape)


def partner(value, step):
    lane = lanes(value.shape)
    return jnp.where((lane // step) % 2 == 0, roll(value, -step), roll(value, step))


def pair_sum(value, step):
    return value + partner(value, step)


def pair_first(value, step):
    lane = lanes(value.shape)
    return jnp.where((lane // step) % 2 == 0, value, roll(value, step))


def kernel(
    f_in, al_in, bx_in, by_in, bz_in, out,
    b0, c0, w0, v0a, v0b, x0, t0, b1, c1, w1, v1a, v1b, x1, t1, pr,
    gc, g2, turn, lin, a2, k2, w2, v2a, v2b, a3, k3, a4, k4,
    in_sem, ss, rs,
):
    v0, v1 = (v0a, v0b), (v1a, v1b)
    gx = lax.axis_index("gx")
    gy = lax.axis_index("gy")
    counter = [0]

    def near(dx, dy):
        return (lax.rem(gx + dx + GX, GX), lax.rem(gy + dy + GY, GY))

    def gx_peer(i):
        return (lax.rem(gx + i, GX), gy)

    def gy_peer(i):
        return (gx, lax.rem(gy + i, GY))

    def remote(src, dst, index, device):
        return pltpu.make_async_remote_copy(
            src_ref=src, dst_ref=dst, send_sem=ss.at[index], recv_sem=rs.at[index],
            device_id=device, device_id_type=MESH,
        )

    def halo(view, sides, off_x, n_x, off_y, n_y, widths):
        copies = []
        for dx, dy in sides:
            first_x, last_x, first_y, last_y = widths(dx, dy)
            lo_x, w_x = (off_x, n_x) if dx == 0 else (off_x, first_x) if dx < 0 else (off_x + n_x - last_x, last_x)
            lo_y, w_y = (off_y, n_y) if dy == 0 else (off_y, first_y) if dy < 0 else (off_y + n_y - last_y, last_y)
            src = view(pl.ds(lo_x, w_x), pl.ds(lo_y, w_y))
            dst = view(pl.ds(lo_x - dx * n_x, w_x), pl.ds(lo_y - dy * n_y, w_y))
            copies.append(remote(src, dst, counter[0], near(dx, dy)))
            counter[0] += 1
        return copies

    def start(copies):
        for copy in copies:
            copy.start()

    def arrive(copies):
        for copy in copies:
            copy.wait_recv()

    def many(count, make):
        base = counter[0]
        counter[0] += count

        def each(what):
            def body(i, carry):
                what(make(i, base + i - 1))
                return carry

            lax.fori_loop(1, count + 1, body, 0)

        return each

    def own_rows(rows):
        return pl.ds(pl.multiple_of(8 * gy, 8), rows)

    def c2_gx(i, s):
        return remote(gc.at[gx, own_rows(8)], gc.at[gx, own_rows(8)], s, gx_peer(i))

    def c2_gy(i, s):
        return remote(gc.at[:, own_rows(8)], gc.at[:, own_rows(8)], s, gy_peer(2 * i))

    def c2_core(i, s):
        rows = pl.ds(pl.multiple_of(8 * lax.rem(gy - 2 * (i - 1) + GY, GY), 8), 8)
        return remote(gc.at[:, rows], gc.at[:, rows], s, (gx, gy + 1 - 2 * lax.rem(gy, 2)))

    def r2_gx(i):
        counter[0] += 1
        return remote(g2.at[gx, own_rows(2)], g2.at[gx, own_rows(2)], counter[0] - 1, gx_peer(i))

    send_b0 = []
    for dx, dy in NEAR[4:]:
        for from_x, to_x, to_y in [(0, 1, 3), (1, 3, 2)] if dx > 0 and dy > 0 else [(0, 2, 4), (2, 4, 2)]:
            lo_x = 4 + from_x if dx < 0 else 20 - to_x
            lo_y = 4 if dy < 0 else 12 - to_y
            w_x = to_x - from_x
            src = b0.at[:, pl.ds(lo_x, w_x), pl.ds(lo_y, to_y)]
            dst = b0.at[:, pl.ds(lo_x - 16 * dx, w_x), pl.ds(lo_y - 8 * dy, to_y)]
            send_b0.append(remote(src, dst, counter[0], near(dx, dy)))
            counter[0] += 1
    send_b0 += halo(lambda x, y: b0.at[:, x, y], NEAR[:4], 4, 16, 4, 8, lambda dx, dy: (5, 4, 5, 4))
    send_c1 = halo(
        lambda x, y: b1.at[pl.ds(1, 4), x, y], NEAR + FAR_Y + FAR_XY, 8, 8, 8, 4,
        lambda dx, dy: (2, 2, 2, 1) if abs(dy) == 2 else (6, 5, 4, 4),
    )
    send_f1 = halo(
        lambda x, y: b1.at[0, x, y], NEAR, 8, 8, 8, 4,
        lambda dx, dy: (4, 4, 4, 4) if dx == 0 or dy == 0 else (3, 3, 3, 3),
    )
    send_x0 = halo(
        lambda x, y: x0.at[x, y], NEAR, 4, 16, 4, 8,
        lambda dx, dy: (4, 4, 4, 4) if dx == 0 or dy == 0 else (3, 3, 3, 3),
    )
    send_x1 = halo(
        lambda x, y: x1.at[:, x, y], NEAR + FAR_Y + FAR_XY, 8, 8, 8, 4,
        lambda dx, dy: (2, 2, 2, 2) if abs(dy) == 2 else (6, 6, 4, 4),
    )
    send_c2a = many(GX - 1, c2_gx)
    c2b_base = counter[0]
    send_c2b = many(GY // 2 - 1, c2_gy)
    send_c2c = many(GY // 2, c2_core)
    send_r2a = [r2_gx(i) for i in FAR_FIRST]
    along_x = [8 * lax.rem(gy // 8 + a, 4) for a in range(4)]
    along_y = [2 * lax.rem(gy // 2 + b, 4) for b in range(4)]
    core = [lax.rem(gy + e, 2) for e in range(2)]
    line = [(gx, along_x[a] + along_y[b] + core[e]) for a, b, e in LINE]
    send_r2b = []
    for device in line:
        own = g2.at[:, own_rows(2)]
        send_r2b.append(remote(own, own, counter[0], device))
        counter[0] += 1

    inputs = [
        pltpu.make_async_copy(ref, b0.at[i, pl.ds(4, 16), pl.ds(4, 8)], in_sem.at[i])
        for i, ref in enumerate((f_in, al_in, bx_in, by_in, bz_in))
    ]
    start(inputs)
    barrier = pltpu.get_barrier_semaphore()

    def greet(device):
        pl.semaphore_signal(barrier, inc=1, device_id=device, device_id_type=MESH)

    diagonal = [side for side in NEAR + FAR_XY if side[0] and side[1]]
    for device in line[:18]:
        greet(device)
    for i in FAR_FIRST:
        greet(gx_peer(i))
    for dx, dy in diagonal:
        greet(near(dx, dy))
    for device in line[18:]:
        greet(device)

    for copy in inputs:
        copy.wait()

    def split_slots(value):
        pairs = value.reshape(value.shape[0] // 2, 2, *value.shape[1:])
        return pairs[:, 0], pairs[:, 1]

    def coarsen(ref, lo, n, off, rows, step, first):
        def take(i, odd):
            return split_slots(ref[i, pl.ds(lo, n), pl.ds(off + odd, rows // 2, stride=2)])

        result = []
        for name in range(4):
            i = first + name
            even_a, even_b = take(i, 0)
            if name == 2:
                value = pair_sum(even_a + even_b, step) * 0.25
            else:
                odd_a, odd_b = take(i, 1)
                if name == 0:
                    value = pair_sum((even_a + even_b) + (odd_a + odd_b), step) * 0.125
                elif name == 1:
                    value = pair_sum(even_a + odd_a, step) * 0.25
                else:
                    value = pair_first((even_a + even_b) + (odd_a + odd_b), step) * 0.25
            result.append(value)
        return result

    for i, value in enumerate(coarsen(b0, 4, 16, 4, 8, 1, 1)):
        b1[1 + i, 8:16, 8:12] = value

    def pack(value):
        lane = lanes(value.shape[1:]) % 4
        packed = value[3]
        for i in range(2, -1, -1):
            packed = jnp.where(lane == i, value[i], packed)
        return packed

    packed = [pack(value) for value in coarsen(b1, 8, 8, 8, 4, 2, 1)]
    for i in range(4):
        gc[gx, pl.ds(8 * gy + 2 * i, 2)] = packed[i]

    pl.semaphore_wait(barrier, GX - 1 + GY - 1 + len(diagonal))

    start(send_b0)
    send_c2a(lambda copy: copy.start())
    start(send_c1)

    def valid(s, rows, off_x, n_x, off_y, n_y):
        shape = (CHUNK, 16, 128)
        x = gx * n_x + s - off_x + lax.broadcasted_iota(jnp.int32, shape, 0)
        y = gy * n_y + rows - off_y + lax.broadcasted_iota(jnp.int32, shape, 1)
        inside = jnp.logical_and(y >= 0, y < GY * n_y)
        return jnp.logical_and(inside, jnp.logical_and(x >= 0, x < GX * n_x)), x, y

    def slots(lo, hi, body):
        runs = -(-(hi - lo) // CHUNK)
        first = lo - (runs * CHUNK - (hi - lo)) // 2

        def run(i, carry):
            body(first + CHUNK * i)
            return carry

        lax.fori_loop(0, runs, run, 0, unroll=3)

    def some(s):
        return pl.ds(s, CHUNK)

    def prepare(b, c, row, scale, step, n_x, n_y, off, lo, hi):
        def body(s):
            at = pl.ds(row, 16)
            ok, x, y = valid(s, row, off, n_x, off, n_y)
            lane = lanes(ok.shape)
            low_x, low_y, low_z = b[2, some(s), at], b[3, some(s), at], b[4, some(s), at]
            up_x = jnp.where(x + 1 < GX * n_x, b[2, some(s + 1), at], 0.0)
            up_y = jnp.where(y + 1 < GY * n_y, b[3, some(s), pl.ds(row + 1, 16)], 0.0)
            up_z = jnp.where(lane >= 128 - step, 0.0, roll(low_z, -step))
            diagonal = SHIFT * b[1, some(s), at] + scale * (low_x + up_x + low_y + up_y + low_z + up_z)
            inverse = jnp.where(ok, 1.0 / diagonal, 0.0)
            scaled = scale * inverse
            c[1, some(s)] = low_x * scaled
            c[2, some(s)] = up_x * scaled
            c[3, some(s)] = low_y * scaled
            c[4, some(s)] = up_y * scaled
            c[5, some(s)] = jnp.where(lane < step, 0.0, low_z * scaled)
            c[6, some(s)] = up_z * scaled
            c[7, some(s)] = diagonal
            c[8, some(s)] = inverse

        slots(lo, hi, body)

    def scaled_residual(c, w, v, s, step, rows=16, off=0):
        at = pl.ds(8 + off, rows)
        centre = v[some(s + 1), at]
        k = pl.ds(off, rows)
        t = some(s)
        total = w[t, k] - centre
        along_x = c[1, t, k] * v[t, at] + c[2, t, k] * v[some(s + 2), at]
        before, after = v[some(s + 1), pl.ds(7 + off, rows)], v[some(s + 1), pl.ds(9 + off, rows)]
        along_y = c[3, t, k] * before + c[4, t, k] * after
        along_z = c[5, t, k] * roll(centre, step) + c[6, t, k] * roll(centre, -step)
        return centre, total + (along_x + along_y) + along_z

    def sweep(c, w, v, a, s, step, k, first, rows=16, off=0):
        keep, gain = TABLE[k]
        centre, r = scaled_residual(c, w, v[a], s, step, rows, off)
        change = gain * r
        if not first:
            change = change + keep * (centre - v[1 - a][some(s + 1), pl.ds(8 + off, rows)])
        return centre + change

    def smooth_up(b, c, w, v, row, step, lo, hi, rows, off):
        def begin(s):
            g = b[0, some(s), pl.ds(row, 16)] * c[8, some(s)]
            w[some(s)] = g
            v[0][some(s + 1), pl.ds(8, 16)] = TABLE[0][1] * g

        slots(lo, hi, begin)

        def second(s):
            keep, gain = TABLE[1]
            centre, r = scaled_residual(c, w, v[0], s, step)
            v[1][some(s + 1), pl.ds(8, 16)] = centre + gain * r + keep * centre

        slots(lo + 1, hi - 1, second)
        for k in (2, 3):
            a = (k - 1) % 2

            def body(s, k=k, a=a):
                v[1 - a][some(s + 1), pl.ds(8 + off, rows)] = sweep(c, w, v, a, s, step, k, False, rows, off)

            slots(lo + k, hi - k, body)

    def pair_slots(value):
        first, second = split_slots(value)
        return first + second

    arrive(send_b0)
    prepare(b0, c0, 0, 1.0, 1, 16, 8, 4, 0, 24)
    smooth_up(b0, c0, w0, v0, 0, 1, 0, 24, 16, 0)

    def resid0(s):
        centre, r = scaled_residual(c0, w0, v0[1], s, 1, 8, 4)
        x0[some(s), 4:12] = centre
        t0[pl.ds((s - 4) // 2, CHUNK // 2), 0:8] = pair_slots(r * c0[7, some(s), 4:12])

    slots(4, 20, resid0)
    both = t0[:, pl.ds(0, 4, stride=2)] + t0[:, pl.ds(1, 4, stride=2)]
    f1 = pair_sum(both, 1) * 0.125
    b1[0, 8:16, 8:12] = f1
    x1[1, 8:16, 8:12] = f1
    start(send_f1)
    send_c2a(lambda copy: copy.wait_recv())
    send_c2b(lambda copy: copy.start())
    start(send_x0)

    arrive(send_c1)
    prepare(b1, c1, 2, 0.25, 2, 8, 4, 8, 2, 22)
    arrive(send_f1)

    smooth_up(b1, c1, w1, v1, 2, 2, 4, 20, 8, 4)

    def resid1(s):
        centre, r = scaled_residual(c1, w1, v1[1], s, 2, 4, 6)
        x1[0, some(s), 8:12] = centre
        t1[pl.ds((s - 8) // 2, CHUNK // 2), 0:4] = pair_slots(r * c1[7, some(s), 6:10])

    slots(8, 16, resid1)
    both = t1[0:4, pl.ds(0, 2, stride=2)] + t1[0:4, pl.ds(1, 2, stride=2)]
    g2[gx, own_rows(2)] = pack(pair_sum(both, 2) * 0.125)
    start(send_r2a)
    start(send_x1)

    def forward(i, carry):
        @pl.when(i > 1)
        def _():
            c2_gy(i - 1, c2b_base + i - 2).wait_recv()

        c2_core(i, c2b_base + GY // 2 + i - 2).start()
        return carry

    lax.fori_loop(1, GY // 2 + 1, forward, 0)


    tile = (1, 8, 128)
    sub = lax.broadcasted_iota(jnp.int32, tile, 1)
    lane = lanes(tile)
    ENDS = {"x": (lane // 16 == 0, lane // 16 == 7), "y": (lane % 16 == 0, lane % 16 == 15), "z": (sub == 0, sub == 7)}

    def turned(value, shift):
        return pltpu.roll(value, shift % 8, 1)

    def high(get, n, j, k, axis):
        if axis == "x":
            value = get(j, k)
            last = roll(value[:1], -16)
            return last if n == 1 else jnp.concatenate([value[1:], last], axis=0)
        if axis == "y":
            return get(j + 1, k) if j + 1 < n else roll(get(0, k), -1)
        return get(j, k + 1) if k + 1 < n else turned(get(j, 0), -1)

    def low(get, n, j, k, axis):
        if axis == "x":
            value = get(j, k)
            first = roll(value[n - 1 :], 16)
            return first if n == 1 else jnp.concatenate([first, value[: n - 1]], axis=0)
        if axis == "y":
            return get(j - 1, k) if j > 0 else roll(get(n - 1, k), 1)
        return get(j, k - 1) if k > 0 else turned(get(j, n - 1), 1)

    def without(value, n, j, k, axis, end):
        edge = (n - 1) * end
        mask = ENDS[axis][end]
        if axis == "x":
            parts = [value[i : i + 1] for i in range(n)]
            parts[edge] = jnp.where(mask, 0.0, parts[edge])
            return parts[0] if n == 1 else jnp.concatenate(parts, axis=0)
        if (j if axis == "y" else k) != edge:
            return value
        return jnp.where(mask, 0.0, value)

    def blocks(n):
        return [(j, k) for j in range(n) for k in range(n)]

    def prepare_whole(a, c, level):
        scale = 0.25**level
        n = a.shape[1]
        for j, k in blocks(n):
            diagonal = SHIFT * a[0, j, k]
            faces = []
            for i, axis in enumerate("xyz"):
                below = a[1 + i, j, k]
                above = high(lambda j, k, i=i: a[1 + i, j, k], n, j, k, axis)
                above = without(above, n, j, k, axis, 1)
                faces.append((without(below, n, j, k, axis, 0), above))
                diagonal = diagonal + scale * (below + above)
            inverse = 1.0 / diagonal
            scaled = scale * inverse
            for i, (below, above) in enumerate(faces):
                c[1 + 2 * i, j, k] = below * scaled
                c[2 + 2 * i, j, k] = above * scaled
            c[7, j, k] = diagonal
            c[8, j, k] = inverse

    def coarser(take, n, j, k, skip=""):
        total = None
        for fine_j in (2 * j, 2 * j + 1)[: 1 if skip == "y" else 2]:
            for fine_k in (2 * k, 2 * k + 1)[: 1 if skip == "z" else 2]:
                value = take(fine_j, fine_k)
                total = value if total is None else total + value
        pairs = total.reshape(n // 2, 2, 8, 128)
        return pairs[:, 0] if skip == "x" else pairs[:, 0] + pairs[:, 1]

    def coarsen_whole(fine, coarse):
        n = fine.shape[1]
        for j, k in blocks(n // 2):
            for i, skip in enumerate(("", "x", "y", "z")):
                value = coarser(lambda j, k, i=i: fine[i, j, k], n, j, k, skip)
                coarse[i, j, k] = value * (0.25 if skip else 0.125)

    def whole_residual(c, w, get, n, j, k):
        centre = get(j, k)
        parts = []
        for i, axis in enumerate("xyz"):
            parts.append(c[1 + 2 * i, j, k] * low(get, n, j, k, axis) + c[2 + 2 * i, j, k] * high(get, n, j, k, axis))
        return centre, (w(j, k) - centre) + (parts[0] + parts[1]) + parts[2]

    class InRefs:
        def __init__(self, ref):
            self.ref = ref

        def __call__(self, j, k):
            return self.ref[j, k]

        def put(self, j, k, value):
            self.ref[j, k] = value

    class InValues:
        def __init__(self):
            self.values = {}

        def __call__(self, j, k):
            return self.values[j, k]

        def put(self, j, k, value):
            self.values[j, k] = value

    def sweeps_whole(c, w, old, new, n, table, lo, hi):
        for sweep_index in range(lo, hi):
            keep, gain = table[sweep_index]
            results = []
            for j, k in blocks(n):
                centre, r = whole_residual(c, w, old, n, j, k)
                change = gain * r
                if sweep_index == 1 and lo == 1:
                    change = change + keep * centre
                elif sweep_index:
                    change = change + keep * (centre - new(j, k))
                if isinstance(new, InRefs):
                    new.put(j, k, centre + change)
                else:
                    results.append((j, k, centre + change))
            if results:
                new = InValues()
                for j, k, value in results:
                    new.put(j, k, value)
            old, new = new, old
        return old, new

    def start_whole(c, w, v, n, table, f):
        for j, k in blocks(n):
            g = f(j, k) * c[8, j, k]
            w.put(j, k, g)
            v.put(j, k, table[0][1] * g)

    def restricted(c, w, v, n):
        result = InValues()
        scaled = InValues()
        for j, k in blocks(n):
            _, r = whole_residual(c, w, v, n, j, k)
            scaled.put(j, k, r * c[7, j, k])
        for j, k in blocks(n // 2):
            result.put(j, k, coarser(scaled, n, j, k) * 0.125)
        return result

    def corrected(v, coarse, n, into):
        for j, k in blocks(n):
            value = coarse(j // 2, k // 2)
            value = jnp.broadcast_to(value[:, None], (n // 2, 2, 8, 128)).reshape(n, 8, 128)
            into.put(j, k, v(j, k) + value)

    send_c2c(lambda copy: copy.wait_recv())
    for j in range(4):
        for name in range(4):
            rows = gc[:, pl.ds(8 * (j // 2) + 2 * name + j % 2, 16, stride=16)]
            turn[name, j] = rows.reshape(128, 128).T
    for j in range(4):
        for name in range(4):
            for k in range(4):
                for i in range(4):
                    a2[name, j, k, i] = turn[name, j, pl.ds(4 * k + i, 8, stride=16)]
    prepare_whole(a2, k2, 2)
    arrive(send_r2a)
    start(send_r2b)
    coarsen_whole(a2, a3)
    prepare_whole(a3, k3, 3)
    coarsen_whole(a3, a4)
    prepare_whole(a4, k4, 4)
    arrive(send_r2b)

    for j in range(4):
        rows = g2[:, pl.ds(8 * (j // 2) + j % 2, 16, stride=16)]
        turn[4, j] = rows.reshape(128, 128).T

    def f2(j, k):
        return jnp.stack([turn[4, j, pl.ds(4 * k + i, 8, stride=16)] for i in range(4)])

    field2, before2, source2 = InRefs(v2a), InRefs(v2b), InRefs(w2)
    start_whole(k2, source2, field2, 4, TABLE, f2)
    field2, before2 = sweeps_whole(k2, source2, field2, before2, 4, TABLE, 1, SWEEPS)
    field3, source3 = InValues(), InValues()
    start_whole(k3, source3, field3, 2, TABLE, restricted(k2, source2, field2, 4))
    field3, _ = sweeps_whole(k3, source3, field3, InValues(), 2, TABLE, 1, SWEEPS)
    field4, source4 = InValues(), InValues()
    start_whole(k4, source4, field4, 1, COARSE, restricted(k3, source3, field3, 2))
    field4, _ = sweeps_whole(k4, source4, field4, InValues(), 1, COARSE, 1, COARSE_SWEEPS)
    next3 = InValues()
    corrected(field3, field4, 2, next3)
    field3, _ = sweeps_whole(k3, source3, next3, InValues(), 2, TABLE, 0, SWEEPS)
    corrected(field2, field3, 4, field2)
    field2, _ = sweeps_whole(k2, source2, field2, before2, 4, TABLE, 0, SWEEPS)

    for j in range(4):
        for k in range(4):
            value = field2(j, k)
            for i in range(4):
                turn[4, j, pl.ds(4 * k + i, 8, stride=16)] = value[i]
    for j in range(4):
        lin[pl.ds(1, GX), pl.ds(8 + j, 16, stride=4)] = turn[4, j].T.reshape(GX, 16, 128)
    arrive(send_x1)
    lane_row = lanes((8, 128)) % 4

    def spread(block):
        value = lin[gx + block, pl.ds(8 + 2 * gy - 3, 8)]
        for x in range(4):
            one = jnp.where(lane_row == x, value, 0.0)
            one = pair_sum(pair_sum(one, 1), 2)
            pr[4 * block + x, pl.ds(0, 8, stride=2)] = one
            pr[4 * block + x, pl.ds(1, 8, stride=2)] = one

    for block in range(3):
        spread(block)

    def twice(value):
        count = value.shape[0]
        return jnp.broadcast_to(value[:, None], (count, 2, 16, 128)).reshape(2 * count, 16, 128)

    def correct1(s):
        ok, _, _ = valid(s, 2, 8, 8, 8, 4)
        added = twice(pr[pl.ds(s // 2, CHUNK // 2)])
        v1[0][some(s + 1), pl.ds(8, 16)] = jnp.where(ok, x1[0, some(s), pl.ds(2, 16)] + added, 0.0)
        w1[some(s)] = jnp.where(ok, x1[1, some(s), pl.ds(2, 16)] * c1[8, some(s)], 0.0)

    slots(2, 22, correct1)

    def smooth_down(c, w, v, step, lo, hi, last):
        for k in range(SWEEPS):
            a = k % 2

            def body(s, k=k, a=a):
                if k == SWEEPS - 1:
                    last(s, sweep(c, w, v, a, s, step, k, False, 8, 4))
                    return
                value = sweep(c, w, v, a, s, step, k, k == 0)
                v[1 - a][some(s + 1), pl.ds(8, 16)] = value

            slots(lo + k, hi - k, body)

    def spread0(s, value):
        t1[some(s - 6), 0:8] = value

    smooth_down(c1, w1, v1, 2, 3, 21, spread0)

    for odd in range(2):
        pr[:, pl.ds(odd, 8, stride=2)] = t1[:, 0:8]
    arrive(send_x0)

    def correct0(s):
        ok, _, _ = valid(s, 0, 4, 16, 4, 8)
        added = twice(pr[pl.ds(s // 2, CHUNK // 2)])
        v0[0][some(s + 1), pl.ds(8, 16)] = jnp.where(ok, x0[some(s)] + added, 0.0)

    slots(0, 24, correct0)

    def finish(s, value):
        out[some(s - 4)] = value

    smooth_down(c0, w0, v0, 1, 1, 23, finish)

    for copy in send_b0 + send_c1 + send_f1 + send_x0 + send_x1 + send_r2a + send_r2b:
        copy.wait_send()
    for each in (send_c2a, send_c2b, send_c2c):
        each(lambda copy: copy.wait_send())


def step(right_side, alpha, beta_x, beta_y, beta_z):
    copies = 12 + 14 + 8 + 8 + 14 + 2 * (GX - 1 + GY - 1)
    vmem = [
        (5, 25, 24, 128),
        (9, 24, 16, 128),
        (24, 16, 128),
        (26, 32, 128),
        (26, 32, 128),
        (24, 16, 128),
        (8, 16, 128),
        (5, 25, 24, 128),
        (9, 24, 16, 128),
        (24, 16, 128),
        (26, 32, 128),
        (26, 32, 128),
        (2, 24, 24, 128),
        (12, 16, 128),
        (12, 16, 128),
        (GX, 8 * GY + 8, 128),
        (GX, 8 * GY, 128),
        (5, 4, 128, 128),
        (GX + 2, 80, 128),
    ]
    for n in (4, 2, 1):
        vmem += [(4, n, n, n, 8, 128), (9, n, n, n, 8, 128)]
        if n == 4:
            vmem += [(n, n, n, 8, 128)] * 3
    return pl.pallas_call(
        kernel,
        out_shape=pltpu.VMEM((16, 8, 128), F32),
        in_specs=[pl.BlockSpec(memory_space=pl.ANY)] * 5,
        out_specs=pl.BlockSpec(memory_space=pltpu.VMEM),
        scratch_shapes=[pltpu.VMEM(shape, F32) for shape in vmem]
        + [
            pltpu.SemaphoreType.DMA((5,)),
            pltpu.SemaphoreType.DMA((copies,)),
            pltpu.SemaphoreType.DMA((copies,)),
        ],
        compiler_params=pltpu.CompilerParams(
            collective_id=0, has_side_effects=True, vmem_limit_bytes=60 * 1024 * 1024
        ),
        name="vcycle",
    )(right_side, alpha, beta_x, beta_y, beta_z)


def solution(mesh):
    spec = P("gx", "gy", None)
    return jax.shard_map(step, mesh=mesh, in_specs=(spec,) * 5, out_specs=spec, check_vma=False)
```
